32 devices in a mesh: seq: 8 (over z, x), fsdp: 4 (over y, core).
Axes of the slice: x: 2, y: 2, z: 4, core: 2. Of those that a mesh axis runs over, the one named last changes fastest.
Arguments:
- block_input: float32 [8, 1024, 1536], P('fsdp', 'seq'), may hold values from -6 to 6
- teacher: float32 [8, 1024, 1536], P('fsdp', 'seq'), may hold values from -6 to 6
- valid_lengths: int32 [8], replicated, may hold values from 128 to 1024, as said below
- norm_gain: bfloat16 [1536], P('fsdp'), may hold values from 0.5 to 1.5
- w_gate: bfloat16 [1536, 2048], P('fsdp'), may hold values from -0.15625 to 0.15625
- w_input: bfloat16 [1536, 2048], P('fsdp'), may hold values from -0.15625 to 0.15625
- conv_weight: bfloat16 [4, 2048], P(None, 'fsdp'), may hold values from -3 to 3
- conv_bias: bfloat16 [2048], P('fsdp'), may hold values from -1.5 to 1.5
- w_rate: bfloat16 [2048, 128], P('fsdp'), may hold values from -0.5 to 0.5
- bias_rate: bfloat16 [2048], P('fsdp'), may hold values from -2.5 to 2.5
- w_inlet: bfloat16 [2048, 128], P('fsdp'), may hold values from -0.5 to 0.5
- bias_inlet: bfloat16 [2048], P('fsdp'), may hold values from -2.5 to 2.5
- decay_param: bfloat16 [2048], P('fsdp'), may hold values from 4 to 16
- w_out: bfloat16 [2048, 1536], P('fsdp'), may hold values from -0.25 to 0.25
- mlp_gain: bfloat16 [1536], P('fsdp'), may hold values from 0.5 to 1.5
- w_up: bfloat16 [1536, 4608], P('fsdp'), may hold values from -0.15625 to 0.15625
- w_value: bfloat16 [1536, 4608], P('fsdp'), may hold values from -0.15625 to 0.15625
- w_down: bfloat16 [4608, 1536], P('fsdp'), may hold values from -0.09375 to 0.09375
Outputs:
- block_output: float32 [8, 1024, 1536], P('fsdp', 'seq')
- grad_input: float32 [8, 1024, 1536], P('fsdp', 'seq')
- grad_norm_gain: float32 [1536], P(('seq', 'fsdp'))
- grad_w_gate: float32 [1536, 2048], P(('seq', 'fsdp'))
- grad_w_input: float32 [1536, 2048], P(('seq', 'fsdp'))
- grad_conv_weight: float32 [4, 2048], P(None, ('seq', 'fsdp'))
- grad_conv_bias: float32 [2048], P(('seq', 'fsdp'))
- grad_w_rate: float32 [2048, 128], P(('seq', 'fsdp'))
- grad_bias_rate: float32 [2048], P(('seq', 'fsdp'))
- grad_w_inlet: float32 [2048, 128], P(('seq', 'fsdp'))
- grad_bias_inlet: float32 [2048], P(('seq', 'fsdp'))
- grad_decay_param: float32 [2048], P(('seq', 'fsdp'))
- grad_w_out: float32 [2048, 1536], P(('seq', 'fsdp'))
- grad_mlp_gain: float32 [1536], P(('seq', 'fsdp'))
- grad_w_up: float32 [1536, 4608], P(('seq', 'fsdp'))
- grad_w_value: float32 [1536, 4608], P(('seq', 'fsdp'))
- grad_w_down: float32 [4608, 1536], P(('seq', 'fsdp'))
The draws below stay inside these ranges and needn't reach their ends.
Inputs may be any that keep to these rules, and one draw needn't show every extreme that they name: `valid_lengths`: on each index of fsdp one of its 2 sequences is valid to its end.
All inputs are finite; a program needn't handle non-finite values.
Results may differ from the reference program's by a relative error of at most 0.012.
Values may be sent and summed in bfloat16 or wider, within the bound.
A program may use at most 448 MiB of HBM per device.

```python
import math
import jax
import jax.numpy as jnp
from jax import lax

D = 1536
R = 2048
FF = 4608
HB = 128
CONV = 4
ROWS_DEV = 2
LENGTH = 1024
ROWS = 8


def draw_valid_lengths(key, part):
    key = jax.random.fold_in(key, 11)
    key_short, key_pick = jax.random.split(key)
    shorter = jax.random.randint(key_short, (ROWS,), LENGTH // 8, LENGTH + 1)
    picked = jax.random.randint(key_pick, (ROWS // ROWS_DEV,), 0, ROWS_DEV)
    slot_index = jnp.arange(ROWS, dtype=jnp.int32) % ROWS_DEV
    full_row = slot_index == jnp.repeat(picked, ROWS_DEV)
    return jnp.where(full_row, LENGTH, shorter).astype(jnp.int32)


def draw_decay_param(key, part):
    key = jax.random.fold_in(key, 5)
    key_kind, key_spot = jax.random.split(key)
    share = 0.5
    slow_kind = jax.random.uniform(key_kind, (R,), jnp.float32) < share
    spot = jax.random.uniform(key_spot, (R,), jnp.float32)
    slow_low = math.log(0.03 / LENGTH)
    slow_high = math.log(0.25 / LENGTH)
    fast_high = math.log(0.008)
    log_rate = jnp.where(slow_kind, slow_low + spot * (slow_high - slow_low), slow_high + spot * (fast_high - slow_high))
    rate_value = jnp.exp(log_rate)
    return (-jnp.log(jnp.expm1(rate_value))).astype(jnp.bfloat16)


def level_of(own_key, dims, shards, least, high):
    def one(position, shards_of):
        draws = jax.random.uniform(jax.random.fold_in(jax.random.fold_in(own_key, 6), position), (shards_of,), jnp.float32, least / len(shards), high / len(shards))
        return jnp.repeat(jnp.exp(draws), dims[position] // shards_of).reshape((-1,) + (1,) * (len(dims) - position - 1))

    level = one(*shards[0])
    for cut in shards[1:]:
        level = level * one(*cut)
    return level


def bell_draw(own_key, shape, spread, reach, pieces=(), kind=jnp.bfloat16):
    gain = level_of(own_key, shape, pieces, -0.22, 0.18) if pieces else 1.0
    array = jax.random.normal(own_key, shape, jnp.float32) * spread * gain
    return jnp.minimum(jnp.maximum(array, -reach), reach).astype(kind)


def setup_inputs(seed: int = 0) -> dict:
    seeds = jax.random.split(jax.random.key(seed), 19)
    block_input = bell_draw(seeds[0], (ROWS, LENGTH, D), 1.0, 6.0, ((0, 4), (1, 8)), jnp.float32)
    teacher = bell_draw(seeds[1], (ROWS, LENGTH, D), 1.0, 6.0, ((0, 4), (1, 8)), jnp.float32)
    valid_lengths = draw_valid_lengths(jax.random.fold_in(seeds[18], 71), 0)
    norm_gain = jnp.clip(1.0 + 0.1 * jax.random.normal(seeds[3], (D,), jnp.float32), 0.5, 1.5).astype(jnp.bfloat16)
    w_gate = bell_draw(seeds[4], (D, R), D ** -0.5, 0.15625, ((0, 4),))
    w_input = bell_draw(seeds[5], (D, R), D ** -0.5, 0.15625, ((0, 4),))
    conv_weight = bell_draw(seeds[6], (CONV, R), CONV ** -0.5, 3.0, ((1, 4),))
    conv_bias = bell_draw(seeds[7], (R,), 0.3, 1.5, ((0, 4),))
    w_rate = bell_draw(seeds[8], (R, HB), HB ** -0.5, 0.5, ((0, 4),))
    bias_rate = bell_draw(seeds[9], (R,), 0.5, 2.5, ((0, 4),))
    w_inlet = bell_draw(seeds[10], (R, HB), HB ** -0.5, 0.5, ((0, 4),))
    bias_inlet = bell_draw(seeds[11], (R,), 0.5, 2.5, ((0, 4),))
    decay_param = draw_decay_param(jax.random.fold_in(seeds[18], 71), 0)
    w_out = bell_draw(seeds[13], (R, D), (R // 4) ** -0.5, 0.25, ((0, 4),))
    mlp_gain = jnp.clip(1.0 + 0.1 * jax.random.normal(seeds[14], (D,), jnp.float32), 0.5, 1.5).astype(jnp.bfloat16)
    w_up = bell_draw(seeds[15], (D, FF), D ** -0.5, 0.15625, ((0, 4),))
    w_value = bell_draw(seeds[16], (D, FF), D ** -0.5, 0.15625, ((0, 4),))
    w_down = bell_draw(seeds[17], (FF, D), FF ** -0.5, 0.09375, ((0, 4),))
    return {"block_input": block_input, "teacher": teacher, "valid_lengths": valid_lengths, "norm_gain": norm_gain, "w_gate": w_gate, "w_input": w_input, "conv_weight": conv_weight, "conv_bias": conv_bias, "w_rate": w_rate, "bias_rate": bias_rate, "w_inlet": w_inlet, "bias_inlet": bias_inlet, "decay_param": decay_param, "w_out": w_out, "mlp_gain": mlp_gain, "w_up": w_up, "w_value": w_value, "w_down": w_down}


@jax.custom_vjp
def low(v):
    return lax.optimization_barrier(v.astype(jnp.bfloat16)).astype(jnp.float32)

@jax.custom_vjp
def low_back(v):
    return v

def low_keep(v):
    return (low(v), None)

def low_pass(kept, grad):
    return (grad,)

def back_keep(v):
    return (v, None)

def back_low(kept, grad):
    return (low(grad),)
low.defvjp(low_keep, low_pass)
low_back.defvjp(back_keep, back_low)
EPS_NORM = 1e-06
EPS_MULT = 0.0001
RATE_SCALE = 8.0

def matmul_high(left, right):
    return jnp.dot(left, right, precision=lax.Precision.HIGHEST)

def rms_scale(values, gain_vec):
    return values * lax.rsqrt(lax.optimization_barrier(jnp.mean(values * values, axis=-1, keepdims=True)) + EPS_NORM) * gain_vec

def gate_terms(rate_pre, inlet_pre, decay_vec, values):
    rate_gate = jax.nn.sigmoid(rate_pre)
    inlet_gate = jax.nn.sigmoid(inlet_pre)
    log_decay = -RATE_SCALE * rate_gate * jax.nn.softplus(-decay_vec)
    decay_now = jnp.exp(log_decay)
    factor = jnp.sqrt(EPS_MULT - jnp.expm1(2.0 * log_decay))
    return (decay_now, factor * inlet_gate * values)

def linear_step(first_pair, second_pair):
    return (first_pair[0] * second_pair[0], second_pair[1] + second_pair[0] * first_pair[1])

def head_product(values, blocks):
    head_count = R // HB
    shaped = values.reshape(values.shape[0], head_count, HB)
    stacked = blocks.reshape(head_count, HB, HB)
    return jnp.einsum('thi,hij->thj', shaped, stacked, precision=lax.Precision.HIGHEST).reshape(values.shape[0], R)

def row_forward(params, row_in):
    gain_one, w_gate, w_input, conv_w, conv_b, w_rate, bias_rate, w_inlet, bias_inlet, decay_vec, w_out, gain_two, w_up, w_value, w_down = params
    normed = low(rms_scale(row_in, gain_one))
    gate_pre = low_back(matmul_high(normed, w_gate))
    branch = low(low_back(matmul_high(normed, w_input)))
    padded = jnp.pad(branch, ((CONV - 1, 0), (0, 0)))
    conv_sum = conv_b
    for offset in range(CONV):
        conv_sum = conv_sum + conv_w[offset] * padded[CONV - 1 - offset:CONV - 1 - offset + LENGTH]
    conv_low = low(conv_sum)
    rate_pre = low_back(head_product(conv_low, w_rate)) + bias_rate
    inlet_pre = low_back(head_product(conv_low, w_inlet)) + bias_inlet
    decay_now, pushed = gate_terms(rate_pre, inlet_pre, decay_vec, conv_low)
    unused, states = lax.associative_scan(linear_step, (decay_now, pushed), axis=0)
    merged = low(states * jax.nn.gelu(gate_pre))
    middle = row_in + low_back(matmul_high(merged, w_out))
    normed_two = low(rms_scale(middle, gain_two))
    up_pre = low_back(matmul_high(normed_two, w_up))
    value_pre = low_back(matmul_high(normed_two, w_value))
    hidden = low(jax.nn.gelu(value_pre) * up_pre)
    return middle + low_back(matmul_high(hidden, w_down))

def reference(block_input, teacher, valid_lengths, norm_gain, w_gate, w_input, conv_weight, conv_bias, w_rate, bias_rate, w_inlet, bias_inlet, decay_param, w_out, mlp_gain, w_up, w_value, w_down):
    params = tuple((weight.astype(jnp.float32) for weight in (norm_gain, w_gate, w_input, conv_weight, conv_bias, w_rate, bias_rate, w_inlet, bias_inlet, decay_param, w_out, mlp_gain, w_up, w_value, w_down)))

    def forward(inputs, weights):

        def one_row(row_in):
            return row_forward(weights, row_in)
        return lax.map(jax.checkpoint(one_row), inputs)
    block_output, pullback = jax.vjp(forward, block_input.astype(jnp.float32), params)
    positions = jnp.arange(LENGTH, dtype=jnp.int32)
    valid_mask = positions[None, :] < valid_lengths[:, None]
    count = jnp.sum(valid_lengths).astype(jnp.float32)
    grad_out = jnp.where(valid_mask[:, :, None], block_output - teacher, 0.0) * (ROWS * LENGTH / count)
    grad_input, grads = pullback(grad_out)
    return (block_output, grad_input) + tuple(grads)
```

```python
import jax
import jax.numpy as jnp
from jax import lax
from jax.sharding import PartitionSpec as P
from jax.experimental import pallas as pl
from jax.experimental.pallas import tpu as pltpu

EPS_NORM = 1e-06
EPS_MULT = 0.0001
RATE_SCALE = 8.0
BF = jnp.bfloat16
F32 = jnp.float32
GROUP = "fsdp"
BOTH = ("seq", "fsdp")


def mm(left, right):
    return jnp.dot(left, right, preferred_element_type=F32)


def mm_lt(left, right):
    return lax.dot_general(left, right, (((0,), (0,)), ((), ())), preferred_element_type=F32)


def mm_rt(left, right):
    return lax.dot_general(left, right, (((1,), (1,)), ((), ())), preferred_element_type=F32)


def gelu_pair(v):
    c = 0.7978845608028654
    a = 0.044715
    u = c * (v + a * v * v * v)
    t = jnp.tanh(u)
    g = 0.5 * v * (1.0 + t)
    d = 0.5 * (1.0 + t) + 0.5 * v * (1.0 - t * t) * c * (1.0 + 3.0 * a * v * v)
    return g, d


def linear_step(first_pair, second_pair):
    return (first_pair[0] * second_pair[0], second_pair[1] + second_pair[0] * first_pair[1])


def rms(v, g):
    s = lax.rsqrt(jnp.mean(v * v, axis=-1, keepdims=True) + EPS_NORM)
    return (v * s * g).astype(BF), s


def rms_back(v, s, g, grad):
    gg = grad * g
    gain = jnp.sum(grad * v * s, axis=0)
    return s * gg - v * (s * s * s) * jnp.mean(gg * v, axis=-1, keepdims=True), gain


def ag(a):
    return lax.all_gather(a, GROUP, axis=0, tiled=True)


def rs(a):
    return lax.psum_scatter(a.astype(BF), GROUP, scatter_dimension=0, tiled=True).astype(F32)


def grads_cols(g):
    part = lax.psum_scatter(g.astype(BF), "seq", scatter_dimension=0, tiled=True)
    return lax.all_to_all(part, GROUP, split_axis=0, concat_axis=1, tiled=True).astype(F32)


def grads_rows(g):
    n, m = lax.axis_size("seq"), lax.axis_size(GROUP)
    part = lax.psum_scatter(g.astype(BF), "seq", scatter_dimension=0, tiled=True)
    pairs = [(j * m + f, f * n + j) for j in range(n) for f in range(m)]
    return lax.ppermute(part, BOTH, pairs).astype(F32)


def shifted(shard, axis, by):
    length = lax.axis_size(axis)
    pairs = [(i, i + by) for i in range(length) if 0 <= i + by < length]
    return lax.ppermute(shard, axis, pairs)


MESH = pl.DeviceIdType.MESH
VMEM = pl.BlockSpec(memory_space=pltpu.VMEM)
ANY = pl.BlockSpec(memory_space=pl.ANY)
LIMIT = 60 * 2**20


def ds(start, size):
    if not isinstance(start, int):
        start = pl.multiple_of(start, size if size % 128 else 128)
    return pl.ds(start, size)


def rows_at(block, size):
    return pl.ds(pl.multiple_of(block * size, size), size)


class Place:
    def __init__(self):
        self.n = lax.axis_size("seq")
        self.s, self.f = lax.axis_index("seq"), lax.axis_index("fsdp")
        f = self.f
        self.p1 = f + 1 - 2 * lax.rem(f, 2)
        self.p2 = lax.rem(f + 2, 4)
        self.p3 = lax.rem(self.p1 + 2, 4)
        self.sx = self.s + 1 - 2 * lax.rem(self.s, 2)

    def group(self, f):
        return (self.s, f)

    def line(self, s):
        return (s, self.f)

    def greet(self, whole_line=True):
        barrier = pltpu.get_barrier_semaphore()
        for f in (self.p1, self.p2, self.p3):
            pl.semaphore_signal(barrier, inc=1, device_id=self.group(f), device_id_type=MESH)

        def one(j, _):
            pl.semaphore_signal(
                barrier, inc=1, device_id=self.line(lax.rem(self.s + j, self.n)), device_id_type=MESH
            )
            return 0

        lax.fori_loop(1, self.n, one, 0)
        pl.semaphore_wait(barrier, 3 + self.n - 1)


class Sems:
    def __init__(self, ref):
        self.ref, self.used = ref, 0

    def take(self):
        self.used += 1
        return self.ref.at[self.used - 1]

    def remote(self, src, dst, device):
        return pltpu.make_async_remote_copy(
            src_ref=src, dst_ref=dst, send_sem=self.take(), recv_sem=self.take(),
            device_id=device, device_id_type=MESH,
        )

    def local(self, src, dst):
        copy = pltpu.make_async_copy(src, dst, self.take())
        copy.start()
        return copy


class Gather:
    def __init__(self, at, sems, buf, chunk):
        self.at, self.buf, self.chunk = at, buf, chunk
        mine = lambda f, r: buf.at[rows_at(f * 2 + r, chunk)]
        self.core = [sems.remote(mine(at.f, r), mine(at.f, r), at.group(at.p1)) for r in range(2)]
        self.over = [sems.remote(mine(at.f, r), mine(at.f, r), at.group(at.p2)) for r in range(2)]
        self.pass_on = [sems.remote(mine(at.p2, r), mine(at.p2, r), at.group(at.p1)) for r in range(2)]

    def send(self, r):
        self.over[r].start()
        self.core[r].start()

    def relay(self, r):
        self.over[r].wait_recv()
        self.pass_on[r].start()

    def finish(self):
        for r in range(2):
            self.core[r].wait()
            self.over[r].wait_send()
            self.pass_on[r].wait()


class Scatter:
    def __init__(self, at, sems, core_out, core_in, over_out, over_in, chunk):
        self.at, self.chunk = at, chunk
        self.core_out, self.core_in, self.over_out, self.over_in = core_out, core_in, over_out, over_in
        self.core = [sems.remote(core_out.at[k], core_in.at[k], at.group(at.p1)) for k in range(2)]
        self.over = [
            sems.remote(
                over_out.at[pl.ds(r * chunk, chunk)], over_in.at[pl.ds(r * chunk, chunk)], at.group(at.p2)
            )
            for r in range(2)
        ]

    def run(self, partial, own, between=lambda k: None):
        at = self.at

        def put(ref):
            def store(sl, cols, tile):
                ref[sl, cols] = tile.astype(BF)

            return store

        partial(at.p3, put(self.core_out.at[0]))
        self.core[0].start()
        between(0)

        def add_over(sl, cols, tile):
            self.over_out[sl, cols] = (tile + self.core_in[0, sl, cols].astype(F32)).astype(BF)

        self.core[0].wait_recv()
        partial(at.p2, add_over)
        for r in range(2):
            self.over[r].start()
        between(1)
        partial(at.p1, put(self.core_out.at[1]))
        self.core[1].start()
        between(2)
        self.core[1].wait_recv()

        def add_own(sl, cols, tile):
            own[sl, cols] = own[sl, cols] + tile + self.core_in[1, sl, cols].astype(F32)

        partial(at.f, add_own)
        between(3)

    def arrived(self, r):
        self.over[r].wait_recv()
        return self.over_in[pl.ds(r * self.chunk, self.chunk), :].astype(F32)

    def finish(self):
        for copy in self.core + self.over:
            copy.wait_send()


class Columns:
    def __init__(self, at, sems, weights, buf):
        self.at = at
        rows, width = weights[0].shape
        part = width // 4
        half = rows // 2
        h = lax.rem(at.s, 2)
        self.half, self.rows, self.part, self.buf, self.sems = half, rows, part, buf, sems
        self.near, self.own, self.far, self.side = [], [], [], []
        for k, w in enumerate(weights):
            cols = pl.ds(k * part, part)
            take = lambda f: pl.ds(pl.multiple_of(f * part, 128), part)
            mine = pl.ds(pl.multiple_of(at.f * rows, rows), rows)
            cut = pl.ds(pl.multiple_of(h * half, half), half)
            mine_cut = pl.ds(pl.multiple_of(at.f * rows + h * half, half), half)
            self.own.append(pltpu.make_async_copy(w.at[:, take(at.f)], buf.at[mine, cols], sems.take()))
            self.near.append(sems.remote(w.at[:, take(at.p1)], buf.at[mine, cols], at.group(at.p1)))
            for p in (at.p2, at.p3):
                self.far.append(sems.remote(w.at[cut, take(p)], buf.at[mine_cut, cols], at.group(p)))
                came = buf.at[pl.ds(pl.multiple_of(p * rows + h * half, half), half), cols]
                self.side.append(sems.remote(came, came, at.line(at.sx)))

    def start_far(self):
        for c in self.far:
            c.start()

    def start_near(self):
        for c in self.near + self.own:
            c.start()

    def relay(self, k):
        self.far[k].wait_recv()
        self.side[k].start()

    def finish(self):
        for c in self.own + self.near + self.side:
            c.wait()
        for c in self.far:
            c.wait_send()


def expm1_neg(v):
    series = v * (1 + v * (1 / 2) * (1 + v * (1 / 3) * (1 + v * (1 / 4) * (1 + v * (1 / 5) * (1 + v * (1 / 6))))))
    return jnp.where(v > -0.25, series, jnp.exp(v) - 1.0)


def swap_rows(src, dst, outer, kind):
    total, width = src.shape
    inner = total // outer

    def one(c, _):
        cols = pl.ds(pl.multiple_of(c * 128, 128), 128)
        v = src[:, cols].reshape(outer, inner, 128)
        dst[:, cols] = jnp.swapaxes(v, 0, 1).reshape(total, 128).astype(kind)
        return 0

    lax.fori_loop(0, width // 128, one, 0)


def forward_branch(x, gains, chan, wr, wl, wo, wg, wi, wu, wv,
                   wgi_o, wuv_o, normed_o, n2_o, middle_o, gate_o, pad_o, conv_o, rate_o, inlet_o, decay_o, states_o,
                   merged_o, ends_o, gain_o,
                   wgi, normed, n2, middle, gain, gate, pad, conv, rate, inlet, decay, states, work, merged, ends,
                   tot, core_out, core_in, over_out, over_in, sem, tsend, trecv):
    at = Place()
    here, width = x.shape
    toks = here // 2
    chans = chan.shape[1]
    part = width // 4
    taps = 4
    steps = toks
    group = 8
    halo = (taps - 1) * group
    sems = Sems(sem)
    at.greet()

    shares = [
        sems.remote(gains, gain.at[at.f], at.group(p)) for p in (at.p1, at.p2, at.p3)
    ]
    for c in shares:
        c.start()
    gain[at.f] = gains[...]
    gi = Columns(at, sems, [wg, wi], wgi)
    gi.start_far()
    gi.start_near()
    uv = Columns(at, sems, [wu, wv], wuv_o)
    uv.start_near()
    ag1 = Gather(at, sems, normed, toks)
    for c in shares:
        c.wait()
    for r in range(2):
        sl = pl.ds(r * toks, toks)
        v = x[sl, :]
        scale = lax.rsqrt(jnp.mean(v * v, axis=-1, keepdims=True) + EPS_NORM)
        for p in range(4):
            cols = pl.ds(p * part, part)
            normed[rows_at(at.f * 2 + r, toks), cols] = (x[sl, cols] * scale * gain[p, 0:1, :]).astype(BF)
        ag1.send(r)
    for k in range(4):
        gi.relay(k)
    ag1.relay(0)
    uv.start_far()
    ag1.relay(1)
    ag1.finish()
    gi.finish()
    saves = [sems.local(normed, normed_o), sems.local(wgi, wgi_o), sems.local(gain, gain_o)]

    def branch_rows(m, _):
        sl = rows_at(m, here)
        work[sl, :] = mm(normed[sl, :], wgi[:, chans:]).astype(BF).astype(F32)
        return 0

    lax.fori_loop(0, 4, branch_rows, 0)
    swap_rows(work, pad.at[pl.ds(halo, steps * group)], group, F32)
    edge = pad.at[pl.ds(steps * group, halo)]
    next_one = lax.rem(at.s + 1, at.n)
    tail = sems.remote(edge, pad.at[pl.ds(0, halo)], at.line(next_one))

    @pl.when(at.s < at.n - 1)
    def _():
        tail.start()

    @pl.when(at.s == 0)
    def _():
        pad[0:halo, :] = jnp.zeros((halo, chans), F32)

    def gate_rows(m, _):
        sl = rows_at(m, here)
        work[sl, :] = mm(normed[sl, :], wgi[:, :chans])
        return 0

    lax.fori_loop(0, 4, gate_rows, 0)
    swap_rows(work, gate, group, F32)

    @pl.when(at.s > 0)
    def _():
        tail.wait_recv()

    @pl.when(at.s < at.n - 1)
    def _():
        tail.wait_send()

    uv.relay(0)

    def gates(b, _):
        for h in range(chans // 128):
            cols = pl.ds(h * 128, 128)
            size = 128
            start = pl.multiple_of(b * size, size)
            sl = pl.ds(start, size)
            total = chan[taps : taps + 1, cols]
            for k in range(taps):
                total = total + chan[k : k + 1, cols] * pad[pl.ds(start + (halo - group * k), size), cols]
            low = total.astype(BF)
            blocks = pl.ds(h * 128, 128)
            r = jax.nn.sigmoid(mm(low, wr[blocks, :]) + chan[5:6, cols])
            i = jax.nn.sigmoid(mm(low, wl[blocks, :]) + chan[6:7, cols])
            ld = r * chan[7:8, cols]
            low = low.astype(F32)
            decay[sl, cols] = jnp.exp(ld)
            work[sl, cols] = jnp.sqrt(EPS_MULT - expm1_neg(2.0 * ld)) * i * low
            conv[sl, cols] = low
            rate[sl, cols] = r
            inlet[sl, cols] = i
        return 0

    lax.fori_loop(0, steps * group // 128, gates, 0)
    saves += [
        sems.local(gate, gate_o), sems.local(pad, pad_o), sems.local(conv, conv_o), sems.local(rate, rate_o),
        sems.local(inlet, inlet_o), sems.local(decay, decay_o),
    ]

    unroll = 8

    def totals(b, carry):
        h, p = carry
        for u in range(unroll):
            sl = pl.ds(pl.multiple_of((b * unroll + u) * group, group), group)
            a = decay[sl, :]
            h = a * h + work[sl, :]
            p = p * a
        return h, p

    zero = jnp.zeros((group, chans), F32)
    h, p = lax.fori_loop(0, steps // unroll, totals, (zero, zero + 1.0))
    ends[0:8, :] = p
    ends[8:16, :] = h

    def total_copy(src, to):
        return pltpu.make_async_remote_copy(
            src_ref=ends.at[pl.ds(0, 16)], dst_ref=tot.at[src], send_sem=tsend.at[to], recv_sem=trecv.at[src],
            device_id=at.line(to), device_id_type=MESH,
        )

    def send_total(j, _):
        total_copy(at.s, j).start()
        return 0

    lax.fori_loop(at.s + 1, at.n, send_total, 0)
    uv.relay(1)

    def enter(j, state):
        total_copy(j, j).wait_recv()
        return tot[j, 0:8, :] * state + tot[j, 8:16, :]

    state_in = lax.fori_loop(0, at.s, enter, zero)

    def sent_total(j, _):
        total_copy(at.s, j).wait_send()
        return 0

    lax.fori_loop(at.s + 1, at.n, sent_total, 0)
    ends[16:24, :] = state_in

    def scan(b, h):
        for u in range(unroll):
            sl = pl.ds(pl.multiple_of((b * unroll + u) * group, group), group)
            h = decay[sl, :] * h + work[sl, :]
            states[sl, :] = h
        return h

    lax.fori_loop(0, steps // unroll, scan, state_in)
    saves += [sems.local(states, states_o), sems.local(ends, ends_o)]

    def merge(c, _):
        cols = pl.ds(pl.multiple_of(c * 128, 128), 128)

        def some(b, _):
            sl = rows_at(b, 128)
            work[sl, cols] = states[sl, cols] * gelu_pair(gate[sl, cols])[0]
            return 0

        lax.fori_loop(0, steps * group // 128, some, 0)
        return 0

    lax.fori_loop(0, chans // 128, merge, 0)
    swap_rows(work, merged, steps, BF)
    saves += [sems.local(merged, merged_o)]

    middle[...] = x[...]
    sc = Scatter(at, sems, core_out, core_in, over_out, over_in, toks)

    def partial(o, store):
        def half(r, _):
            sl = rows_at(r, toks)
            tile = mm(merged[rows_at(o * 2 + r, toks), :], wo[...])
            store(sl, slice(None), tile)
            return 0

        lax.fori_loop(0, 2, half, 0)

    sc.run(partial, middle)
    ag2 = Gather(at, sems, n2, toks)
    for r in range(2):
        sl = pl.ds(r * toks, toks)
        v = middle[sl, :] + sc.arrived(r)
        middle[sl, :] = v
        scale = lax.rsqrt(jnp.mean(v * v, axis=-1, keepdims=True) + EPS_NORM)
        for p in range(4):
            cols = pl.ds(p * part, part)
            n2[rows_at(at.f * 2 + r, toks), cols] = (middle[sl, cols] * scale * gain[p, 1:2, :]).astype(BF)
        ag2.send(r)
    saves += [sems.local(middle, middle_o)]
    uv.relay(2)
    uv.relay(3)
    for r in range(2):
        ag2.relay(r)
    ag2.finish()
    sc.finish()
    saves += [sems.local(n2, n2_o)]
    uv.finish()
    for c in saves:
        c.wait()


def call_forward(x, gains, chan, wr, wl, wo, wg, wi, wu, wv):
    here, width = x.shape
    chans = chan.shape[1]
    ffl = wu.shape[1] // 4
    every = here * 4
    n = lax.axis_size("seq")
    f32 = lambda *s: jax.ShapeDtypeStruct(s, F32)
    bf = lambda *s: jax.ShapeDtypeStruct(s, BF)
    vf = lambda *s: pltpu.VMEM(s, F32)
    vb = lambda *s: pltpu.VMEM(s, BF)
    outs = [
        bf(width, 2 * chans), bf(width, 2 * ffl), bf(every, width), bf(every, width), f32(here, width),
        f32(every, chans), f32(every + 24, chans), f32(every, chans), f32(every, chans), f32(every, chans),
        f32(every, chans), f32(every, chans), bf(every, chans), f32(24, chans), f32(4, 8, width // 4),
    ]
    scratch = [
        vb(width, 2 * chans), vb(every, width), vb(every, width), vf(here, width), vf(4, 8, width // 4),
        vf(every, chans), vf(every + 24, chans), vf(every, chans), vf(every, chans), vf(every, chans),
        vf(every, chans), vf(every, chans), vf(every, chans), vb(every, chans), vf(24, chans),
        vf(n, 16, chans), vb(2, here, width), vb(2, here, width), vb(here, width), vb(here, width),
        pltpu.SemaphoreType.DMA((120,)), pltpu.SemaphoreType.DMA((n,)), pltpu.SemaphoreType.DMA((n,)),
    ]
    return pl.pallas_call(
        forward_branch,
        out_shape=outs,
        in_specs=[VMEM] * 6 + [ANY] * 4,
        out_specs=[ANY] * len(outs),
        scratch_shapes=scratch,
        compiler_params=pltpu.CompilerParams(collective_id=1, has_side_effects=True, vmem_limit_bytes=LIMIT),
        name="forward_branch",
    )(x, gains, chan, wr, wl, wo, wg, wi, wu, wv)


def body(
    block_input, teacher, valid_lengths, norm_gain, w_gate, w_input, conv_weight, conv_bias,
    w_rate, bias_rate, w_inlet, bias_inlet, decay_param, w_out, mlp_gain, w_up, w_value, w_down,
):
    n_seq, n_fs = lax.axis_size("seq"), lax.axis_size(GROUP)
    si, fi = lax.axis_index("seq"), lax.axis_index(GROUP)
    rows_dev, toks, width = block_input.shape
    rows = rows_dev * n_fs
    here = rows_dev * toks
    chans = conv_bias.shape[0]
    hb = w_rate.shape[1]
    heads = chans // hb
    taps = conv_weight.shape[0]

    cw = conv_weight.astype(F32)
    heads_shape = (heads, hb, hb)
    wr, wl = w_rate.reshape(heads_shape), w_inlet.reshape(heads_shape)
    sp = jax.nn.softplus(-decay_param.astype(F32))
    x = block_input.reshape(here, width)
    gains = jnp.concatenate([norm_gain[None].astype(F32), mlp_gain[None].astype(F32), jnp.zeros((6, width // 4), F32)])
    vec = lambda v: v.astype(F32)[None]
    chan = jnp.concatenate([cw, vec(conv_bias), vec(bias_rate), vec(bias_inlet), vec(-RATE_SCALE * sp), jnp.zeros((8, chans), F32)])
    (wgi, wuv, normed, n2, middle, gate_tm, pad_tm, conv_tm, rate_tm, inlet_tm, decay_tm, states_tm, merged, ends, gain) = call_forward(
        x, gains, chan, w_rate, w_inlet, w_out, w_gate, w_input, w_up, w_value)
    wg, wi = wgi[:, :chans], wgi[:, chans:]
    wu, wv = wuv[:, :wuv.shape[1]//2], wuv[:, wuv.shape[1]//2:]
    gain_one, gain_two = gain[:, 0].reshape(-1), gain[:, 1].reshape(-1)
    s1 = lax.rsqrt(jnp.mean(x * x, axis=-1, keepdims=True) + EPS_NORM)
    s2 = lax.rsqrt(jnp.mean(middle * middle, axis=-1, keepdims=True) + EPS_NORM)
    tok = lambda v: v.reshape(-1, rows, chans).swapaxes(0, 1)
    padded, clf, r, i, decay, states = tok(pad_tm), tok(conv_tm), tok(rate_tm), tok(inlet_tm), tok(decay_tm), tok(states_tm)
    conv_low = clf.astype(BF)
    heads_in = conv_low.reshape(rows * toks, heads, hb)
    gate_pre = tok(gate_tm).reshape(-1, chans)
    gg, gd = gelu_pair(gate_pre)
    cum_end, state_in = ends[:8], ends[16:24]
    prev = jnp.concatenate([state_in[:, None], states[:, :-1]], axis=1)
    ld = -RATE_SCALE * r * sp
    factor = jnp.sqrt(EPS_MULT - jnp.expm1(2.0 * ld))
    up = mm(n2, wu)
    value = mm(n2, wv)
    vg, vd = gelu_pair(value)
    hidden = (vg * up).astype(BF)
    result = middle + rs(mm(hidden, w_down))
    lens = lax.dynamic_slice_in_dim(valid_lengths, fi * rows_dev, rows_dev)
    pos = si * toks + jnp.arange(toks, dtype=jnp.int32)
    mask = (pos[None, :] < lens[:, None]).reshape(here, 1)
    slots = valid_lengths.shape[0] * toks * n_seq
    count = jnp.sum(valid_lengths).astype(F32)
    grad_out = jnp.where(mask, result - teacher.reshape(here, width), 0.0) * (slots / count)
    gdi = ag(grad_out.astype(BF))
    g_down = mm_lt(hidden, gdi)
    gh = mm_rt(gdi, w_down)
    gu = (gh * vg).astype(BF)
    gv = (gh * up * vd).astype(BF)
    g_up = mm_lt(n2, gu)
    g_value = mm_lt(n2, gv)
    gn2 = rs(mm_rt(gu, wu) + mm_rt(gv, wv))
    gm_norm, gain2 = rms_back(middle, s2, gain_two, gn2)
    grad_middle = grad_out + gm_norm
    gml = ag(grad_middle.astype(BF))
    g_out = mm_lt(merged, gml)
    gmer = mm_rt(gml, w_out)
    gst = (gmer * gg).reshape(rows, toks, chans)
    ggate = (gmer * states.reshape(-1, chans) * gd).astype(BF)
    nextd = jnp.concatenate([decay[:, 1:], jnp.ones((rows, 1, chans), F32)], axis=1)
    carry, ladj = lax.associative_scan(linear_step, (nextd, gst), axis=1, reverse=True)
    tot2 = lax.all_gather(jnp.stack([cum_end, decay[:, 0] * ladj[:, 0]]), "seq")
    adj_in = jnp.zeros((rows, chans), F32)
    for j in reversed(range(n_seq)):
        adj_in = jnp.where(j > si, tot2[j, 0] * adj_in + tot2[j, 1], adj_in)
    adj = ladj + carry * adj_in[:, None]
    gdec = adj * prev
    gfac = adj * i * clf
    gld = gdec * decay - gfac * (decay * decay) / factor
    grate = gld * (-RATE_SCALE * sp) * r * (1.0 - r)
    ginl = adj * factor * clf * i * (1.0 - i)
    gdp = jnp.sum(gld * r, axis=(0, 1)) * RATE_SCALE * jax.nn.sigmoid(-decay_param.astype(F32))
    gcd = adj * factor * i
    grb, gib = jnp.sum(grate, (0, 1)), jnp.sum(ginl, (0, 1))
    grl, gil = grate.astype(BF).reshape(-1, heads, hb), ginl.astype(BF).reshape(-1, heads, hb)
    gwr = jnp.einsum("nhi,nhj->hij", heads_in, grl, preferred_element_type=F32).reshape(chans, hb)
    gwi = jnp.einsum("nhi,nhj->hij", heads_in, gil, preferred_element_type=F32).reshape(chans, hb)
    bk = lambda a, w: jnp.einsum("nhj,hij->nhi", a, w, preferred_element_type=F32).reshape(rows, toks, chans)
    gconv = gcd + bk(grl, wr) + bk(gil, wl)
    gcw = jnp.stack([jnp.sum(gconv * padded[:, taps - 1 - k: taps - 1 - k + toks], (0, 1)) for k in range(taps)])
    gcb = jnp.sum(gconv, (0, 1))
    gpad = jnp.zeros((rows, toks + taps - 1, chans), F32)
    for k in range(taps):
        gpad = gpad.at[:, taps - 1 - k: taps - 1 - k + toks].add(cw[k] * gconv)
    edge = shifted(gpad[:, : taps - 1], "seq", -1)
    gbr = gpad[:, taps - 1:].at[:, toks - (taps - 1):].add(edge).reshape(-1, chans).astype(BF)
    g_gate = mm_lt(normed, ggate)
    g_input = mm_lt(normed, gbr)
    gn1 = rs(mm_rt(ggate, wg) + mm_rt(gbr, wi))
    gi_norm, gain1 = rms_back(x, s1, gain_one, gn1)
    grad_input = grad_middle + gi_norm

    chan = jnp.concatenate([gcw, gcb[None], grb[None], gib[None], gdp[None]], 0)
    per = chans // n_seq
    chan = chan.reshape(8, n_seq, per).transpose(1, 0, 2).reshape(n_seq, 8 * per)
    blk = jnp.zeros((n_fs, n_seq, 8 * per), F32).at[fi].set(chan).reshape(n_fs * n_seq, 8 * per)
    gw = jnp.stack([gain1, gain2]).reshape(2, n_fs * n_seq, -1).transpose(1, 0, 2).reshape(n_fs * n_seq, -1)
    small = lax.psum_scatter(jnp.concatenate([blk, gw], 1), BOTH, scatter_dimension=0, tiled=True)[0]
    ch = small[: 8 * per].reshape(8, per)
    gn = small[8 * per:].reshape(2, -1)
    og = grads_rows(jnp.concatenate([g_out, gwr, gwi], 1))
    return (
        result.reshape(block_input.shape), grad_input.reshape(block_input.shape), gn[0],
        grads_cols(g_gate), grads_cols(g_input), ch[:4], ch[4], og[:, width: width + hb], ch[5],
        og[:, width + hb:], ch[6], ch[7], og[:, :width], gn[1], grads_cols(g_up), grads_cols(g_value), grads_rows(g_down),
    )


def solution(mesh):
    rowsh, vec, mat = P("fsdp", "seq", None), P("fsdp"), P("fsdp", None)
    ov, om = P(BOTH), P(BOTH, None)
    return jax.shard_map(
        body,
        mesh=mesh,
        in_specs=(rowsh, rowsh, P(), vec, mat, mat, P(None, "fsdp"), vec, mat, vec, mat, vec, vec, mat, vec, mat, mat, mat),
        out_specs=(rowsh, rowsh, ov, om, om, P(None, BOTH), ov, om, ov, om, ov, ov, om, ov, om, om, om),
        check_vma=False,
    )
```

```python
import jax
import jax.numpy as jnp
from jax import lax
from jax.sharding import PartitionSpec as P
from jax.experimental import pallas as pl
from jax.experimental.pallas import tpu as pltpu

EPS_NORM = 1e-06
EPS_MULT = 0.0001
RATE_SCALE = 8.0
BF = jnp.bfloat16
F32 = jnp.float32
GROUP = "fsdp"
BOTH = ("seq", "fsdp")


def mm(left, right):
    return jnp.dot(left, right, preferred_element_type=F32)


def mm_lt(left, right):
    return lax.dot_general(left, right, (((0,), (0,)), ((), ())), preferred_element_type=F32)


def mm_rt(left, right):
    return lax.dot_general(left, right, (((1,), (1,)), ((), ())), preferred_element_type=F32)


def gelu_pair(v):
    c = 0.7978845608028654
    a = 0.044715
    u = c * (v + a * v * v * v)
    t = jnp.tanh(u)
    g = 0.5 * v * (1.0 + t)
    d = 0.5 * (1.0 + t) + 0.5 * v * (1.0 - t * t) * c * (1.0 + 3.0 * a * v * v)
    return g, d


def linear_step(first_pair, second_pair):
    return (first_pair[0] * second_pair[0], second_pair[1] + second_pair[0] * first_pair[1])


def rms(v, g):
    s = lax.rsqrt(jnp.mean(v * v, axis=-1, keepdims=True) + EPS_NORM)
    return (v * s * g).astype(BF), s


def rms_back(v, s, g, grad):
    gg = grad * g
    gain = jnp.sum(grad * v * s, axis=0)
    return s * gg - v * (s * s * s) * jnp.mean(gg * v, axis=-1, keepdims=True), gain


def ag(a):
    return lax.all_gather(a, GROUP, axis=0, tiled=True)


def rs(a):
    return lax.psum_scatter(a.astype(BF), GROUP, scatter_dimension=0, tiled=True).astype(F32)


def grads_cols(g):
    part = lax.psum_scatter(g.astype(BF), "seq", scatter_dimension=0, tiled=True)
    return lax.all_to_all(part, GROUP, split_axis=0, concat_axis=1, tiled=True).astype(F32)


def grads_rows(g):
    n, m = lax.axis_size("seq"), lax.axis_size(GROUP)
    part = lax.psum_scatter(g.astype(BF), "seq", scatter_dimension=0, tiled=True)
    pairs = [(j * m + f, f * n + j) for j in range(n) for f in range(m)]
    return lax.ppermute(part, BOTH, pairs).astype(F32)


def shifted(shard, axis, by):
    length = lax.axis_size(axis)
    pairs = [(i, i + by) for i in range(length) if 0 <= i + by < length]
    return lax.ppermute(shard, axis, pairs)


MESH = pl.DeviceIdType.MESH
VMEM = pl.BlockSpec(memory_space=pltpu.VMEM)
ANY = pl.BlockSpec(memory_space=pl.ANY)
LIMIT = 60 * 2**20


def ds(start, size):
    if not isinstance(start, int):
        start = pl.multiple_of(start, size if size % 128 else 128)
    return pl.ds(start, size)


def rows_at(block, size):
    return pl.ds(pl.multiple_of(block * size, size), size)


class Place:
    def __init__(self):
        self.n = lax.axis_size("seq")
        self.s, self.f = lax.axis_index("seq"), lax.axis_index("fsdp")
        f = self.f
        self.p1 = f + 1 - 2 * lax.rem(f, 2)
        self.p2 = lax.rem(f + 2, 4)
        self.p3 = lax.rem(self.p1 + 2, 4)
        self.sx = self.s + 1 - 2 * lax.rem(self.s, 2)

    def group(self, f):
        return (self.s, f)

    def line(self, s):
        return (s, self.f)

    def greet(self, hop=None):
        barrier = pltpu.get_barrier_semaphore()
        for f in (self.p1, self.p2, self.p3):
            pl.semaphore_signal(barrier, inc=1, device_id=self.group(f), device_id_type=MESH)

        def one(j, _):
            pl.semaphore_signal(
                barrier, inc=1, device_id=self.line(lax.rem(self.s + j, self.n)), device_id_type=MESH
            )
            return 0

        lax.fori_loop(1, self.n, one, 0)
        pl.semaphore_wait(barrier, 3 + self.n - 1 + (0 if hop is None else hop.greet(barrier)))


class Sems:
    def __init__(self, ref):
        self.ref, self.used = ref, 0

    def take(self):
        self.used += 1
        return self.ref.at[self.used - 1]

    def remote(self, src, dst, device):
        return pltpu.make_async_remote_copy(
            src_ref=src, dst_ref=dst, send_sem=self.take(), recv_sem=self.take(),
            device_id=device, device_id_type=MESH,
        )

    def local(self, src, dst):
        copy = pltpu.make_async_copy(src, dst, self.take())
        copy.start()
        return copy


class Gather:
    def __init__(self, at, sems, buf, chunk):
        self.at, self.buf, self.chunk = at, buf, chunk
        mine = lambda f, r: buf.at[rows_at(f * 2 + r, chunk)]
        self.core = [sems.remote(mine(at.f, r), mine(at.f, r), at.group(at.p1)) for r in range(2)]
        self.over = [sems.remote(mine(at.f, r), mine(at.f, r), at.group(at.p2)) for r in range(2)]
        self.pass_on = [sems.remote(mine(at.p2, r), mine(at.p2, r), at.group(at.p1)) for r in range(2)]

    def send(self, r):
        self.over[r].start()
        self.core[r].start()

    def relay(self, r):
        self.over[r].wait_recv()
        self.pass_on[r].start()

    def finish(self):
        for r in range(2):
            self.core[r].wait()
            self.over[r].wait_send()
            self.pass_on[r].wait()


class Scatter:
    def __init__(self, at, sems, core_out, core_in, over_out, over_in, chunk):
        self.at, self.chunk = at, chunk
        self.core_out, self.core_in, self.over_out, self.over_in = core_out, core_in, over_out, over_in
        self.core = [sems.remote(core_out.at[k], core_in.at[k], at.group(at.p1)) for k in range(2)]
        self.over = [
            sems.remote(
                over_out.at[pl.ds(r * chunk, chunk)], over_in.at[pl.ds(r * chunk, chunk)], at.group(at.p2)
            )
            for r in range(2)
        ]

    def run(self, partial, own, between=lambda k: None):
        at = self.at

        def put(ref):
            def store(sl, cols, tile):
                ref[sl, cols] = tile.astype(BF)

            return store

        partial(at.p3, put(self.core_out.at[0]))
        self.core[0].start()
        between(0)

        def add_over(sl, cols, tile):
            self.over_out[sl, cols] = (tile + self.core_in[0, sl, cols].astype(F32)).astype(BF)

        self.core[0].wait_recv()
        partial(at.p2, add_over)
        for r in range(2):
            self.over[r].start()
        between(1)
        partial(at.p1, put(self.core_out.at[1]))
        self.core[1].start()
        between(2)
        self.core[1].wait_recv()

        def add_own(sl, cols, tile):
            own[sl, cols] = own[sl, cols] + tile + self.core_in[1, sl, cols].astype(F32)

        partial(at.f, add_own)
        between(3)

    def run_tile(self, compute, tile, own, between=lambda k: None):
        at = self.at

        def one(k, _):
            compute(jnp.where(k == 0, at.p3, jnp.where(k == 1, at.p2, jnp.where(k == 2, at.p1, at.f))))

            @pl.when(k == 0)
            def _():
                self.core_out[0] = tile[...].astype(BF)
                self.core[0].start()

            @pl.when(k == 1)
            def _():
                self.core[0].wait_recv()
                for r in range(2):
                    sl = pl.ds(r * self.chunk, self.chunk)
                    self.over_out[sl, :] = (tile[sl, :] + self.core_in[0, sl, :].astype(F32)).astype(BF)
                    self.over[r].start()

            @pl.when(k == 2)
            def _():
                self.core_out[1] = tile[...].astype(BF)
                self.core[1].start()

            @pl.when(k == 3)
            def _():
                self.core[1].wait_recv()
                if own is None:
                    tile[...] = tile[...] + self.core_in[1].astype(F32)
                else:
                    own[...] = own[...] + tile[...] + self.core_in[1].astype(F32)

            between(k)
            return 0

        lax.fori_loop(0, 4, one, 0)

    def arrived(self, r):
        self.over[r].wait_recv()
        return self.over_in[pl.ds(r * self.chunk, self.chunk), :].astype(F32)

    def finish(self):
        for copy in self.core + self.over:
            copy.wait_send()


class Columns:
    def __init__(self, at, sems, weights, buf):
        self.at = at
        rows, width = weights[0].shape
        part = width // 4
        half = rows // 2
        h = lax.rem(at.s, 2)
        self.half, self.rows, self.part, self.buf, self.sems = half, rows, part, buf, sems
        self.near, self.own, self.far, self.side = [], [], [], []
        for k, w in enumerate(weights):
            cols = pl.ds(k * part, part)
            take = lambda f: pl.ds(pl.multiple_of(f * part, 128), part)
            mine = pl.ds(pl.multiple_of(at.f * rows, rows), rows)
            cut = pl.ds(pl.multiple_of(h * half, half), half)
            mine_cut = pl.ds(pl.multiple_of(at.f * rows + h * half, half), half)
            self.own.append(pltpu.make_async_copy(w.at[:, take(at.f)], buf.at[mine, cols], sems.take()))
            self.near.append(sems.remote(w.at[:, take(at.p1)], buf.at[mine, cols], at.group(at.p1)))
            for p in (at.p2, at.p3):
                self.far.append(sems.remote(w.at[cut, take(p)], buf.at[mine_cut, cols], at.group(p)))
                came = buf.at[pl.ds(pl.multiple_of(p * rows + h * half, half), half), cols]
                self.side.append(sems.remote(came, came, at.line(at.sx)))

    def start_far(self):
        for c in self.far:
            c.start()

    def start_near(self):
        for c in self.near + self.own:
            c.start()

    def relay(self, k):
        self.far[k].wait_recv()
        self.side[k].start()

    def finish(self):
        for c in self.own + self.near + self.side:
            c.wait()
        for c in self.far:
            c.wait_send()


def expm1_neg(v):
    series = v * (1 + v * (1 / 2) * (1 + v * (1 / 3) * (1 + v * (1 / 4) * (1 + v * (1 / 5) * (1 + v * (1 / 6))))))
    return jnp.where(v > -0.25, series, jnp.exp(v) - 1.0)


def swap_rows(src, dst, outer, kind):
    total, width = src.shape
    inner = total // outer

    def one(c, _):
        cols = pl.ds(pl.multiple_of(c * 128, 128), 128)
        v = src[:, cols].reshape(outer, inner, 128)
        dst[:, cols] = jnp.swapaxes(v, 0, 1).reshape(total, 128).astype(kind)
        return 0

    lax.fori_loop(0, width // 128, one, 0)


def forward_branch(x, gains, chan, wr, wl, wo, wg, wi, wu, wv,
                   wgi_o, wuv_o, normed_o, n2_o, middle_o, gate_o, pad_o, conv_o, rate_o, inlet_o, decay_o, states_o,
                   merged_o, ends_o, gain_o,
                   wgi, normed, n2, middle, gain, gate, pad, conv, rate, inlet, decay, states, work, merged, ends,
                   tot, core_out, core_in, over_out, over_in, sem, tsend, trecv):
    at = Place()
    here, width = x.shape
    toks = here // 2
    chans = chan.shape[1]
    part = width // 4
    taps = 4
    steps = toks
    group = 8
    halo = (taps - 1) * group
    sems = Sems(sem)
    at.greet()

    shares = [
        sems.remote(gains, gain.at[at.f], at.group(p)) for p in (at.p1, at.p2, at.p3)
    ]
    for c in shares:
        c.start()
    gain[at.f] = gains[...]
    gi = Columns(at, sems, [wg, wi], wgi)
    gi.start_far()
    gi.start_near()
    uv = Columns(at, sems, [wu, wv], wuv_o)
    uv.start_near()
    ag1 = Gather(at, sems, normed, toks)
    for c in shares:
        c.wait()
    for r in range(2):
        sl = pl.ds(r * toks, toks)
        v = x[sl, :]
        scale = lax.rsqrt(jnp.mean(v * v, axis=-1, keepdims=True) + EPS_NORM)
        for p in range(4):
            cols = pl.ds(p * part, part)
            normed[rows_at(at.f * 2 + r, toks), cols] = (x[sl, cols] * scale * gain[p, 0:1, :]).astype(BF)
        ag1.send(r)
    for k in range(4):
        gi.relay(k)
    ag1.relay(0)
    uv.start_far()
    ag1.relay(1)
    ag1.finish()
    gi.finish()
    saves = [sems.local(normed, normed_o), sems.local(wgi, wgi_o), sems.local(gain, gain_o)]

    def branch_rows(m, _):
        sl = rows_at(m, here)
        work[sl, :] = mm(normed[sl, :], wgi[:, chans:]).astype(BF).astype(F32)
        return 0

    lax.fori_loop(0, 4, branch_rows, 0)
    swap_rows(work, pad.at[pl.ds(halo, steps * group)], group, F32)
    edge = pad.at[pl.ds(steps * group, halo)]
    next_one = lax.rem(at.s + 1, at.n)
    tail = sems.remote(edge, pad.at[pl.ds(0, halo)], at.line(next_one))

    @pl.when(at.s < at.n - 1)
    def _():
        tail.start()

    @pl.when(at.s == 0)
    def _():
        pad[0:halo, :] = jnp.zeros((halo, chans), F32)

    def gate_rows(m, _):
        sl = rows_at(m, here)
        work[sl, :] = mm(normed[sl, :], wgi[:, :chans])
        return 0

    lax.fori_loop(0, 4, gate_rows, 0)
    swap_rows(work, gate, group, F32)

    @pl.when(at.s > 0)
    def _():
        tail.wait_recv()

    @pl.when(at.s < at.n - 1)
    def _():
        tail.wait_send()

    uv.relay(0)

    def gates(b, _):
        for h in range(chans // 128):
            cols = pl.ds(h * 128, 128)
            size = 128
            start = pl.multiple_of(b * size, size)
            sl = pl.ds(start, size)
            total = chan[taps : taps + 1, cols]
            for k in range(taps):
                total = total + chan[k : k + 1, cols] * pad[pl.ds(start + (halo - group * k), size), cols]
            low = total.astype(BF)
            blocks = pl.ds(h * 128, 128)
            r = jax.nn.sigmoid(mm(low, wr[blocks, :]) + chan[5:6, cols])
            i = jax.nn.sigmoid(mm(low, wl[blocks, :]) + chan[6:7, cols])
            ld = r * chan[7:8, cols]
            conv[sl, cols] = low
            low = low.astype(F32)
            decay[sl, cols] = jnp.exp(ld)
            work[sl, cols] = jnp.sqrt(EPS_MULT - expm1_neg(2.0 * ld)) * i * low
            rate[sl, cols] = r
            inlet[sl, cols] = i
        return 0

    lax.fori_loop(0, steps * group // 128, gates, 0)
    saves += [
        sems.local(gate, gate_o), sems.local(pad, pad_o), sems.local(conv, conv_o), sems.local(rate, rate_o),
        sems.local(inlet, inlet_o), sems.local(decay, decay_o),
    ]

    unroll = 8

    def totals(b, carry):
        h, p = carry
        for u in range(unroll):
            sl = pl.ds(pl.multiple_of((b * unroll + u) * group, group), group)
            a = decay[sl, :]
            h = a * h + work[sl, :]
            p = p * a
        return h, p

    zero = jnp.zeros((group, chans), F32)
    h, p = lax.fori_loop(0, steps // unroll, totals, (zero, zero + 1.0))
    ends[0:8, :] = p
    ends[8:16, :] = h

    def total_copy(src, to):
        return pltpu.make_async_remote_copy(
            src_ref=ends.at[pl.ds(0, 16)], dst_ref=tot.at[src], send_sem=tsend.at[to], recv_sem=trecv.at[src],
            device_id=at.line(to), device_id_type=MESH,
        )

    def send_total(j, _):
        total_copy(at.s, j).start()
        return 0

    lax.fori_loop(at.s + 1, at.n, send_total, 0)
    uv.relay(1)

    def enter(j, state):
        total_copy(j, j).wait_recv()
        return tot[j, 0:8, :] * state + tot[j, 8:16, :]

    state_in = lax.fori_loop(0, at.s, enter, zero)

    def sent_total(j, _):
        total_copy(at.s, j).wait_send()
        return 0

    lax.fori_loop(at.s + 1, at.n, sent_total, 0)
    ends[16:24, :] = state_in

    def scan(b, h):
        for u in range(unroll):
            sl = pl.ds(pl.multiple_of((b * unroll + u) * group, group), group)
            h = decay[sl, :] * h + work[sl, :]
            states[sl, :] = h
        return h

    lax.fori_loop(0, steps // unroll, scan, state_in)
    saves += [sems.local(states, states_o), sems.local(ends, ends_o)]

    def merge(c, _):
        cols = pl.ds(pl.multiple_of(c * 128, 128), 128)

        def some(b, _):
            sl = rows_at(b, 128)
            work[sl, cols] = states[sl, cols] * gelu_pair(gate[sl, cols])[0]
            return 0

        lax.fori_loop(0, steps * group // 128, some, 0)
        return 0

    lax.fori_loop(0, chans // 128, merge, 0)
    swap_rows(work, merged, steps, BF)
    saves += [sems.local(merged, merged_o)]

    middle[...] = x[...]
    sc = Scatter(at, sems, core_out, core_in, over_out, over_in, toks)

    def partial(o, store):
        def half(r, _):
            sl = rows_at(r, toks)
            tile = mm(merged[rows_at(o * 2 + r, toks), :], wo[...])
            store(sl, slice(None), tile)
            return 0

        lax.fori_loop(0, 2, half, 0)

    sc.run(partial, middle)
    ag2 = Gather(at, sems, n2, toks)
    for r in range(2):
        sl = pl.ds(r * toks, toks)
        v = middle[sl, :] + sc.arrived(r)
        middle[sl, :] = v
        scale = lax.rsqrt(jnp.mean(v * v, axis=-1, keepdims=True) + EPS_NORM)
        for p in range(4):
            cols = pl.ds(p * part, part)
            n2[rows_at(at.f * 2 + r, toks), cols] = (middle[sl, cols] * scale * gain[p, 1:2, :]).astype(BF)
        ag2.send(r)
    saves += [sems.local(middle, middle_o)]
    uv.relay(2)
    uv.relay(3)
    for r in range(2):
        ag2.relay(r)
    ag2.finish()
    sc.finish()
    saves += [sems.local(n2, n2_o)]
    uv.finish()
    for c in saves:
        c.wait()


def call_forward(x, gains, chan, wr, wl, wo, wg, wi, wu, wv):
    here, width = x.shape
    chans = chan.shape[1]
    ffl = wu.shape[1] // 4
    every = here * 4
    n = lax.axis_size("seq")
    f32 = lambda *s: jax.ShapeDtypeStruct(s, F32)
    bf = lambda *s: jax.ShapeDtypeStruct(s, BF)
    vf = lambda *s: pltpu.VMEM(s, F32)
    vb = lambda *s: pltpu.VMEM(s, BF)
    outs = [
        bf(width, 2 * chans), bf(width, 2 * ffl), bf(every, width), bf(every, width), f32(here, width),
        f32(every, chans), f32(every + 24, chans), bf(every, chans), f32(every, chans), f32(every, chans),
        f32(every, chans), f32(every, chans), bf(every, chans), f32(24, chans), f32(4, 8, width // 4),
    ]
    scratch = [
        vb(width, 2 * chans), vb(every, width), vb(every, width), vf(here, width), vf(4, 8, width // 4),
        vf(every, chans), vf(every + 24, chans), vb(every, chans), vf(every, chans), vf(every, chans),
        vf(every, chans), vf(every, chans), vf(every, chans), vb(every, chans), vf(24, chans),
        vf(n, 16, chans), vb(2, here, width), vb(2, here, width), vb(here, width), vb(here, width),
        pltpu.SemaphoreType.DMA((120,)), pltpu.SemaphoreType.DMA((n,)), pltpu.SemaphoreType.DMA((n,)),
    ]
    return pl.pallas_call(
        forward_branch,
        out_shape=outs,
        in_specs=[VMEM] * 6 + [ANY] * 4,
        out_specs=[ANY] * len(outs),
        scratch_shapes=scratch,
        compiler_params=pltpu.CompilerParams(collective_id=1, has_side_effects=True, vmem_limit_bytes=LIMIT),
        name="forward_branch",
    )(x, gains, chan, wr, wl, wo, wg, wi, wu, wv)


class Hop:
    def __init__(self, at):
        b = at.f * at.n + at.s
        self.to = (lax.div(b, 4), lax.rem(b, 4))
        c = at.s * 4 + at.f
        self.source = (lax.rem(c, at.n), lax.div(c, at.n))
        self.stays = b == c

    def greet(self, barrier):
        @pl.when(jnp.logical_not(self.stays))
        def _():
            for device in (self.to, self.source):
                pl.semaphore_signal(barrier, inc=1, device_id=device, device_id_type=MESH)

        return jnp.where(self.stays, 0, 2)

    def start(self, sems, src, dst):
        far = sems.remote(src, dst, self.to)
        near = pltpu.make_async_copy(src, dst, sems.take())

        @pl.when(self.stays)
        def _():
            near.start()

        @pl.when(jnp.logical_not(self.stays))
        def _():
            far.start()

        return near, far

    def wait(self, pair):
        near, far = pair

        @pl.when(self.stays)
        def _():
            near.wait()

        @pl.when(jnp.logical_not(self.stays))
        def _():
            far.wait()


class Ring:
    def __init__(self, at, grads, slots, send, recv, by_rows):
        self.at, self.grads, self.slots, self.sem, self.rem = at, grads, slots, send, recv
        n = at.n
        self.q = self.place(at.s)
        rows, width = slots.shape[1:]
        self.rows = rows
        if by_rows:
            self.cut = [(pl.ds(i * rows // 4, rows // 4), pl.ds(0, width)) for i in range(4)]
        else:
            self.cut = [(pl.ds(0, rows), pl.ds(i * width // 4, width // 4)) for i in range(4)]
        self.way = (1, -1, 1, -1)
        self.to = {w: at.line(self.owner(lax.rem(self.q + w + n, n))) for w in (1, -1)}

    def place(self, s):
        half = lax.div(s, 2)
        return jnp.where(lax.rem(s, 2) == 0, half, self.at.n - 1 - half)

    def owner(self, q):
        n = self.at.n
        return jnp.where(q < n // 2, 2 * q, 2 * (n - 1 - q) + 1)

    def block(self, i, behind):
        n = self.at.n
        s = self.owner(lax.rem(self.q - self.way[i] * behind + 2 * n, n))
        r, c = self.cut[i]
        return self.grads.at[pl.ds(pl.multiple_of(s * self.rows + r.start, 16), r.size), c]

    def copy(self, i, k, src):
        r, c = self.cut[i]
        return pltpu.make_async_remote_copy(
            src_ref=src, dst_ref=self.slots.at[k, r, c], send_sem=self.sem.at[i, k], recv_sem=self.rem.at[i, k],
            device_id=self.to[self.way[i]], device_id_type=MESH,
        )

    def start(self):
        for i in range(4):
            self.copy(i, 0, self.block(i, 1)).start()

    def summed(self, i, k):
        r, c = self.cut[i]
        slot = self.slots.at[k, r, c]
        self.copy(i, k, slot).wait_recv()
        return slot, slot[...].astype(F32) + self.block(i, k + 2)[...].astype(F32)

    def step(self, k):
        for i in range(4):
            slot, value = self.summed(i, k)
            slot[...] = value.astype(BF)
            self.copy(i, k + 1, slot).start()

    def last(self, out, after=lambda i: None):
        k = self.at.n - 2
        for i in range(4):
            _, value = self.summed(i, k)
            out[self.cut[i]] = value
            after(i)

    def finish(self):
        def one(k, _):
            for i in range(4):
                r, c = self.cut[i]
                self.copy(i, k, self.slots.at[k, r, c]).wait_send()
            return 0

        lax.fori_loop(0, self.at.n - 1, one, 0)


class Spread:
    def __init__(self, at, sems, src, out, col=0, width=None):
        self.at = at
        rows = src.shape[0] // 4
        width = width or src.shape[1]
        self.copies = []
        cols = pl.ds(pl.multiple_of(at.f * width, 128), width)
        for p in (at.p1, at.p2, at.p3):
            piece = src.at[pl.ds(pl.multiple_of(p * rows, 8), rows), pl.ds(col, width)]
            self.copies.append(sems.remote(piece, out.at[:, cols], at.group(p)))
        piece = src.at[pl.ds(pl.multiple_of(at.f * rows, 8), rows), pl.ds(col, width)]
        self.copies.append(pltpu.make_async_copy(piece, out.at[:, cols], sems.take()))

    def start(self):
        for c in self.copies:
            c.start()

    def wait(self):
        for c in self.copies:
            c.wait()


def mlp(n2_h, wuv_h, wd_h, middle_h, teacher_h, scale, gain,
        result_o, gmid_o, gml_o, gain_o, down_o, up_o, value_o,
        n2, wuv, wd, hidden, ge, gdi, gml, middle, own, gout, tile, core_out, core_in, over_out, over_in,
        gwd, gwu, gwv, slots_d, slots_u, last_d, last_u, gain_acc, sem, ring_sem):
    at = Place()
    sems = Sems(sem)
    here, width = middle.shape
    toks = here // 2
    ffl = hidden.shape[1]
    part = width // 4
    col = 384
    loads = [sems.local(n2_h, n2), sems.local(wuv_h, wuv), sems.local(wd_h, wd)]
    loads2 = [sems.local(middle_h, middle), sems.local(middle_h, own), sems.local(teacher_h, gout)]
    hop = Hop(at)
    at.greet(hop)
    for c in loads + loads2:
        c.wait()

    def forward(o):
        sl = rows_at(o, here)

        def some(c, _):
            cols = pl.ds(pl.multiple_of(c * col, 128), col)
            cols2 = pl.ds(pl.multiple_of(c * col + ffl, 128), col)
            up = mm(n2[sl, :], wuv[:, cols])
            g, d = gelu_pair(mm(n2[sl, :], wuv[:, cols2]))
            hidden[sl, cols] = (g * up).astype(BF)
            ge[sl, cols] = g.astype(BF)
            ge[sl, cols2] = (up * d).astype(BF)
            return 0

        lax.fori_loop(0, ffl // col, some, 0)

        def out(c, _):
            cols = pl.ds(pl.multiple_of(c * 512, 128), 512)
            tile[:, cols] = mm(hidden[sl, :], wd[:, cols])
            return 0

        lax.fori_loop(0, width // 512, out, 0)

    sc = Scatter(at, sems, core_out, core_in, over_out, over_in, toks)
    sc.run_tile(forward, tile, own)
    ag = Gather(at, sems, gdi, toks)
    for r in range(2):
        sl = pl.ds(r * toks, toks)
        v = own[sl, :] + sc.arrived(r)
        own[sl, :] = v
        v = (v - gout[sl, :]) * scale[sl, 0:1]
        v = jnp.where(scale[sl, 0:1] > 0.0, v, 0.0)
        gout[sl, :] = v
        gdi[rows_at(at.f * 2 + r, toks), :] = v.astype(BF)
        ag.send(r)
    saves = [sems.local(own, result_o)]
    for r in range(2):
        ag.relay(r)
    ag.finish()
    sc.finish()
    saves[0].wait()

    def down_rows(m, _):
        cols = pl.ds(pl.multiple_of(m * 128, 128), 128)
        gwd[rows_at(m, 128), :] = mm_lt(hidden[:, cols], gdi[...]).astype(BF)
        return 0

    lax.fori_loop(0, ffl // 128, down_rows, 0)
    ring_d = Ring(at, gwd, slots_d, ring_sem.at[0], ring_sem.at[1], False)
    ring_u = Ring(at, gwu, slots_u, ring_sem.at[2], ring_sem.at[3], True)
    ring_d.start()

    def backward(o):
        sl = rows_at(o, here)

        def some(c, _):
            cols = pl.ds(pl.multiple_of(c * col, 128), col)
            cols2 = pl.ds(pl.multiple_of(c * col + ffl, 128), col)
            gh = mm_rt(gdi[sl, :], wd[cols, :])
            ge[sl, cols] = (gh * ge[sl, cols].astype(F32)).astype(BF)
            ge[sl, cols2] = (gh * ge[sl, cols2].astype(F32)).astype(BF)
            return 0

        lax.fori_loop(0, ffl // col, some, 0)

        def out(c, _):
            cols = pl.ds(pl.multiple_of(c * 512, 128), 512)
            tile[:, cols] = mm_rt(ge[sl, :], wuv[cols, :])
            return 0

        lax.fori_loop(0, width // 512, out, 0)

    sc2 = Scatter(at, sems, core_out, core_in, over_out, over_in, toks)
    sc2.run_tile(backward, tile, None, ring_d.step)

    def weight_rows(grads, first):
        def one(m, _):
            cols = pl.ds(pl.multiple_of(m * 256, 256), 256)
            grads[rows_at(m, 256), :] = mm_lt(n2[:, cols], ge[:, first : first + ffl]).astype(BF)
            return 0

        return one

    up_rows, value_rows = weight_rows(gwu, 0), weight_rows(gwv, ffl)
    six = width // 256
    lax.fori_loop(0, six, up_rows, 0)
    ring_d.step(4)
    lax.fori_loop(0, six // 2, value_rows, 0)
    ring_d.step(5)
    ring_u.start()
    lax.fori_loop(six // 2, six, value_rows, 0)
    saves = [sems.local(gwv, value_o)]
    ring_d.last(last_d)
    hopping = hop.start(sems, last_d, down_o)
    ring_u.step(0)
    ag2 = Gather(at, sems, gml, toks)
    acc = jnp.zeros((1, width), F32)
    for r in range(2):
        sl = pl.ds(r * toks, toks)
        g = tile[sl, :] + sc2.arrived(r)
        v = middle[sl, :]
        s = lax.rsqrt(jnp.mean(v * v, axis=-1, keepdims=True) + EPS_NORM)
        acc = acc + jnp.sum(g * v * s, axis=0, keepdims=True)
        gg = g * gain[...]
        mean = jnp.mean(gg * v, axis=-1, keepdims=True)
        new = gout[sl, :] + s * gg - v * (s * s * s * mean)
        own[sl, :] = new
        gml[rows_at(at.f * 2 + r, toks), :] = new.astype(BF)
        ag2.send(r)
        ring_u.step(1 + r)
    gain_acc[...] = jnp.broadcast_to(acc, gain_acc.shape)
    saves += [sems.local(own, gmid_o), sems.local(gain_acc, gain_o)]
    ag2.relay(0)
    ring_u.step(3)
    ag2.relay(1)
    ring_u.step(4)
    ag2.finish()
    sc2.finish()
    saves += [sems.local(gml, gml_o)]
    ring_u.step(5)
    spread = Spread(at, sems, last_u, up_o)
    ring_u.last(last_u)
    spread.start()
    hop.wait(hopping)
    ring_d.finish()
    ring_u.finish()
    spread.wait()
    for c in saves:
        c.wait()


def call_mlp(n2, wuv, wd, middle, teacher, scale, gain):
    every, width = n2.shape
    here = middle.shape[0]
    ffl = wd.shape[0]
    n = lax.axis_size("seq")
    f32 = lambda *s: jax.ShapeDtypeStruct(s, F32)
    bf = lambda *s: jax.ShapeDtypeStruct(s, BF)
    vf = lambda *s: pltpu.VMEM(s, F32)
    vb = lambda *s: pltpu.VMEM(s, BF)
    outs = [
        f32(here, width), f32(here, width), bf(every, width), f32(8, width), f32(ffl // n, width),
        f32(width // n // 4, 4 * ffl), bf(width, ffl),
    ]
    scratch = [
        vb(every, width), vb(width, 2 * ffl), vb(ffl, width), vb(every, ffl), vb(every, 2 * ffl), vb(every, width),
        vb(every, width), vf(here, width), vf(here, width), vf(here, width), vf(here, width),
        vb(2, here, width), vb(2, here, width), vb(here, width), vb(here, width),
        vb(ffl, width), vb(width, ffl), vb(width, ffl), vb(n - 1, ffl // n, width), vb(n - 1, width // n, ffl),
        vf(ffl // n, width), vf(width // n, ffl), vf(8, width),
        pltpu.SemaphoreType.DMA((100,)), pltpu.SemaphoreType.DMA((4, 4, n - 1)),
    ]
    return pl.pallas_call(
        mlp,
        out_shape=outs,
        in_specs=[ANY] * 5 + [VMEM] * 2,
        out_specs=[ANY] * len(outs),
        scratch_shapes=scratch,
        compiler_params=pltpu.CompilerParams(collective_id=2, has_side_effects=True, vmem_limit_bytes=LIMIT),
        name="mlp",
    )(n2, wuv, wd, middle, teacher, scale, gain)


class Line:
    def __init__(self, at, src, tot, send, recv):
        self.at, self.src, self.tot, self.send_sem, self.recv_sem = at, src, tot, send, recv

    def copy(self, slot, to):
        return pltpu.make_async_remote_copy(
            src_ref=self.src, dst_ref=self.tot.at[slot], send_sem=self.send_sem.at[to], recv_sem=self.recv_sem.at[slot],
            device_id=self.at.line(to), device_id_type=MESH,
        )

    def send(self, first, end):
        def one(j, _):
            @pl.when(j != self.at.s)
            def _():
                self.copy(self.at.s, j).start()

            return 0

        lax.fori_loop(first, end, one, 0)

    def sent(self, first, end):
        def one(j, _):
            @pl.when(j != self.at.s)
            def _():
                self.copy(self.at.s, j).wait_send()

            return 0

        lax.fori_loop(first, end, one, 0)

    def wait(self, j):
        self.copy(j, j).wait_recv()


def branch_back(chan, wr, wl, gain, gain2,
                gml_h, merged_h, wo_h, wgi_h, normed_h, gate_h, pad_h, conv_h, rate_h, inlet_h, decay_h, states_h, ends_h,
                gwv_h, x_h, gmid_h,
                ginput_o, value_o, gate_o, input_o, out_o, rate_o, inlet_o, chan_o, gains_o,
                gml, merged, wo, wgi, normed, gate, pad, conv, rate, inlet, decay, states, ends, gwv, own,
                work, gconv, pair, heads_r, heads_l, acc, tile, core_out, core_in, over_out, over_in,
                go, ggi, slots_v, slots_o, slots_g, last_v, last_o, last_g,
                passed, tot, small, small_in, small_sum, group_in, gains,
                sem, ring_sem, line_sem):
    at = Place()
    sems = Sems(sem)
    here, width = own.shape
    toks = here // 2
    chans = chan.shape[1]
    group, taps = 8, 4
    steps = toks
    every = steps * group
    halo = (taps - 1) * group
    n = at.n
    early = [sems.local(gwv_h, gwv), sems.local(gml_h, gml), sems.local(wo_h, wo)]
    second = [sems.local(gate_h, gate), sems.local(states_h, states.at[pl.ds(group, every)]), sems.local(ends_h, ends)]
    third = [sems.local(decay_h, decay), sems.local(merged_h, merged), sems.local(normed_h, normed)]
    fourth = [
        sems.local(a, b)
        for a, b in ((pad_h, pad), (conv_h, conv), (rate_h, rate), (inlet_h, inlet), (wgi_h, wgi), (gmid_h, own))
    ]
    hop = Hop(at)
    at.greet(hop)
    ring_v = Ring(at, gwv, slots_v, ring_sem.at[0], ring_sem.at[1], True)
    ring_o = Ring(at, go, slots_o, ring_sem.at[2], ring_sem.at[3], True)
    ring_g = Ring(at, ggi, slots_g, ring_sem.at[4], ring_sem.at[5], True)
    for c in early:
        c.wait()
    ring_v.start()

    def merged_rows(m, _):
        sl = rows_at(m, here)
        work[sl, :] = mm_rt(gml[sl, :], wo[...])
        return 0

    lax.fori_loop(0, 4, merged_rows, 0)
    for c in second:
        c.wait()
    states[0:group, :] = ends[16:24, :]
    ring_v.step(0)

    def split(c, _):
        cols = pl.ds(pl.multiple_of(c * 128, 128), 128)
        g = jnp.swapaxes(work[:, cols].reshape(group, steps, 128), 0, 1).reshape(every, 128)
        act, slope = gelu_pair(gate[:, cols])
        gate[:, cols] = g * act
        down = g * states[pl.ds(group, every), cols] * slope
        pair[:, cols] = jnp.swapaxes(down.reshape(steps, group, 128), 0, 1).reshape(every, 128).astype(BF)
        return 0

    lax.fori_loop(0, chans // 128, split, 0)
    for c in third:
        c.wait()
    unroll = 8
    blocks = steps // unroll

    def totals(b, carry):
        for u in range(unroll):
            sl = pl.ds(pl.multiple_of((steps - 1 - (b * unroll + u)) * group, group), group)
            carry = decay[sl, :] * (gate[sl, :] + carry)
        return carry

    zero = jnp.zeros((group, chans), F32)
    passed[0:8, :] = ends[0:8, :]
    passed[8:16, :] = lax.fori_loop(0, blocks, totals, zero)
    line = Line(at, passed, tot, line_sem.at[0], line_sem.at[1])
    line.send(0, at.s)
    ring_v.step(1)

    def out_rows(m, _):
        cols = pl.ds(pl.multiple_of(m * 256, 256), 256)
        go[rows_at(m, 256), 0:width] = mm_lt(merged[:, cols], gml[...]).astype(BF)
        return 0

    lax.fori_loop(0, chans // 256, out_rows, 0)
    ring_v.step(2)

    def normed_rows(first):
        def one(m, _):
            cols = pl.ds(pl.multiple_of(m * 256, 256), 256)
            ggi[rows_at(m, 256), first : first + chans] = mm_lt(normed[:, cols], pair[:, first : first + chans]).astype(BF)
            return 0

        return one

    lax.fori_loop(0, width // 256, normed_rows(0), 0)
    ring_v.step(3)

    def enter(k, state):
        j = n - 1 - k
        line.wait(j)
        return tot[j, 0:8, :] * state + tot[j, 8:16, :]

    carry_in = lax.fori_loop(0, n - 1 - at.s, enter, zero)
    line.sent(0, at.s)

    def scan(b, carry):
        for u in range(unroll):
            sl = pl.ds(pl.multiple_of((steps - 1 - (b * unroll + u)) * group, group), group)
            adjoint = gate[sl, :] + carry
            gate[sl, :] = adjoint
            carry = decay[sl, :] * adjoint
        return carry

    lax.fori_loop(0, blocks, scan, carry_in)
    ring_v.step(4)
    for c in fourth:
        c.wait()
    heads_r[...] = jnp.zeros_like(heads_r)
    heads_l[...] = jnp.zeros_like(heads_l)
    acc[...] = jnp.zeros_like(acc)
    edge = sems.remote(
        gconv.at[pl.ds(0, halo)], gconv.at[pl.ds(every, halo)], at.line(lax.rem(at.s + n - 1, n))
    )

    def gates(b, _):
        size = 128
        start = pl.multiple_of(b * size, size)
        sl = pl.ds(start, size)
        for h in range(chans // 128):
            cols = pl.ds(h * 128, 128)
            sp8 = chan[7:8, cols]
            r, i, dec, adj = rate[sl, cols], inlet[sl, cols], decay[sl, cols], gate[sl, cols]
            low_bf = conv[sl, cols]
            low = low_bf.astype(F32)
            factor = jnp.sqrt(EPS_MULT - expm1_neg(2.0 * (r * sp8)))
            ai = adj * i
            af = adj * factor
            gld = adj * states[sl, cols] * dec - ai * low * (dec * dec) / factor
            gldr = gld * r
            grate = gldr * sp8 * (1.0 - r)
            ginl = af * low * i * (1.0 - i)
            grl, gil = grate.astype(BF), ginl.astype(BF)
            hb = pl.ds(h * 128, 128)
            gc = af * i + mm_rt(grl, wr[hb, :]) + mm_rt(gil, wl[hb, :])
            heads_r[hb, :] += mm_lt(low_bf, grl)
            heads_l[hb, :] += mm_lt(low_bf, gil)
            gconv[sl, cols] = gc
            fold = lambda v: jnp.sum(v.reshape(size // 8, 8, 128), axis=0)
            for k in range(taps):
                acc[k, :, cols] += fold(gc * pad[pl.ds(start + (halo - group * k), size), cols])
            acc[4, :, cols] += fold(gc)
            acc[5, :, cols] += fold(grate)
            acc[6, :, cols] += fold(ginl)
            acc[7, :, cols] += fold(gldr)

        @pl.when(jnp.logical_and(b == 0, at.s > 0))
        def _():
            edge.start()

        return 0

    lax.fori_loop(0, every // 128, gates, 0)

    @pl.when(at.s == n - 1)
    def _():
        gconv[pl.ds(every, halo), :] = jnp.zeros((halo, chans), F32)

    thirds = width // chans
    inputs = [
        sems.local(x_h.at[:, pl.ds(k * chans, chans)], pad.at[pl.ds(k * here, here)]) for k in range(thirds)
    ]
    go[:, width : width + 128] = heads_r[...].astype(BF)
    go[:, width + 128 :] = heads_l[...].astype(BF)
    ring_o.start()
    ring_v.step(5)
    for k in range(8):
        small[k : k + 1, :] = jnp.sum(acc[k], axis=0, keepdims=True)
    small[7:8, :] = small[7:8, :] * chan[8:9, :]

    @pl.when(at.s < n - 1)
    def _():
        edge.wait_recv()

    @pl.when(at.s > 0)
    def _():
        edge.wait_send()

    def taps_back(b, _):
        start = pl.multiple_of(b * 128, 128)
        for h in range(chans // 128):
            cols = pl.ds(h * 128, 128)
            total = chan[0:1, cols] * gconv[pl.ds(start, 128), cols]
            for k in range(1, taps):
                total = total + chan[k : k + 1, cols] * gconv[pl.ds(start + group * k, 128), cols]
            work[pl.ds(start, 128), cols] = total
        return 0

    lax.fori_loop(0, every // 128, taps_back, 0)
    swap_rows(work, pair.at[:, pl.ds(chans, chans)], steps, BF)
    spread_v = Spread(at, sems, last_v, value_o)
    ring_v.last(last_v)
    spread_v.start()
    lax.fori_loop(0, width // 256, normed_rows(chans), 0)
    ring_g.start()
    ring_o.step(0)

    def back(o):
        sl = rows_at(o, here)

        def some(c, _):
            cols = pl.ds(pl.multiple_of(c * 512, 128), 512)
            tile[:, cols] = mm_rt(pair[sl, :], wgi[cols, :])
            return 0

        lax.fori_loop(0, width // 512, some, 0)

    sc = Scatter(at, sems, core_out, core_in, over_out, over_in, toks)
    sc.run_tile(back, tile, None, lambda k: ring_o.step(k + 1))
    ring_g.step(0)
    ring_o.step(5)
    ring_g.step(1)
    ring_o.last(last_o)
    hops = [
        hop.start(sems, last_o.at[:, pl.ds(0, width)], out_o),
        hop.start(sems, last_o.at[:, pl.ds(width, 128)], rate_o),
        hop.start(sems, last_o.at[:, pl.ds(width + 128, 128)], inlet_o),
    ]
    gain1 = jnp.zeros((1, width), F32)
    for c in inputs:
        c.wait()
    for r in range(2):
        sl = pl.ds(r * toks, toks)
        g = tile[sl, :] + sc.arrived(r)
        v = jnp.concatenate([pad[pl.ds(k * here + r * toks, toks), :] for k in range(thirds)], axis=1)
        s = lax.rsqrt(jnp.mean(v * v, axis=-1, keepdims=True) + EPS_NORM)
        gain1 = gain1 + jnp.sum(g * v * s, axis=0, keepdims=True)
        gg = g * gain[...]
        mean = jnp.mean(gg * v, axis=-1, keepdims=True)
        own[sl, :] = own[sl, :] + s * gg - v * (s * s * s * mean)
        ring_g.step(2 + r)
    saves = [sems.local(own, ginput_o)]
    for k in range(3):
        small[8 + k : 9 + k, :] = gain1[:, k * chans : (k + 1) * chans]
        small[11 + k : 12 + k, :] = gain2[0:1, k * chans : (k + 1) * chans]
    small[14:16, :] = jnp.zeros((2, chans), F32)
    share = Line(at, small, small_in, line_sem.at[2], line_sem.at[3])
    share.send(0, n)
    ring_g.step(4)
    small_in[at.s] = small[...]

    def arrive(j, total):
        @pl.when(j != at.s)
        def _():
            share.wait(j)

        return total + small_in[j]

    small_sum[...] = lax.fori_loop(0, n, arrive, jnp.zeros(small.shape, F32))
    hops.append(hop.start(sems, small_sum.at[pl.ds(0, 8)], chan_o))
    lower = small_sum.at[pl.ds(8, 8)]
    around = [sems.remote(lower, group_in.at[at.f], at.group(p)) for p in (at.p1, at.p2, at.p3)]
    for c in around:
        c.start()
    group_in[at.f] = small_sum[8:16, :]
    ring_g.step(5)
    spreads = [Spread(at, sems, last_g, gate_o, 0, chans), Spread(at, sems, last_g, input_o, chans, chans)]
    ring_g.last(last_g)
    for c in spreads:
        c.start()
    for c in around:
        c.wait()
    gains[...] = group_in[0] + group_in[1] + group_in[2] + group_in[3]
    saves += [sems.local(gains, gains_o)]
    share.sent(0, n)
    sc.finish()
    for h in hops:
        hop.wait(h)
    for r in (ring_v, ring_o, ring_g):
        r.finish()
    for c in [spread_v] + spreads + saves:
        c.wait()


def call_back(chan, wr, wl, gain, gain2, gml, merged, wo, wgi, normed, gate, pad, conv, rate, inlet, decay, states, ends, gwv, x, gmid):
    every, width = gml.shape
    here = x.shape[0]
    chans = chan.shape[1]
    ffl = gwv.shape[1]
    n = lax.axis_size("seq")
    f32 = lambda *s: jax.ShapeDtypeStruct(s, F32)
    vf = lambda *s: pltpu.VMEM(s, F32)
    vb = lambda *s: pltpu.VMEM(s, BF)
    rows, crow = width // n, chans // n
    outs = [
        f32(here, width), f32(rows // 4, 4 * ffl), f32(rows // 4, 4 * chans), f32(rows // 4, 4 * chans), f32(crow, width),
        f32(crow, 128), f32(crow, 128), f32(8, chans), f32(8, chans),
    ]
    scratch = [
        vb(every, width), vb(every, chans), vb(chans, width), vb(width, 2 * chans), vb(every, width),
        vf(every, chans), vf(every + 24, chans), vb(every, chans), vf(every, chans), vf(every, chans), vf(every, chans),
        vf(every + 8, chans), vf(24, chans), vb(width, ffl), vf(here, width),
        vf(every, chans), vf(every + 24, chans), vb(every, 2 * chans), vf(chans, 128), vf(chans, 128), vf(8, 8, chans),
        vf(here, width), vb(2, here, width), vb(2, here, width), vb(here, width), vb(here, width),
        vb(chans, width + 256), vb(width, 2 * chans), vb(n - 1, rows, ffl), vb(n - 1, crow, width + 256), vb(n - 1, rows, 2 * chans),
        vf(rows, ffl), vf(crow, width + 256), vf(rows, 2 * chans),
        vf(16, chans), vf(n, 16, chans), vf(16, chans), vf(n, 16, chans), vf(16, chans), vf(4, 8, chans), vf(8, chans),
        pltpu.SemaphoreType.DMA((90,)), pltpu.SemaphoreType.DMA((6, 4, n - 1)), pltpu.SemaphoreType.DMA((4, n)),
    ]
    return pl.pallas_call(
        branch_back,
        out_shape=outs,
        in_specs=[VMEM] * 5 + [ANY] * 16,
        out_specs=[ANY] * len(outs),
        scratch_shapes=scratch,
        compiler_params=pltpu.CompilerParams(collective_id=3, has_side_effects=True, vmem_limit_bytes=LIMIT),
        name="branch_back",
    )(chan, wr, wl, gain, gain2, gml, merged, wo, wgi, normed, gate, pad, conv, rate, inlet, decay, states, ends, gwv, x, gmid)


def body(
    block_input, teacher, valid_lengths, norm_gain, w_gate, w_input, conv_weight, conv_bias,
    w_rate, bias_rate, w_inlet, bias_inlet, decay_param, w_out, mlp_gain, w_up, w_value, w_down,
):
    n_seq, n_fs = lax.axis_size("seq"), lax.axis_size(GROUP)
    si, fi = lax.axis_index("seq"), lax.axis_index(GROUP)
    rows_dev, toks, width = block_input.shape
    rows = rows_dev * n_fs
    here = rows_dev * toks
    chans = conv_bias.shape[0]
    hb = w_rate.shape[1]
    heads = chans // hb
    taps = conv_weight.shape[0]

    cw = conv_weight.astype(F32)
    sp = jax.nn.softplus(-decay_param.astype(F32))
    x = block_input.reshape(here, width)
    gains = jnp.concatenate([norm_gain[None].astype(F32), mlp_gain[None].astype(F32), jnp.zeros((6, width // 4), F32)])
    vec = lambda v: v.astype(F32)[None]
    chan = jnp.concatenate([cw, vec(conv_bias), vec(bias_rate), vec(bias_inlet), vec(-RATE_SCALE * sp), vec(RATE_SCALE * jax.nn.sigmoid(-decay_param.astype(F32))), jnp.zeros((7, chans), F32)])
    (wgi, wuv, normed, n2, middle, gate_tm, pad_tm, conv_tm, rate_tm, inlet_tm, decay_tm, states_tm, merged, ends, gain) = call_forward(
        x, gains, chan, w_rate, w_inlet, w_out, w_gate, w_input, w_up, w_value)
    lens = lax.dynamic_slice_in_dim(valid_lengths, fi * rows_dev, rows_dev)
    pos = si * toks + jnp.arange(toks, dtype=jnp.int32)
    mask = (pos[None, :] < lens[:, None]).reshape(here, 1)
    slots = valid_lengths.shape[0] * toks * n_seq
    count = jnp.sum(valid_lengths).astype(F32)
    if all((v // n_seq) % 64 == 0 for v in (width, chans)):
        scale = jnp.broadcast_to(jnp.where(mask, slots / count, 0.0), (here, 128))
        result, grad_middle, gml, gain2, down_sum, up_sum, g_value = call_mlp(
            n2, wuv, w_down, middle, teacher.reshape(here, width), scale, gain[:, 1].reshape(1, -1))
        grad_input, value_sum, gate_sum, input_sum, out_sum, rate_sum, inlet_sum, ch, gn = call_back(
            chan, w_rate, w_inlet, gain[:, 0].reshape(1, -1), gain2, gml, merged, w_out, wgi, normed, gate_tm, pad_tm,
            conv_tm, rate_tm, inlet_tm, decay_tm, states_tm, ends, g_value, x, grad_middle)
        place = si * n_fs + fi
        per = chans // n_seq
        ch = lax.dynamic_slice_in_dim(ch, lax.rem(place, n_seq) * per, per, 1)
        per = width // (n_seq * n_fs)
        gn = lax.dynamic_slice_in_dim(gn[:6].reshape(2, width), place * per, per, 1)
        return (
            result.reshape(block_input.shape), grad_input.reshape(block_input.shape), gn[0], gate_sum, input_sum,
            ch[:4], ch[4], rate_sum, ch[5], inlet_sum, ch[6], ch[7], out_sum, gn[1], up_sum, value_sum, down_sum,
        )

    heads_shape = (heads, hb, hb)
    wr, wl = w_rate.reshape(heads_shape), w_inlet.reshape(heads_shape)
    wg, wi = wgi[:, :chans], wgi[:, chans:]
    wu, wv = wuv[:, :wuv.shape[1]//2], wuv[:, wuv.shape[1]//2:]
    gain_one, gain_two = gain[:, 0].reshape(-1), gain[:, 1].reshape(-1)
    s1 = lax.rsqrt(jnp.mean(x * x, axis=-1, keepdims=True) + EPS_NORM)
    s2 = lax.rsqrt(jnp.mean(middle * middle, axis=-1, keepdims=True) + EPS_NORM)
    tok = lambda v: v.reshape(-1, rows, chans).swapaxes(0, 1)
    padded, clf, r, i, decay, states = tok(pad_tm), tok(conv_tm), tok(rate_tm), tok(inlet_tm), tok(decay_tm), tok(states_tm)
    conv_low, clf = clf, clf.astype(F32)
    heads_in = conv_low.reshape(rows * toks, heads, hb)
    gate_pre = tok(gate_tm).reshape(-1, chans)
    gg, gd = gelu_pair(gate_pre)
    cum_end, state_in = ends[:8], ends[16:24]
    prev = jnp.concatenate([state_in[:, None], states[:, :-1]], axis=1)
    ld = -RATE_SCALE * r * sp
    factor = jnp.sqrt(EPS_MULT - jnp.expm1(2.0 * ld))
    up = mm(n2, wu)
    value = mm(n2, wv)
    vg, vd = gelu_pair(value)
    hidden = (vg * up).astype(BF)
    result = middle + rs(mm(hidden, w_down))
    grad_out = jnp.where(mask, result - teacher.reshape(here, width), 0.0) * (slots / count)
    gdi = ag(grad_out.astype(BF))
    g_down = mm_lt(hidden, gdi)
    gh = mm_rt(gdi, w_down)
    gu = (gh * vg).astype(BF)
    gv = (gh * up * vd).astype(BF)
    g_up = mm_lt(n2, gu)
    g_value = mm_lt(n2, gv)
    gn2 = rs(mm_rt(gu, wu) + mm_rt(gv, wv))
    gm_norm, gain2 = rms_back(middle, s2, gain_two, gn2)
    grad_middle = grad_out + gm_norm
    gml = ag(grad_middle.astype(BF))
    g_out = mm_lt(merged, gml)
    gmer = mm_rt(gml, w_out)
    gst = (gmer * gg).reshape(rows, toks, chans)
    ggate = (gmer * states.reshape(-1, chans) * gd).astype(BF)
    nextd = jnp.concatenate([decay[:, 1:], jnp.ones((rows, 1, chans), F32)], axis=1)
    carry, ladj = lax.associative_scan(linear_step, (nextd, gst), axis=1, reverse=True)
    tot2 = lax.all_gather(jnp.stack([cum_end, decay[:, 0] * ladj[:, 0]]), "seq")
    adj_in = jnp.zeros((rows, chans), F32)
    for j in reversed(range(n_seq)):
        adj_in = jnp.where(j > si, tot2[j, 0] * adj_in + tot2[j, 1], adj_in)
    adj = ladj + carry * adj_in[:, None]
    gdec = adj * prev
    gfac = adj * i * clf
    gld = gdec * decay - gfac * (decay * decay) / factor
    grate = gld * (-RATE_SCALE * sp) * r * (1.0 - r)
    ginl = adj * factor * clf * i * (1.0 - i)
    gdp = jnp.sum(gld * r, axis=(0, 1)) * RATE_SCALE * jax.nn.sigmoid(-decay_param.astype(F32))
    gcd = adj * factor * i
    grb, gib = jnp.sum(grate, (0, 1)), jnp.sum(ginl, (0, 1))
    grl, gil = grate.astype(BF).reshape(-1, heads, hb), ginl.astype(BF).reshape(-1, heads, hb)
    gwr = jnp.einsum("nhi,nhj->hij", heads_in, grl, preferred_element_type=F32).reshape(chans, hb)
    gwi = jnp.einsum("nhi,nhj->hij", heads_in, gil, preferred_element_type=F32).reshape(chans, hb)
    bk = lambda a, w: jnp.einsum("nhj,hij->nhi", a, w, preferred_element_type=F32).reshape(rows, toks, chans)
    gconv = gcd + bk(grl, wr) + bk(gil, wl)
    gcw = jnp.stack([jnp.sum(gconv * padded[:, taps - 1 - k: taps - 1 - k + toks], (0, 1)) for k in range(taps)])
    gcb = jnp.sum(gconv, (0, 1))
    gpad = jnp.zeros((rows, toks + taps - 1, chans), F32)
    for k in range(taps):
        gpad = gpad.at[:, taps - 1 - k: taps - 1 - k + toks].add(cw[k] * gconv)
    edge = shifted(gpad[:, : taps - 1], "seq", -1)
    gbr = gpad[:, taps - 1:].at[:, toks - (taps - 1):].add(edge).reshape(-1, chans).astype(BF)
    g_gate = mm_lt(normed, ggate)
    g_input = mm_lt(normed, gbr)
    gn1 = rs(mm_rt(ggate, wg) + mm_rt(gbr, wi))
    gi_norm, gain1 = rms_back(x, s1, gain_one, gn1)
    grad_input = grad_middle + gi_norm

    chan = jnp.concatenate([gcw, gcb[None], grb[None], gib[None], gdp[None]], 0)
    per = chans // n_seq
    chan = chan.reshape(8, n_seq, per).transpose(1, 0, 2).reshape(n_seq, 8 * per)
    blk = jnp.zeros((n_fs, n_seq, 8 * per), F32).at[fi].set(chan).reshape(n_fs * n_seq, 8 * per)
    gw = jnp.stack([gain1, gain2]).reshape(2, n_fs * n_seq, -1).transpose(1, 0, 2).reshape(n_fs * n_seq, -1)
    small = lax.psum_scatter(jnp.concatenate([blk, gw], 1), BOTH, scatter_dimension=0, tiled=True)[0]
    ch = small[: 8 * per].reshape(8, per)
    gn = small[8 * per:].reshape(2, -1)
    og = grads_rows(jnp.concatenate([g_out, gwr, gwi], 1))
    return (
        result.reshape(block_input.shape), grad_input.reshape(block_input.shape), gn[0],
        grads_cols(g_gate), grads_cols(g_input), ch[:4], ch[4], og[:, width: width + hb], ch[5],
        og[:, width + hb:], ch[6], ch[7], og[:, :width], gn[1], grads_cols(g_up), grads_cols(g_value), grads_rows(g_down),
    )


def solution(mesh):
    rowsh, vec, mat = P("fsdp", "seq", None), P("fsdp"), P("fsdp", None)
    ov, om = P(BOTH), P(BOTH, None)
    return jax.shard_map(
        body,
        mesh=mesh,
        in_specs=(rowsh, rowsh, P(), vec, mat, mat, P(None, "fsdp"), vec, mat, vec, mat, vec, vec, mat, vec, mat, mat, mat),
        out_specs=(rowsh, rowsh, ov, om, om, P(None, BOTH), ov, om, ov, om, ov, ov, om, ov, om, om, om),
        check_vma=False,
    )
```

```python
import jax
import jax.numpy as jnp
from jax import lax
from jax.sharding import PartitionSpec as P
from jax.experimental import pallas as pl
from jax.experimental.pallas import tpu as pltpu

EPS_NORM = 1e-06
EPS_MULT = 0.0001
RATE_SCALE = 8.0
BF = jnp.bfloat16
F32 = jnp.float32
GROUP = "fsdp"
BOTH = ("seq", "fsdp")


def mm(left, right):
    return jnp.dot(left, right, preferred_element_type=F32)


def mm_lt(left, right):
    return lax.dot_general(left, right, (((0,), (0,)), ((), ())), preferred_element_type=F32)


def mm_rt(left, right):
    return lax.dot_general(left, right, (((1,), (1,)), ((), ())), preferred_element_type=F32)


def gelu_pair(v):
    c = 0.7978845608028654
    a = 0.044715
    u = c * (v + a * v * v * v)
    t = jnp.tanh(u)
    g = 0.5 * v * (1.0 + t)
    d = 0.5 * (1.0 + t) + 0.5 * v * (1.0 - t * t) * c * (1.0 + 3.0 * a * v * v)
    return g, d


def linear_step(first_pair, second_pair):
    return (first_pair[0] * second_pair[0], second_pair[1] + second_pair[0] * first_pair[1])


def rms(v, g):
    s = lax.rsqrt(jnp.mean(v * v, axis=-1, keepdims=True) + EPS_NORM)
    return (v * s * g).astype(BF), s


def rms_back(v, s, g, grad):
    gg = grad * g
    gain = jnp.sum(grad * v * s, axis=0)
    return s * gg - v * (s * s * s) * jnp.mean(gg * v, axis=-1, keepdims=True), gain


def ag(a):
    return lax.all_gather(a, GROUP, axis=0, tiled=True)


def rs(a):
    return lax.psum_scatter(a.astype(BF), GROUP, scatter_dimension=0, tiled=True).astype(F32)


def grads_cols(g):
    part = lax.psum_scatter(g.astype(BF), "seq", scatter_dimension=0, tiled=True)
    return lax.all_to_all(part, GROUP, split_axis=0, concat_axis=1, tiled=True).astype(F32)


def grads_rows(g):
    n, m = lax.axis_size("seq"), lax.axis_size(GROUP)
    part = lax.psum_scatter(g.astype(BF), "seq", scatter_dimension=0, tiled=True)
    pairs = [(j * m + f, f * n + j) for j in range(n) for f in range(m)]
    return lax.ppermute(part, BOTH, pairs).astype(F32)


def shifted(shard, axis, by):
    length = lax.axis_size(axis)
    pairs = [(i, i + by) for i in range(length) if 0 <= i + by < length]
    return lax.ppermute(shard, axis, pairs)


MESH = pl.DeviceIdType.MESH
VMEM = pl.BlockSpec(memory_space=pltpu.VMEM)
ANY = pl.BlockSpec(memory_space=pl.ANY)
LIMIT = 63 * 2**20


def ds(start, size):
    if not isinstance(start, int):
        start = pl.multiple_of(start, size if size % 128 else 128)
    return pl.ds(start, size)


def rows_at(block, size):
    return pl.ds(pl.multiple_of(block * size, size), size)


class Place:
    def __init__(self):
        self.n = lax.axis_size("seq")
        self.s, self.f = lax.axis_index("seq"), lax.axis_index("fsdp")
        f = self.f
        self.p1 = f + 1 - 2 * lax.rem(f, 2)
        self.p2 = lax.rem(f + 2, 4)
        self.p3 = lax.rem(self.p1 + 2, 4)
        self.sx = self.s + 1 - 2 * lax.rem(self.s, 2)

    def group(self, f):
        return (self.s, f)

    def line(self, s):
        return (s, self.f)

    def greet(self, hop=None):
        barrier = pltpu.get_barrier_semaphore()
        for f in (self.p1, self.p2, self.p3):
            pl.semaphore_signal(barrier, inc=1, device_id=self.group(f), device_id_type=MESH)

        def one(j, _):
            pl.semaphore_signal(
                barrier, inc=1, device_id=self.line(lax.rem(self.s + j, self.n)), device_id_type=MESH
            )
            return 0

        lax.fori_loop(1, self.n, one, 0)
        pl.semaphore_wait(barrier, 3 + self.n - 1 + (0 if hop is None else hop.greet(barrier)))


class Sems:
    def __init__(self, ref):
        self.ref, self.used = ref, 0

    def take(self):
        self.used += 1
        return self.ref.at[self.used - 1]

    def remote(self, src, dst, device):
        return pltpu.make_async_remote_copy(
            src_ref=src, dst_ref=dst, send_sem=self.take(), recv_sem=self.take(),
            device_id=device, device_id_type=MESH,
        )

    def local(self, src, dst):
        copy = pltpu.make_async_copy(src, dst, self.take())
        copy.start()
        return copy


class Gather:
    def __init__(self, at, sems, buf, chunk):
        self.at, self.buf, self.chunk = at, buf, chunk
        mine = lambda f, r: buf.at[rows_at(f * 2 + r, chunk)]
        self.core = [sems.remote(mine(at.f, r), mine(at.f, r), at.group(at.p1)) for r in range(2)]
        self.over = [sems.remote(mine(at.f, r), mine(at.f, r), at.group(at.p2)) for r in range(2)]
        self.pass_on = [sems.remote(mine(at.p2, r), mine(at.p2, r), at.group(at.p1)) for r in range(2)]

    def send(self, r):
        self.over[r].start()
        self.core[r].start()

    def relay(self, r):
        self.over[r].wait_recv()
        self.pass_on[r].start()

    def finish(self):
        for r in range(2):
            self.core[r].wait()
            self.over[r].wait_send()
            self.pass_on[r].wait()


class Scatter:
    def __init__(self, at, sems, core_out, core_in, over_out, over_in, chunk):
        self.at, self.chunk = at, chunk
        self.core_out, self.core_in, self.over_out, self.over_in = core_out, core_in, over_out, over_in
        self.core = [sems.remote(core_out.at[k], core_in.at[k], at.group(at.p1)) for k in range(2)]
        self.over = [
            sems.remote(
                over_out.at[pl.ds(r * chunk, chunk)], over_in.at[pl.ds(r * chunk, chunk)], at.group(at.p2)
            )
            for r in range(2)
        ]

    def run(self, partial, own, between=lambda k: None):
        at = self.at

        def put(ref):
            def store(sl, cols, tile):
                ref[sl, cols] = tile.astype(BF)

            return store

        partial(at.p3, put(self.core_out.at[0]))
        self.core[0].start()
        between(0)

        def add_over(sl, cols, tile):
            self.over_out[sl, cols] = (tile + self.core_in[0, sl, cols].astype(F32)).astype(BF)

        self.core[0].wait_recv()
        partial(at.p2, add_over)
        for r in range(2):
            self.over[r].start()
        between(1)
        partial(at.p1, put(self.core_out.at[1]))
        self.core[1].start()
        between(2)
        self.core[1].wait_recv()

        def add_own(sl, cols, tile):
            own[sl, cols] = own[sl, cols] + tile + self.core_in[1, sl, cols].astype(F32)

        partial(at.f, add_own)
        between(3)

    def run_tile(self, compute, tile, own, between=lambda k: None):
        at = self.at

        def one(k, _):
            compute(jnp.where(k == 0, at.p3, jnp.where(k == 1, at.p2, jnp.where(k == 2, at.p1, at.f))))

            @pl.when(k == 0)
            def _():
                self.core_out[0] = tile[...].astype(BF)
                self.core[0].start()

            @pl.when(k == 1)
            def _():
                self.core[0].wait_recv()
                for r in range(2):
                    sl = pl.ds(r * self.chunk, self.chunk)
                    self.over_out[sl, :] = (tile[sl, :] + self.core_in[0, sl, :].astype(F32)).astype(BF)
                    self.over[r].start()

            @pl.when(k == 2)
            def _():
                self.core_out[1] = tile[...].astype(BF)
                self.core[1].start()

            @pl.when(k == 3)
            def _():
                self.core[1].wait_recv()
                if own is None:
                    tile[...] = tile[...] + self.core_in[1].astype(F32)
                else:
                    own[...] = own[...] + tile[...] + self.core_in[1].astype(F32)

            between(k)
            return 0

        lax.fori_loop(0, 4, one, 0)

    def arrived(self, r):
        self.over[r].wait_recv()
        return self.over_in[pl.ds(r * self.chunk, self.chunk), :].astype(F32)

    def finish(self):
        for copy in self.core + self.over:
            copy.wait_send()


class Columns:
    def __init__(self, at, sems, weights, buf):
        rows, width = weights[0].shape
        part = width // 4
        cut = rows // 4
        h = lax.rem(at.s, 4)
        one = h + 1 - 2 * lax.rem(h, 2)
        mates = [at.line(at.s - h + m) for m in (one, lax.rem(h + 2, 4), lax.rem(one + 2, 4))]
        self.near, self.own, self.far, self.side = [], [], [], []
        for k, w in enumerate(weights):
            cols = pl.ds(k * part, part)
            take = lambda f: pl.ds(pl.multiple_of(f * part, 128), part)
            mine = pl.ds(pl.multiple_of(at.f * rows, rows), rows)
            quarter = pl.ds(pl.multiple_of(h * cut, cut), cut)
            mine_cut = pl.ds(pl.multiple_of(at.f * rows + h * cut, cut), cut)
            self.own.append(pltpu.make_async_copy(w.at[:, take(at.f)], buf.at[mine, cols], sems.take()))
            self.near.append(sems.remote(w.at[:, take(at.p1)], buf.at[mine, cols], at.group(at.p1)))
            for p in (at.p2, at.p3):
                self.far.append(sems.remote(w.at[quarter, take(p)], buf.at[mine_cut, cols], at.group(p)))
                came = buf.at[pl.ds(pl.multiple_of(p * rows + h * cut, cut), cut), cols]
                self.side.append([sems.remote(came, came, mate) for mate in mates])

    def start_far(self):
        for c in self.far:
            c.start()

    def start_near(self):
        for c in self.near + self.own:
            c.start()

    def relay(self, k):
        self.far[k].wait_recv()
        for c in self.side[k]:
            c.start()

    def finish(self):
        for c in self.own + self.near + sum(self.side, []):
            c.wait()
        for c in self.far:
            c.wait_send()


def expm1_neg(v):
    series = v * (1 + v * (1 / 2) * (1 + v * (1 / 3) * (1 + v * (1 / 4) * (1 + v * (1 / 5) * (1 + v * (1 / 6))))))
    return jnp.where(v > -0.25, series, jnp.exp(v) - 1.0)


def swap_rows(src, dst, outer, kind):
    total, width = src.shape
    inner = total // outer

    def one(c, _):
        cols = pl.ds(pl.multiple_of(c * 128, 128), 128)
        v = src[:, cols].reshape(outer, inner, 128)
        dst[:, cols] = jnp.swapaxes(v, 0, 1).reshape(total, 128).astype(kind)
        return 0

    lax.fori_loop(0, width // 128, one, 0)


def forward_branch(x, gains, chan, wr, wl, wo, wg, wi, wu, wv,
                   wgi_o, wuv_o, normed_o, n2_o, middle_o, gate_o, pad_o, conv_o, rate_o, inlet_o, decay_o, states_o,
                   merged_o, ends_o, gain_o,
                   wgi, normed, n2, middle, gain, gate, pad, conv, rate, inlet, decay, states, work, merged, ends,
                   tot, core_out, core_in, over_out, over_in, sem, tsend, trecv):
    at = Place()
    here, width = x.shape
    toks = here // 2
    chans = chan.shape[1]
    part = width // 4
    taps = 4
    steps = toks
    group = 8
    halo = (taps - 1) * group
    sems = Sems(sem)
    at.greet()

    shares = [
        sems.remote(gains, gain.at[at.f], at.group(p)) for p in (at.p1, at.p2, at.p3)
    ]
    for c in shares:
        c.start()
    gain[at.f] = gains[...]
    gi = Columns(at, sems, [wg, wi], wgi)
    gi.start_far()
    gi.start_near()
    uv = Columns(at, sems, [wu, wv], wuv_o)
    uv.start_near()
    ag1 = Gather(at, sems, normed, toks)
    for c in shares:
        c.wait()
    for r in range(2):
        sl = pl.ds(r * toks, toks)
        v = x[sl, :]
        scale = lax.rsqrt(jnp.mean(v * v, axis=-1, keepdims=True) + EPS_NORM)
        for p in range(4):
            cols = pl.ds(p * part, part)
            normed[rows_at(at.f * 2 + r, toks), cols] = (x[sl, cols] * scale * gain[p, 0:1, :]).astype(BF)
        ag1.send(r)
    for k in range(4):
        gi.relay(k)
    ag1.relay(0)
    uv.start_far()
    ag1.relay(1)
    ag1.finish()
    gi.finish()
    saves = [sems.local(normed, normed_o), sems.local(wgi, wgi_o), sems.local(gain, gain_o)]

    def branch_rows(m, _):
        sl = rows_at(m, here)
        work[sl, :] = mm(normed[sl, :], wgi[:, chans:]).astype(BF).astype(F32)
        return 0

    lax.fori_loop(0, 4, branch_rows, 0)
    swap_rows(work, pad.at[pl.ds(halo, steps * group)], group, F32)
    edge = pad.at[pl.ds(steps * group, halo)]
    next_one = lax.rem(at.s + 1, at.n)
    tail = sems.remote(edge, pad.at[pl.ds(0, halo)], at.line(next_one))

    @pl.when(at.s < at.n - 1)
    def _():
        tail.start()

    @pl.when(at.s == 0)
    def _():
        pad[0:halo, :] = jnp.zeros((halo, chans), F32)

    def gate_rows(m, _):
        sl = rows_at(m, here)
        work[sl, :] = mm(normed[sl, :], wgi[:, :chans])
        return 0

    lax.fori_loop(0, 4, gate_rows, 0)
    swap_rows(work, gate, group, F32)

    @pl.when(at.s > 0)
    def _():
        tail.wait_recv()

    @pl.when(at.s < at.n - 1)
    def _():
        tail.wait_send()


    def gates(b, _):
        for h in range(chans // 128):
            cols = pl.ds(h * 128, 128)
            size = 128
            start = pl.multiple_of(b * size, size)
            sl = pl.ds(start, size)
            total = chan[taps : taps + 1, cols]
            for k in range(taps):
                total = total + chan[k : k + 1, cols] * pad[pl.ds(start + (halo - group * k), size), cols]
            low = total.astype(BF)
            blocks = pl.ds(h * 128, 128)
            r = jax.nn.sigmoid(mm(low, wr[blocks, :]) + chan[5:6, cols])
            i = jax.nn.sigmoid(mm(low, wl[blocks, :]) + chan[6:7, cols])
            ld = r * chan[7:8, cols]
            conv[sl, cols] = low
            low = low.astype(F32)
            decay[sl, cols] = jnp.exp(ld)
            work[sl, cols] = jnp.sqrt(EPS_MULT - expm1_neg(2.0 * ld)) * i * low
            rate[sl, cols] = r
            inlet[sl, cols] = i
        return 0

    lax.fori_loop(0, steps * group // 128, gates, 0)
    saves += [
        sems.local(gate, gate_o), sems.local(pad, pad_o), sems.local(conv, conv_o), sems.local(rate, rate_o),
        sems.local(inlet, inlet_o), sems.local(decay, decay_o),
    ]

    unroll = 8

    def totals(b, carry):
        h, p = carry
        for u in range(unroll):
            sl = pl.ds(pl.multiple_of((b * unroll + u) * group, group), group)
            a = decay[sl, :]
            h = a * h + work[sl, :]
            p = p * a
        return h, p

    zero = jnp.zeros((group, chans), F32)
    h, p = lax.fori_loop(0, steps // unroll, totals, (zero, zero + 1.0))
    ends[0:8, :] = p
    ends[8:16, :] = h

    def total_copy(src, to):
        return pltpu.make_async_remote_copy(
            src_ref=ends.at[pl.ds(0, 16)], dst_ref=tot.at[src], send_sem=tsend.at[to], recv_sem=trecv.at[src],
            device_id=at.line(to), device_id_type=MESH,
        )

    def send_total(j, _):
        total_copy(at.s, j).start()
        return 0

    lax.fori_loop(at.s + 1, at.n, send_total, 0)

    def enter(j, state):
        total_copy(j, j).wait_recv()
        return tot[j, 0:8, :] * state + tot[j, 8:16, :]

    state_in = lax.fori_loop(0, at.s, enter, zero)

    def sent_total(j, _):
        total_copy(at.s, j).wait_send()
        return 0

    lax.fori_loop(at.s + 1, at.n, sent_total, 0)
    ends[16:24, :] = state_in

    def scan(b, h):
        for u in range(unroll):
            sl = pl.ds(pl.multiple_of((b * unroll + u) * group, group), group)
            h = decay[sl, :] * h + work[sl, :]
            states[sl, :] = h
        return h

    lax.fori_loop(0, steps // unroll, scan, state_in)
    saves += [sems.local(states, states_o), sems.local(ends, ends_o)]

    def merge(c, _):
        cols = pl.ds(pl.multiple_of(c * 128, 128), 128)

        def some(b, _):
            sl = rows_at(b, 128)
            work[sl, cols] = states[sl, cols] * gelu_pair(gate[sl, cols])[0]
            return 0

        lax.fori_loop(0, steps * group // 128, some, 0)
        return 0

    lax.fori_loop(0, chans // 128, merge, 0)
    swap_rows(work, merged, steps, BF)
    saves += [sems.local(merged, merged_o)]

    middle[...] = x[...]
    sc = Scatter(at, sems, core_out, core_in, over_out, over_in, toks)

    def partial(o, store):
        def half(r, _):
            sl = rows_at(r, toks)
            tile = mm(merged[rows_at(o * 2 + r, toks), :], wo[...])
            store(sl, slice(None), tile)
            return 0

        lax.fori_loop(0, 2, half, 0)

    def between(k):
        if k >= 2:
            uv.relay(2 * k - 4)
            uv.relay(2 * k - 3)

    sc.run(partial, middle, between)
    ag2 = Gather(at, sems, n2, toks)
    for r in range(2):
        sl = pl.ds(r * toks, toks)
        v = middle[sl, :] + sc.arrived(r)
        middle[sl, :] = v
        scale = lax.rsqrt(jnp.mean(v * v, axis=-1, keepdims=True) + EPS_NORM)
        for p in range(4):
            cols = pl.ds(p * part, part)
            n2[rows_at(at.f * 2 + r, toks), cols] = (middle[sl, cols] * scale * gain[p, 1:2, :]).astype(BF)
        ag2.send(r)
    saves += [sems.local(middle, middle_o)]
    for r in range(2):
        ag2.relay(r)
    ag2.finish()
    sc.finish()
    saves += [sems.local(n2, n2_o)]
    uv.finish()
    for c in saves:
        c.wait()


def call_forward(x, gains, chan, wr, wl, wo, wg, wi, wu, wv):
    here, width = x.shape
    chans = chan.shape[1]
    ffl = wu.shape[1] // 4
    every = here * 4
    n = lax.axis_size("seq")
    f32 = lambda *s: jax.ShapeDtypeStruct(s, F32)
    bf = lambda *s: jax.ShapeDtypeStruct(s, BF)
    vf = lambda *s: pltpu.VMEM(s, F32)
    vb = lambda *s: pltpu.VMEM(s, BF)
    outs = [
        bf(width, 2 * chans), bf(width, 2 * ffl), bf(every, width), bf(every, width), f32(here, width),
        f32(every, chans), f32(every + 24, chans), bf(every, chans), f32(every, chans), f32(every, chans),
        f32(every, chans), f32(every, chans), bf(every, chans), f32(24, chans), f32(4, 8, width // 4),
    ]
    scratch = [
        vb(width, 2 * chans), vb(every, width), vb(every, width), vf(here, width), vf(4, 8, width // 4),
        vf(every, chans), vf(every + 24, chans), vb(every, chans), vf(every, chans), vf(every, chans),
        vf(every, chans), vf(every, chans), vf(every, chans), vb(every, chans), vf(24, chans),
        vf(n, 16, chans), vb(2, here, width), vb(2, here, width), vb(here, width), vb(here, width),
        pltpu.SemaphoreType.DMA((170,)), pltpu.SemaphoreType.DMA((n,)), pltpu.SemaphoreType.DMA((n,)),
    ]
    return pl.pallas_call(
        forward_branch,
        out_shape=outs,
        in_specs=[VMEM] * 6 + [ANY] * 4,
        out_specs=[ANY] * len(outs),
        scratch_shapes=scratch,
        compiler_params=pltpu.CompilerParams(collective_id=1, has_side_effects=True, vmem_limit_bytes=LIMIT),
        name="forward_branch",
    )(x, gains, chan, wr, wl, wo, wg, wi, wu, wv)


class Hop:
    def __init__(self, at):
        b = at.f * at.n + at.s
        self.to = (lax.div(b, 4), lax.rem(b, 4))
        c = at.s * 4 + at.f
        self.source = (lax.rem(c, at.n), lax.div(c, at.n))
        self.stays = b == c

    def greet(self, barrier):
        @pl.when(jnp.logical_not(self.stays))
        def _():
            for device in (self.to, self.source):
                pl.semaphore_signal(barrier, inc=1, device_id=device, device_id_type=MESH)

        return jnp.where(self.stays, 0, 2)

    def start(self, sems, src, dst):
        far = sems.remote(src, dst, self.to)
        near = pltpu.make_async_copy(src, dst, sems.take())

        @pl.when(self.stays)
        def _():
            near.start()

        @pl.when(jnp.logical_not(self.stays))
        def _():
            far.start()

        return near, far

    def wait(self, pair):
        near, far = pair

        @pl.when(self.stays)
        def _():
            near.wait()

        @pl.when(jnp.logical_not(self.stays))
        def _():
            far.wait()


class Ring:
    def __init__(self, at, grads, slots, send, recv, by_rows):
        self.at, self.grads, self.slots, self.sem, self.rem = at, grads, slots, send, recv
        n = at.n
        self.q = self.place(at.s)
        rows, width = slots.shape[1:]
        self.rows = rows
        if by_rows:
            self.cut = [(pl.ds(i * rows // 4, rows // 4), pl.ds(0, width)) for i in range(4)]
        else:
            self.cut = [(pl.ds(0, rows), pl.ds(i * width // 4, width // 4)) for i in range(4)]
        self.way = (1, -1, 1, -1)
        self.to = {w: at.line(self.owner(lax.rem(self.q + w + n, n))) for w in (1, -1)}

    def place(self, s):
        half = lax.div(s, 2)
        return jnp.where(lax.rem(s, 2) == 0, half, self.at.n - 1 - half)

    def owner(self, q):
        n = self.at.n
        return jnp.where(q < n // 2, 2 * q, 2 * (n - 1 - q) + 1)

    def block(self, i, behind):
        n = self.at.n
        s = self.owner(lax.rem(self.q - self.way[i] * behind + 2 * n, n))
        r, c = self.cut[i]
        return self.grads.at[pl.ds(pl.multiple_of(s * self.rows + r.start, 16), r.size), c]

    def copy(self, i, k, src):
        r, c = self.cut[i]
        return pltpu.make_async_remote_copy(
            src_ref=src, dst_ref=self.slots.at[k, r, c], send_sem=self.sem.at[i, k], recv_sem=self.rem.at[i, k],
            device_id=self.to[self.way[i]], device_id_type=MESH,
        )

    def start(self):
        for i in range(4):
            self.copy(i, 0, self.block(i, 1)).start()

    def summed(self, i, k):
        r, c = self.cut[i]
        slot = self.slots.at[k, r, c]
        self.copy(i, k, slot).wait_recv()
        return slot, slot[...].astype(F32) + self.block(i, k + 2)[...].astype(F32)

    def step(self, k):
        for i in range(4):
            slot, value = self.summed(i, k)
            slot[...] = value.astype(BF)
            self.copy(i, k + 1, slot).start()

    def last(self, out, after=lambda i: None):
        k = self.at.n - 2
        for i in range(4):
            _, value = self.summed(i, k)
            out[self.cut[i]] = value.astype(out.dtype)
            after(i)

    def finish(self):
        def one(k, _):
            for i in range(4):
                r, c = self.cut[i]
                self.copy(i, k, self.slots.at[k, r, c]).wait_send()
            return 0

        lax.fori_loop(0, self.at.n - 1, one, 0)


class Regroup:
    def __init__(self, at, sems, src, dst):
        size = src.shape[0] // at.n
        self.far, self.near = [], []
        for h in range(at.n // 4):
            slot = dst.at[pl.ds(pl.multiple_of((at.f * (at.n // 4) + h) * size, 16), size)]
            block = lambda p: src.at[pl.ds(pl.multiple_of((p + 4 * h) * size, 16), size)]
            for p in (at.p2, at.p3, at.p1):
                self.far.append(sems.remote(block(p), slot, at.group(p)))
            self.near.append(pltpu.make_async_copy(block(at.f), slot, sems.take()))

    def start(self):
        for c in self.far + self.near:
            c.start()

    def wait(self):
        for c in self.far + self.near:
            c.wait()


class Spread:
    def __init__(self, at, sems, src, came):
        self.at, self.src, self.came = at, src, came
        rows = came.shape[1]
        send, recv = [sems.take() for _ in range(4)], [sems.take() for _ in range(4)]
        self.copies = []
        for k in range(1, 4):
            to = lax.rem(at.f + k, 4)
            piece = src.at[pl.ds(pl.multiple_of(to * rows, 16), rows)]
            self.copies.append(
                pltpu.make_async_remote_copy(
                    src_ref=piece, dst_ref=came.at[at.f], send_sem=send[k], recv_sem=recv[k],
                    device_id=at.group(to), device_id_type=MESH,
                )
            )

    def start(self):
        rows = self.came.shape[1]
        for c in self.copies:
            c.start()
        self.came[self.at.f] = self.src[pl.ds(pl.multiple_of(self.at.f * rows, 16), rows), :]

    def wait(self):
        for c in self.copies:
            c.wait()


def mlp(n2_h, wuv_h, wd_h, middle_h, teacher_h, scale, gain,
        result_o, gmid_o, gml_o, gain_o, down_o, up_o, value_o,
        n2, wuv, wd, hidden, ge, gdi, gml, middle, own, gout, tile, core_out, core_in, over_out, over_in,
        gwd, gwu, gwv, slots_u, last_u, gain_acc, sem, ring_sem):
    at = Place()
    sems = Sems(sem)
    here, width = middle.shape
    toks = here // 2
    ffl = hidden.shape[1]
    part = width // 4
    col = 384
    loads = [sems.local(n2_h, n2), sems.local(wuv_h, wuv), sems.local(wd_h, wd)]
    loads2 = [sems.local(middle_h, middle), sems.local(middle_h, own), sems.local(teacher_h, gout)]
    at.greet()
    for c in loads + loads2:
        c.wait()

    def forward(o):
        sl = rows_at(o, here)

        def some(c, _):
            cols = pl.ds(pl.multiple_of(c * col, 128), col)
            cols2 = pl.ds(pl.multiple_of(c * col + ffl, 128), col)
            up = mm(n2[sl, :], wuv[:, cols])
            g, d = gelu_pair(mm(n2[sl, :], wuv[:, cols2]))
            hidden[sl, cols] = (g * up).astype(BF)
            ge[sl, cols] = g.astype(BF)
            ge[sl, cols2] = (up * d).astype(BF)
            return 0

        lax.fori_loop(0, ffl // col, some, 0)

        def out(c, _):
            cols = pl.ds(pl.multiple_of(c * 512, 128), 512)
            tile[:, cols] = mm(hidden[sl, :], wd[:, cols])
            return 0

        lax.fori_loop(0, width // 512, out, 0)

    sc = Scatter(at, sems, core_out, core_in, over_out, over_in, toks)
    sc.run_tile(forward, tile, own)
    ag = Gather(at, sems, gdi, toks)
    for r in range(2):
        sl = pl.ds(r * toks, toks)
        v = own[sl, :] + sc.arrived(r)
        own[sl, :] = v
        v = (v - gout[sl, :]) * scale[sl, 0:1]
        v = jnp.where(scale[sl, 0:1] > 0.0, v, 0.0)
        gout[sl, :] = v
        gdi[rows_at(at.f * 2 + r, toks), :] = v.astype(BF)
        ag.send(r)
    saves = [sems.local(own, result_o)]
    for r in range(2):
        ag.relay(r)
    ag.finish()
    sc.finish()
    saves.pop().wait()

    def down_rows(m, _):
        cols = pl.ds(pl.multiple_of(m * 128, 128), 128)
        gwd[rows_at(m, 128), :] = mm_lt(hidden[:, cols], gdi[...]).astype(BF)
        return 0

    def hidden_rows(o, _):
        sl = rows_at(o, here)

        def some(c, _):
            cols = pl.ds(pl.multiple_of(c * col, 128), col)
            cols2 = pl.ds(pl.multiple_of(c * col + ffl, 128), col)
            gh = mm_rt(gdi[sl, :], wd[cols, :])
            ge[sl, cols] = (gh * ge[sl, cols].astype(F32)).astype(BF)
            ge[sl, cols2] = (gh * ge[sl, cols2].astype(F32)).astype(BF)
            return 0

        lax.fori_loop(0, ffl // col, some, 0)
        return 0

    def weight_rows(grads, first):
        def one(m, _):
            cols = pl.ds(pl.multiple_of(m * 256, 256), 256)
            grads[rows_at(m, 256), :] = mm_lt(n2[:, cols], ge[:, first : first + ffl]).astype(BF)
            return 0

        return one

    def backward(o):
        sl = rows_at(o, here)

        def out(c, _):
            cols = pl.ds(pl.multiple_of(c * 512, 128), 512)
            tile[:, cols] = mm_rt(ge[sl, :], wuv[cols, :])
            return 0

        lax.fori_loop(0, width // 512, out, 0)

    ring_u = Ring(at, gwu, slots_u, ring_sem.at[0], ring_sem.at[1], True)
    six = width // 256
    lax.fori_loop(0, 4, hidden_rows, 0)
    lax.fori_loop(0, six, weight_rows(gwu, 0), 0)
    ring_u.start()
    sc2 = Scatter(at, sems, core_out, core_in, over_out, over_in, toks)

    def between(k):
        @pl.when(k >= 2)
        def _():
            ring_u.step(k - 2)

    sc2.run_tile(backward, tile, None, between)
    lax.fori_loop(0, six, weight_rows(gwv, ffl), 0)
    ring_u.step(2)
    lax.fori_loop(0, ffl // 128, down_rows, 0)
    ring_u.step(3)
    saves += [sems.local(gwv, value_o), sems.local(gwd, down_o)]
    ag2 = Gather(at, sems, gml, toks)
    acc = jnp.zeros((1, width), F32)
    for r in range(2):
        sl = pl.ds(r * toks, toks)
        g = tile[sl, :] + sc2.arrived(r)
        v = middle[sl, :]
        s = lax.rsqrt(jnp.mean(v * v, axis=-1, keepdims=True) + EPS_NORM)
        acc = acc + jnp.sum(g * v * s, axis=0, keepdims=True)
        gg = g * gain[...]
        mean = jnp.mean(gg * v, axis=-1, keepdims=True)
        new = gout[sl, :] + s * gg - v * (s * s * s * mean)
        own[sl, :] = new
        gml[rows_at(at.f * 2 + r, toks), :] = new.astype(BF)
        ag2.send(r)
    gain_acc[...] = jnp.broadcast_to(acc, gain_acc.shape)
    saves += [sems.local(own, gmid_o), sems.local(gain_acc, gain_o)]
    ring_u.step(4)
    ag2.relay(0)
    ring_u.step(5)
    ag2.relay(1)
    ring_u.last(last_u)
    saves += [sems.local(last_u, up_o)]
    ag2.finish()
    sc2.finish()
    saves += [sems.local(gml, gml_o)]
    ring_u.finish()
    for c in saves:
        c.wait()


def call_mlp(n2, wuv, wd, middle, teacher, scale, gain):
    every, width = n2.shape
    here = middle.shape[0]
    ffl = wd.shape[0]
    n = lax.axis_size("seq")
    f32 = lambda *s: jax.ShapeDtypeStruct(s, F32)
    bf = lambda *s: jax.ShapeDtypeStruct(s, BF)
    vf = lambda *s: pltpu.VMEM(s, F32)
    vb = lambda *s: pltpu.VMEM(s, BF)
    outs = [
        f32(here, width), f32(here, width), bf(every, width), f32(8, width), bf(ffl, width),
        bf(width // n, ffl), bf(width, ffl),
    ]
    scratch = [
        vb(every, width), vb(width, 2 * ffl), vb(ffl, width), vb(every, ffl), vb(every, 2 * ffl), vb(every, width),
        vb(every, width), vf(here, width), vf(here, width), vf(here, width), vf(here, width),
        vb(2, here, width), vb(2, here, width), vb(here, width), vb(here, width),
        vb(ffl, width), vb(width, ffl), vb(width, ffl), vb(n - 1, width // n, ffl),
        vb(width // n, ffl), vf(8, width),
        pltpu.SemaphoreType.DMA((100,)), pltpu.SemaphoreType.DMA((2, 4, n - 1)),
    ]
    return pl.pallas_call(
        mlp,
        out_shape=outs,
        in_specs=[ANY] * 5 + [VMEM] * 2,
        out_specs=[ANY] * len(outs),
        scratch_shapes=scratch,
        compiler_params=pltpu.CompilerParams(collective_id=2, has_side_effects=True, vmem_limit_bytes=LIMIT),
        name="mlp",
    )(n2, wuv, wd, middle, teacher, scale, gain)


class Line:
    def __init__(self, at, src, tot, send, recv):
        self.at, self.src, self.tot, self.send_sem, self.recv_sem = at, src, tot, send, recv

    def copy(self, slot, to):
        return pltpu.make_async_remote_copy(
            src_ref=self.src, dst_ref=self.tot.at[slot], send_sem=self.send_sem.at[to], recv_sem=self.recv_sem.at[slot],
            device_id=self.at.line(to), device_id_type=MESH,
        )

    def send(self, first, end):
        def one(j, _):
            @pl.when(j != self.at.s)
            def _():
                self.copy(self.at.s, j).start()

            return 0

        lax.fori_loop(first, end, one, 0)

    def sent(self, first, end):
        def one(j, _):
            @pl.when(j != self.at.s)
            def _():
                self.copy(self.at.s, j).wait_send()

            return 0

        lax.fori_loop(first, end, one, 0)

    def wait(self, j):
        self.copy(j, j).wait_recv()


def branch_back(chan, wr, wl, gain, gain2,
                gml_h, merged_h, wo_h, wgi_h, normed_h, gate_h, pad_h, conv_h, rate_h, inlet_h, decay_h, states_h, ends_h,
                gwd_h, x_h, gmid_h, up_h, value_h,
                ginput_o, up_o, value_o, down_o, gate_o, input_o, out_o, rate_o, inlet_o, chan_o, gains_o,
                gml, merged, wo, wgi, gate, pad, conv, rate, inlet, decay, states, ends, gwd, gwv, own,
                work, gconv, pair, heads_r, heads_l, acc, tile, core_in, over_out, over_in,
                go, ggi, slots_d, slots_v, slots_o, slots_g, last_u, last_o, last_g, came_u, came_v, came_o, came_g,
                passed, tot, small, small_in, small_sum, group_in, gains,
                sem, ring_sem, line_sem):
    at = Place()
    sems = Sems(sem)
    here, width = own.shape
    toks = here // 2
    chans = chan.shape[1]
    group, taps = 8, 4
    steps = toks
    every = steps * group
    halo = (taps - 1) * group
    n = at.n
    ffl = came_u.shape[2]
    early = [
        sems.local(value_h, gwv), sems.local(up_h, last_u), sems.local(gml_h, gml),
        sems.local(wo_h.at[pl.ds(0, here)], wo.at[0]), sems.local(wo_h.at[pl.ds(here, here)], wo.at[1]),
    ]
    second = [sems.local(gate_h, gate), sems.local(states_h, states.at[pl.ds(group, every)]), sems.local(ends_h, ends)]
    third = [sems.local(decay_h, decay), sems.local(merged_h, merged)]
    fourth = [
        sems.local(a, b)
        for a, b in ((pad_h, pad), (conv_h, conv), (rate_h, rate), (inlet_h, inlet), (wgi_h, wgi), (gmid_h, own))
    ]
    hop = Hop(at)
    at.greet(hop)
    ring_d = Ring(at, gwd, slots_d, ring_sem.at[0], ring_sem.at[1], False)
    ring_v = Ring(at, gwv, slots_v, ring_sem.at[6], ring_sem.at[7], True)
    ring_o = Ring(at, go, slots_o, ring_sem.at[2], ring_sem.at[3], True)
    ring_g = Ring(at, ggi, slots_g, ring_sem.at[4], ring_sem.at[5], True)
    for c in early:
        c.wait()
    ring_v.start()
    regroup = Regroup(at, sems, gwd_h, gwd)
    spread_u = Spread(at, sems, last_u, came_u)
    spread_u.start()
    regroup.start()

    def staged(came, first, size, outs, base=0):
        rows = came.shape[1]
        for f in range(4):
            at_col = f * size
            done = 0
            while done < size:
                block, col = divmod(at_col + done, width)
                step = min(size - done, width - col)
                tile[base + block * rows : base + (block + 1) * rows, col : col + step] = came[
                    f, :, first + done : first + done + step
                ].astype(F32)
                done += step
        copies, done = [], 0
        while done < 4 * size:
            step = min(width, 4 * size - done)
            copies.append(
                sems.local(tile.at[pl.ds(base + done // width * rows, rows), pl.ds(0, step)], outs.at[:, pl.ds(done, step)])
            )
            done += step
        return copies

    def merged_rows(m, _):
        sl = rows_at(m, here)
        for h in range(2):
            work[sl, pl.ds(h * here, here)] = mm_rt(gml[sl, :], wo[h])
        return 0

    lax.fori_loop(0, 4, merged_rows, 0)
    for c in second:
        c.wait()
    states[0:group, :] = ends[16:24, :]

    def split(c, _):
        cols = pl.ds(pl.multiple_of(c * 128, 128), 128)
        g = jnp.swapaxes(work[:, cols].reshape(group, steps, 128), 0, 1).reshape(every, 128)
        act, slope = gelu_pair(gate[:, cols])
        gate[:, cols] = g * act
        down = g * states[pl.ds(group, every), cols] * slope
        pair[:, cols] = jnp.swapaxes(down.reshape(steps, group, 128), 0, 1).reshape(every, 128).astype(BF)
        return 0

    lax.fori_loop(0, chans // 128, split, 0)
    ring_v.step(0)
    for c in third:
        c.wait()
    unroll = 8
    blocks = steps // unroll

    def totals(b, carry):
        for u in range(unroll):
            sl = pl.ds(pl.multiple_of((steps - 1 - (b * unroll + u)) * group, group), group)
            carry = decay[sl, :] * (gate[sl, :] + carry)
        return carry

    zero = jnp.zeros((group, chans), F32)
    passed[0:8, :] = ends[0:8, :]
    passed[8:16, :] = lax.fori_loop(0, blocks, totals, zero)
    line = Line(at, passed, tot, line_sem.at[0], line_sem.at[1])
    line.send(0, at.s)

    def out_rows(m, _):
        cols = pl.ds(pl.multiple_of(m * 256, 256), 256)
        go[rows_at(m, 256), 0:width] = mm_lt(merged[:, cols], gml[...]).astype(BF)
        return 0

    lax.fori_loop(0, chans // 256, out_rows, 0)
    normed, core_out = gml, wo
    fourth.append(sems.local(normed_h, normed))

    def enter(k, state):
        j = n - 1 - k
        line.wait(j)
        return tot[j, 0:8, :] * state + tot[j, 8:16, :]

    carry_in = lax.fori_loop(0, n - 1 - at.s, enter, zero)
    line.sent(0, at.s)

    def scan(b, carry):
        for u in range(unroll):
            sl = pl.ds(pl.multiple_of((steps - 1 - (b * unroll + u)) * group, group), group)
            adjoint = gate[sl, :] + carry
            gate[sl, :] = adjoint
            carry = decay[sl, :] * adjoint
        return carry

    lax.fori_loop(0, blocks, scan, carry_in)
    ring_v.step(1)
    spread_u.wait()
    staging = staged(came_u, 0, ffl, up_o)
    for c in fourth:
        c.wait()
    heads_r[...] = jnp.zeros_like(heads_r)
    heads_l[...] = jnp.zeros_like(heads_l)
    acc[...] = jnp.zeros_like(acc)
    edge = sems.remote(
        gconv.at[pl.ds(0, halo)], gconv.at[pl.ds(every, halo)], at.line(lax.rem(at.s + n - 1, n))
    )

    def gates(b, _):
        size = 128
        start = pl.multiple_of(b * size, size)
        sl = pl.ds(start, size)
        for h in range(chans // 128):
            cols = pl.ds(h * 128, 128)
            sp8 = chan[7:8, cols]
            r, i, dec, adj = rate[sl, cols], inlet[sl, cols], decay[sl, cols], gate[sl, cols]
            low_bf = conv[sl, cols]
            low = low_bf.astype(F32)
            factor = jnp.sqrt(EPS_MULT - expm1_neg(2.0 * (r * sp8)))
            ai = adj * i
            af = adj * factor
            gld = adj * states[sl, cols] * dec - ai * low * (dec * dec) / factor
            gldr = gld * r
            grate = gldr * sp8 * (1.0 - r)
            ginl = af * low * i * (1.0 - i)
            grl, gil = grate.astype(BF), ginl.astype(BF)
            hb = pl.ds(h * 128, 128)
            gc = af * i + mm_rt(grl, wr[hb, :]) + mm_rt(gil, wl[hb, :])
            heads_r[hb, :] += mm_lt(low_bf, grl)
            heads_l[hb, :] += mm_lt(low_bf, gil)
            gconv[sl, cols] = gc
            fold = lambda v: jnp.sum(v.reshape(size // 8, 8, 128), axis=0)
            for k in range(taps):
                acc[k, :, cols] += fold(gc * pad[pl.ds(start + (halo - group * k), size), cols])
            acc[4, :, cols] += fold(gc)
            acc[5, :, cols] += fold(grate)
            acc[6, :, cols] += fold(ginl)
            acc[7, :, cols] += fold(gldr)

        @pl.when(jnp.logical_and(b == 0, at.s > 0))
        def _():
            edge.start()

        return 0

    lax.fori_loop(0, every // 128, gates, 0)

    @pl.when(at.s == n - 1)
    def _():
        gconv[pl.ds(every, halo), :] = jnp.zeros((halo, chans), F32)

    thirds = width // chans
    inputs = [
        sems.local(x_h.at[:, pl.ds(k * chans, chans)], pad.at[pl.ds(k * here, here)]) for k in range(thirds)
    ]
    go[:, width : width + 128] = heads_r[...].astype(BF)
    go[:, width + 128 :] = heads_l[...].astype(BF)
    ring_o.start()
    ring_v.step(2)
    for k in range(8):
        small[k : k + 1, :] = jnp.sum(acc[k], axis=0, keepdims=True)
    small[7:8, :] = small[7:8, :] * chan[8:9, :]

    @pl.when(at.s < n - 1)
    def _():
        edge.wait_recv()

    @pl.when(at.s > 0)
    def _():
        edge.wait_send()

    def taps_back(b, _):
        start = pl.multiple_of(b * 128, 128)
        for h in range(chans // 128):
            cols = pl.ds(h * 128, 128)
            total = chan[0:1, cols] * gconv[pl.ds(start, 128), cols]
            for k in range(1, taps):
                total = total + chan[k : k + 1, cols] * gconv[pl.ds(start + group * k, 128), cols]
            work[pl.ds(start, 128), cols] = total
        return 0

    lax.fori_loop(0, every // 128, taps_back, 0)
    swap_rows(work, pair.at[:, pl.ds(chans, chans)], steps, BF)
    ring_v.step(3)

    def normed_rows(m, _):
        cols = pl.ds(pl.multiple_of(m * 256, 256), 256)
        ggi[rows_at(m, 256), :] = mm_lt(normed[:, cols], pair[...]).astype(BF)
        return 0

    lax.fori_loop(0, width // 256, normed_rows, 0)
    ring_g.start()
    for c in staging:
        c.wait()

    def back(o):
        sl = rows_at(o, here)

        def some(c, _):
            cols = pl.ds(pl.multiple_of(c * 512, 128), 512)
            tile[:, cols] = mm_rt(pair[sl, :], wgi[cols, :])
            return 0

        lax.fori_loop(0, width // 512, some, 0)

    sc = Scatter(at, sems, core_out, core_in, over_out, over_in, toks)

    def between(k):
        for j, ring, step in ((1, ring_v, 4), (2, ring_o, 0), (3, ring_v, 5)):

            @pl.when(k == j)
            def _():
                ring.step(step)

    sc.run_tile(back, tile, None, between)
    ring_g.step(0)
    spread_v = Spread(at, sems, last_u, came_v)
    ring_v.last(last_u)
    spread_v.start()
    regroup.wait()
    ring_d.start()
    ring_o.step(1)
    ring_g.step(1)
    gain1 = jnp.zeros((1, width), F32)
    for c in inputs:
        c.wait()
    for r in range(2):
        sl = pl.ds(r * toks, toks)
        g = tile[sl, :] + sc.arrived(r)
        v = jnp.concatenate([pad[pl.ds(k * here + r * toks, toks), :] for k in range(thirds)], axis=1)
        s = lax.rsqrt(jnp.mean(v * v, axis=-1, keepdims=True) + EPS_NORM)
        gain1 = gain1 + jnp.sum(g * v * s, axis=0, keepdims=True)
        gg = g * gain[...]
        mean = jnp.mean(gg * v, axis=-1, keepdims=True)
        own[sl, :] = own[sl, :] + s * gg - v * (s * s * s * mean)
    saves = [sems.local(own, ginput_o)]
    ring_d.step(0)
    ring_g.step(2)
    ring_o.step(2)
    for k in range(3):
        small[8 + k : 9 + k, :] = gain1[:, k * chans : (k + 1) * chans]
        small[11 + k : 12 + k, :] = gain2[0:1, k * chans : (k + 1) * chans]
    small[14:16, :] = jnp.zeros((2, chans), F32)
    share = Line(at, small, small_in, line_sem.at[2], line_sem.at[3])
    share.send(0, n)
    ring_d.step(1)
    spread_v.wait()
    saves += staged(came_v, 0, ffl, value_o)
    ring_g.step(3)
    ring_o.step(3)
    ring_d.step(2)
    small_in[at.s] = small[...]

    def arrive(j, total):
        @pl.when(j != at.s)
        def _():
            share.wait(j)

        return total + small_in[j]

    small_sum[...] = lax.fori_loop(0, n, arrive, jnp.zeros(small.shape, F32))
    ring_g.step(4)
    ring_o.step(4)
    ring_d.step(3)
    hops = [hop.start(sems, small_sum.at[pl.ds(0, 8)], chan_o)]
    lower = small_sum.at[pl.ds(8, 8)]
    around = [sems.remote(lower, group_in.at[at.f], at.group(p)) for p in (at.p1, at.p2, at.p3)]
    for c in around:
        c.start()
    group_in[at.f] = small_sum[8:16, :]
    ring_g.step(5)
    ring_o.step(5)
    ring_d.step(4)
    spread_g = Spread(at, sems, last_g, came_g)
    ring_g.last(last_g)
    spread_g.start()
    ring_o.last(last_o)
    hops.append(hop.start(sems, last_o, came_o))
    for c in saves:
        c.wait()
    ring_d.step(5)
    ring_d.last(tile)
    saves = [sems.local(tile.at[pl.ds(0, gwd.shape[0] // n)], down_o)]
    hop.wait(hops[1])
    crow = came_o.shape[0]
    for k in range(thirds + 1):
        size = min(chans, came_o.shape[1] - k * chans)
        rate[k * crow : (k + 1) * crow, 0:size] = came_o[:, k * chans : k * chans + size].astype(F32)
    saves += [
        sems.local(rate.at[pl.ds(k * crow, crow)], out_o.at[:, pl.ds(k * chans, chans)]) for k in range(thirds)
    ]
    saves += [
        sems.local(rate.at[pl.ds(thirds * crow, crow), pl.ds(k * 128, 128)], o) for k, o in enumerate((rate_o, inlet_o))
    ]
    for c in around:
        c.wait()
    gains[...] = group_in[0] + group_in[1] + group_in[2] + group_in[3]
    saves += [sems.local(gains, gains_o)]
    share.sent(0, n)
    sc.finish()
    for r in (ring_v, ring_d, ring_o, ring_g):
        r.finish()
    spread_g.wait()
    for c in saves:
        c.wait()
    saves = staged(came_g, 0, chans, gate_o) + staged(came_g, chans, chans, input_o, here // 2)
    hop.wait(hops[0])
    for c in saves:
        c.wait()


def call_back(chan, wr, wl, gain, gain2, gml, merged, wo, wgi, normed, gate, pad, conv, rate, inlet, decay, states, ends, gwd, x, gmid, up, value):
    every, width = gml.shape
    here = x.shape[0]
    chans = chan.shape[1]
    ffl = gwd.shape[0]
    n = lax.axis_size("seq")
    f32 = lambda *s: jax.ShapeDtypeStruct(s, F32)
    vf = lambda *s: pltpu.VMEM(s, F32)
    vb = lambda *s: pltpu.VMEM(s, BF)
    rows, crow = width // n, chans // n
    outs = [
        f32(here, width), f32(rows // 4, 4 * ffl), f32(rows // 4, 4 * ffl), f32(ffl // n, width), f32(rows // 4, 4 * chans), f32(rows // 4, 4 * chans), f32(crow, width),
        f32(crow, 128), f32(crow, 128), f32(8, chans), f32(8, chans),
    ]
    scratch = [
        vb(every, width), vb(every, chans), vb(2, here, width), vb(width, 2 * chans),
        vf(every, chans), vf(every + 24, chans), vb(every, chans), vf(every, chans), vf(every, chans), vf(every, chans),
        vf(every + 8, chans), vf(24, chans), vb(ffl, width), vb(width, ffl), vf(here, width),
        vf(every, chans), vf(every + 24, chans), vb(every, 2 * chans), vf(chans, 128), vf(chans, 128), vf(8, 8, chans),
        vf(here, width), vb(2, here, width), vb(here, width), vb(here, width),
        vb(chans, width + 256), vb(width, 2 * chans), vb(n - 1, ffl // n, width), vb(n - 1, rows, ffl), vb(n - 1, crow, width + 256), vb(n - 1, rows, 2 * chans),
        vb(rows, ffl), vb(crow, width + 256), vb(rows, 2 * chans), vb(4, rows // 4, ffl), vb(4, rows // 4, ffl),
        vb(crow, width + 256), vb(4, rows // 4, 2 * chans),
        vf(16, chans), vf(n, 16, chans), vf(16, chans), vf(n, 16, chans), vf(16, chans), vf(4, 8, chans), vf(8, chans),
        pltpu.SemaphoreType.DMA((120,)), pltpu.SemaphoreType.DMA((8, 4, n - 1)), pltpu.SemaphoreType.DMA((4, n)),
    ]
    return pl.pallas_call(
        branch_back,
        out_shape=outs,
        in_specs=[VMEM] * 5 + [ANY] * 18,
        out_specs=[ANY] * len(outs),
        scratch_shapes=scratch,
        compiler_params=pltpu.CompilerParams(collective_id=3, has_side_effects=True, vmem_limit_bytes=LIMIT),
        name="branch_back",
    )(chan, wr, wl, gain, gain2, gml, merged, wo, wgi, normed, gate, pad, conv, rate, inlet, decay, states, ends, gwd, x, gmid, up, value)


def body(
    block_input, teacher, valid_lengths, norm_gain, w_gate, w_input, conv_weight, conv_bias,
    w_rate, bias_rate, w_inlet, bias_inlet, decay_param, w_out, mlp_gain, w_up, w_value, w_down,
):
    n_seq, n_fs = lax.axis_size("seq"), lax.axis_size(GROUP)
    si, fi = lax.axis_index("seq"), lax.axis_index(GROUP)
    rows_dev, toks, width = block_input.shape
    rows = rows_dev * n_fs
    here = rows_dev * toks
    chans = conv_bias.shape[0]
    hb = w_rate.shape[1]
    heads = chans // hb
    taps = conv_weight.shape[0]

    cw = conv_weight.astype(F32)
    sp = jax.nn.softplus(-decay_param.astype(F32))
    x = block_input.reshape(here, width)
    gains = jnp.concatenate([norm_gain[None].astype(F32), mlp_gain[None].astype(F32), jnp.zeros((6, width // 4), F32)])
    vec = lambda v: v.astype(F32)[None]
    chan = jnp.concatenate([cw, vec(conv_bias), vec(bias_rate), vec(bias_inlet), vec(-RATE_SCALE * sp), vec(RATE_SCALE * jax.nn.sigmoid(-decay_param.astype(F32))), jnp.zeros((7, chans), F32)])
    (wgi, wuv, normed, n2, middle, gate_tm, pad_tm, conv_tm, rate_tm, inlet_tm, decay_tm, states_tm, merged, ends, gain) = call_forward(
        x, gains, chan, w_rate, w_inlet, w_out, w_gate, w_input, w_up, w_value)
    lens = lax.dynamic_slice_in_dim(valid_lengths, fi * rows_dev, rows_dev)
    pos = si * toks + jnp.arange(toks, dtype=jnp.int32)
    mask = (pos[None, :] < lens[:, None]).reshape(here, 1)
    slots = valid_lengths.shape[0] * toks * n_seq
    count = jnp.sum(valid_lengths).astype(F32)
    if all((v // n_seq) % 64 == 0 for v in (width, chans)):
        scale = jnp.broadcast_to(jnp.where(mask, slots / count, 0.0), (here, 128))
        result, grad_middle, gml, gain2, g_down, up_part, value_part = call_mlp(
            n2, wuv, w_down, middle, teacher.reshape(here, width), scale, gain[:, 1].reshape(1, -1))
        grad_input, up_sum, value_sum, down_sum, gate_sum, input_sum, out_sum, rate_sum, inlet_sum, ch, gn = call_back(
            chan, w_rate, w_inlet, gain[:, 0].reshape(1, -1), gain2, gml, merged, w_out, wgi, normed, gate_tm, pad_tm,
            conv_tm, rate_tm, inlet_tm, decay_tm, states_tm, ends, g_down, x, grad_middle, up_part, value_part)
        place = si * n_fs + fi
        per = chans // n_seq
        ch = lax.dynamic_slice_in_dim(ch, lax.rem(place, n_seq) * per, per, 1)
        per = width // (n_seq * n_fs)
        gn = lax.dynamic_slice_in_dim(gn[:6].reshape(2, width), place * per, per, 1)
        return (
            result.reshape(block_input.shape), grad_input.reshape(block_input.shape), gn[0], gate_sum, input_sum,
            ch[:4], ch[4], rate_sum, ch[5], inlet_sum, ch[6], ch[7], out_sum, gn[1], up_sum, value_sum, down_sum,
        )

    heads_shape = (heads, hb, hb)
    wr, wl = w_rate.reshape(heads_shape), w_inlet.reshape(heads_shape)
    wg, wi = wgi[:, :chans], wgi[:, chans:]
    wu, wv = wuv[:, :wuv.shape[1]//2], wuv[:, wuv.shape[1]//2:]
    gain_one, gain_two = gain[:, 0].reshape(-1), gain[:, 1].reshape(-1)
    s1 = lax.rsqrt(jnp.mean(x * x, axis=-1, keepdims=True) + EPS_NORM)
    s2 = lax.rsqrt(jnp.mean(middle * middle, axis=-1, keepdims=True) + EPS_NORM)
    tok = lambda v: v.reshape(-1, rows, chans).swapaxes(0, 1)
    padded, clf, r, i, decay, states = tok(pad_tm), tok(conv_tm), tok(rate_tm), tok(inlet_tm), tok(decay_tm), tok(states_tm)
    conv_low, clf = clf, clf.astype(F32)
    heads_in = conv_low.reshape(rows * toks, heads, hb)
    gate_pre = tok(gate_tm).reshape(-1, chans)
    gg, gd = gelu_pair(gate_pre)
    cum_end, state_in = ends[:8], ends[16:24]
    prev = jnp.concatenate([state_in[:, None], states[:, :-1]], axis=1)
    ld = -RATE_SCALE * r * sp
    factor = jnp.sqrt(EPS_MULT - jnp.expm1(2.0 * ld))
    up = mm(n2, wu)
    value = mm(n2, wv)
    vg, vd = gelu_pair(value)
    hidden = (vg * up).astype(BF)
    result = middle + rs(mm(hidden, w_down))
    grad_out = jnp.where(mask, result - teacher.reshape(here, width), 0.0) * (slots / count)
    gdi = ag(grad_out.astype(BF))
    g_down = mm_lt(hidden, gdi)
    gh = mm_rt(gdi, w_down)
    gu = (gh * vg).astype(BF)
    gv = (gh * up * vd).astype(BF)
    g_up = mm_lt(n2, gu)
    g_value = mm_lt(n2, gv)
    gn2 = rs(mm_rt(gu, wu) + mm_rt(gv, wv))
    gm_norm, gain2 = rms_back(middle, s2, gain_two, gn2)
    grad_middle = grad_out + gm_norm
    gml = ag(grad_middle.astype(BF))
    g_out = mm_lt(merged, gml)
    gmer = mm_rt(gml, w_out)
    gst = (gmer * gg).reshape(rows, toks, chans)
    ggate = (gmer * states.reshape(-1, chans) * gd).astype(BF)
    nextd = jnp.concatenate([decay[:, 1:], jnp.ones((rows, 1, chans), F32)], axis=1)
    carry, ladj = lax.associative_scan(linear_step, (nextd, gst), axis=1, reverse=True)
    tot2 = lax.all_gather(jnp.stack([cum_end, decay[:, 0] * ladj[:, 0]]), "seq")
    adj_in = jnp.zeros((rows, chans), F32)
    for j in reversed(range(n_seq)):
        adj_in = jnp.where(j > si, tot2[j, 0] * adj_in + tot2[j, 1], adj_in)
    adj = ladj + carry * adj_in[:, None]
    gdec = adj * prev
    gfac = adj * i * clf
    gld = gdec * decay - gfac * (decay * decay) / factor
    grate = gld * (-RATE_SCALE * sp) * r * (1.0 - r)
    ginl = adj * factor * clf * i * (1.0 - i)
    gdp = jnp.sum(gld * r, axis=(0, 1)) * RATE_SCALE * jax.nn.sigmoid(-decay_param.astype(F32))
    gcd = adj * factor * i
    grb, gib = jnp.sum(grate, (0, 1)), jnp.sum(ginl, (0, 1))
    grl, gil = grate.astype(BF).reshape(-1, heads, hb), ginl.astype(BF).reshape(-1, heads, hb)
    gwr = jnp.einsum("nhi,nhj->hij", heads_in, grl, preferred_element_type=F32).reshape(chans, hb)
    gwi = jnp.einsum("nhi,nhj->hij", heads_in, gil, preferred_element_type=F32).reshape(chans, hb)
    bk = lambda a, w: jnp.einsum("nhj,hij->nhi", a, w, preferred_element_type=F32).reshape(rows, toks, chans)
    gconv = gcd + bk(grl, wr) + bk(gil, wl)
    gcw = jnp.stack([jnp.sum(gconv * padded[:, taps - 1 - k: taps - 1 - k + toks], (0, 1)) for k in range(taps)])
    gcb = jnp.sum(gconv, (0, 1))
    gpad = jnp.zeros((rows, toks + taps - 1, chans), F32)
    for k in range(taps):
        gpad = gpad.at[:, taps - 1 - k: taps - 1 - k + toks].add(cw[k] * gconv)
    edge = shifted(gpad[:, : taps - 1], "seq", -1)
    gbr = gpad[:, taps - 1:].at[:, toks - (taps - 1):].add(edge).reshape(-1, chans).astype(BF)
    g_gate = mm_lt(normed, ggate)
    g_input = mm_lt(normed, gbr)
    gn1 = rs(mm_rt(ggate, wg) + mm_rt(gbr, wi))
    gi_norm, gain1 = rms_back(x, s1, gain_one, gn1)
    grad_input = grad_middle + gi_norm

    chan = jnp.concatenate([gcw, gcb[None], grb[None], gib[None], gdp[None]], 0)
    per = chans // n_seq
    chan = chan.reshape(8, n_seq, per).transpose(1, 0, 2).reshape(n_seq, 8 * per)
    blk = jnp.zeros((n_fs, n_seq, 8 * per), F32).at[fi].set(chan).reshape(n_fs * n_seq, 8 * per)
    gw = jnp.stack([gain1, gain2]).reshape(2, n_fs * n_seq, -1).transpose(1, 0, 2).reshape(n_fs * n_seq, -1)
    small = lax.psum_scatter(jnp.concatenate([blk, gw], 1), BOTH, scatter_dimension=0, tiled=True)[0]
    ch = small[: 8 * per].reshape(8, per)
    gn = small[8 * per:].reshape(2, -1)
    og = grads_rows(jnp.concatenate([g_out, gwr, gwi], 1))
    return (
        result.reshape(block_input.shape), grad_input.reshape(block_input.shape), gn[0],
        grads_cols(g_gate), grads_cols(g_input), ch[:4], ch[4], og[:, width: width + hb], ch[5],
        og[:, width + hb:], ch[6], ch[7], og[:, :width], gn[1], grads_cols(g_up), grads_cols(g_value), grads_rows(g_down),
    )


def solution(mesh):
    rowsh, vec, mat = P("fsdp", "seq", None), P("fsdp"), P("fsdp", None)
    ov, om = P(BOTH), P(BOTH, None)
    return jax.shard_map(
        body,
        mesh=mesh,
        in_specs=(rowsh, rowsh, P(), vec, mat, mat, P(None, "fsdp"), vec, mat, vec, mat, vec, vec, mat, vec, mat, mat, mat),
        out_specs=(rowsh, rowsh, ov, om, om, P(None, BOTH), ov, om, ov, om, ov, ov, om, ov, om, om, om),
        check_vma=False,
    )
```

```python
import jax
import jax.numpy as jnp
from jax import lax
from jax.sharding import PartitionSpec as P
from jax.experimental import pallas as pl
from jax.experimental.pallas import tpu as pltpu

EPS_NORM = 1e-06
EPS_MULT = 0.0001
RATE_SCALE = 8.0
BF = jnp.bfloat16
F32 = jnp.float32
GROUP = "fsdp"
BOTH = ("seq", "fsdp")


def mm(left, right):
    return jnp.dot(left, right, preferred_element_type=F32)


def mm_lt(left, right):
    return lax.dot_general(left, right, (((0,), (0,)), ((), ())), preferred_element_type=F32)


def mm_rt(left, right):
    return lax.dot_general(left, right, (((1,), (1,)), ((), ())), preferred_element_type=F32)


def gelu_pair(v):
    c = 0.7978845608028654
    a = 0.044715
    u = c * (v + a * v * v * v)
    t = jnp.tanh(u)
    g = 0.5 * v * (1.0 + t)
    d = 0.5 * (1.0 + t) + 0.5 * v * (1.0 - t * t) * c * (1.0 + 3.0 * a * v * v)
    return g, d


def linear_step(first_pair, second_pair):
    return (first_pair[0] * second_pair[0], second_pair[1] + second_pair[0] * first_pair[1])


def rms(v, g):
    s = lax.rsqrt(jnp.mean(v * v, axis=-1, keepdims=True) + EPS_NORM)
    return (v * s * g).astype(BF), s


def rms_back(v, s, g, grad):
    gg = grad * g
    gain = jnp.sum(grad * v * s, axis=0)
    return s * gg - v * (s * s * s) * jnp.mean(gg * v, axis=-1, keepdims=True), gain


def ag(a):
    return lax.all_gather(a, GROUP, axis=0, tiled=True)


def rs(a):
    return lax.psum_scatter(a.astype(BF), GROUP, scatter_dimension=0, tiled=True).astype(F32)


def grads_cols(g):
    part = lax.psum_scatter(g.astype(BF), "seq", scatter_dimension=0, tiled=True)
    return lax.all_to_all(part, GROUP, split_axis=0, concat_axis=1, tiled=True).astype(F32)


def grads_rows(g):
    n, m = lax.axis_size("seq"), lax.axis_size(GROUP)
    part = lax.psum_scatter(g.astype(BF), "seq", scatter_dimension=0, tiled=True)
    pairs = [(j * m + f, f * n + j) for j in range(n) for f in range(m)]
    return lax.ppermute(part, BOTH, pairs).astype(F32)


def shifted(shard, axis, by):
    length = lax.axis_size(axis)
    pairs = [(i, i + by) for i in range(length) if 0 <= i + by < length]
    return lax.ppermute(shard, axis, pairs)


MESH = pl.DeviceIdType.MESH
VMEM = pl.BlockSpec(memory_space=pltpu.VMEM)
ANY = pl.BlockSpec(memory_space=pl.ANY)
LIMIT = 63 * 2**20


def ds(start, size):
    if not isinstance(start, int):
        start = pl.multiple_of(start, size if size % 128 else 128)
    return pl.ds(start, size)


def rows_at(block, size):
    return pl.ds(pl.multiple_of(block * size, size), size)


class Place:
    def __init__(self):
        self.n = lax.axis_size("seq")
        self.s, self.f = lax.axis_index("seq"), lax.axis_index("fsdp")
        f = self.f
        self.p1 = f + 1 - 2 * lax.rem(f, 2)
        self.p2 = lax.rem(f + 2, 4)
        self.p3 = lax.rem(self.p1 + 2, 4)
        self.sx = self.s + 1 - 2 * lax.rem(self.s, 2)

    def group(self, f):
        return (self.s, f)

    def line(self, s):
        return (s, self.f)

    def greet(self, hop=None):
        barrier = pltpu.get_barrier_semaphore()
        for f in (self.p1, self.p2, self.p3):
            pl.semaphore_signal(barrier, inc=1, device_id=self.group(f), device_id_type=MESH)

        def one(j, _):
            pl.semaphore_signal(
                barrier, inc=1, device_id=self.line(lax.rem(self.s + j, self.n)), device_id_type=MESH
            )
            return 0

        lax.fori_loop(1, self.n, one, 0)
        pl.semaphore_wait(barrier, 3 + self.n - 1 + (0 if hop is None else hop.greet(barrier)))


class Sems:
    def __init__(self, ref):
        self.ref, self.used = ref, 0

    def take(self):
        self.used += 1
        return self.ref.at[self.used - 1]

    def remote(self, src, dst, device):
        return pltpu.make_async_remote_copy(
            src_ref=src, dst_ref=dst, send_sem=self.take(), recv_sem=self.take(),
            device_id=device, device_id_type=MESH,
        )

    def local(self, src, dst):
        copy = pltpu.make_async_copy(src, dst, self.take())
        copy.start()
        return copy


class Gather:
    def __init__(self, at, sems, buf, chunk):
        self.at, self.buf, self.chunk = at, buf, chunk
        mine = lambda f, r: buf.at[rows_at(f * 2 + r, chunk)]
        self.core = [sems.remote(mine(at.f, r), mine(at.f, r), at.group(at.p1)) for r in range(2)]
        self.over = [sems.remote(mine(at.f, r), mine(at.f, r), at.group(at.p2)) for r in range(2)]
        self.pass_on = [sems.remote(mine(at.p2, r), mine(at.p2, r), at.group(at.p1)) for r in range(2)]

    def send(self, r):
        self.over[r].start()
        self.core[r].start()

    def relay(self, r):
        self.over[r].wait_recv()
        self.pass_on[r].start()

    def near(self):
        for r in range(2):
            self.core[r].wait_recv()

    def finish(self):
        for r in range(2):
            self.core[r].wait_send()
            self.over[r].wait_send()
            self.pass_on[r].wait()


class Scatter:
    def __init__(self, at, sems, core_out, core_in, over_out, over_in, chunk):
        self.at, self.chunk = at, chunk
        self.core_out, self.core_in, self.over_out, self.over_in = core_out, core_in, over_out, over_in
        self.core = [sems.remote(core_out.at[k], core_in.at[k], at.group(at.p1)) for k in range(2)]
        self.over = [
            sems.remote(
                over_out.at[pl.ds(r * chunk, chunk)], over_in.at[pl.ds(r * chunk, chunk)], at.group(at.p2)
            )
            for r in range(2)
        ]

    def run(self, partial, own, between=lambda k: None):
        at = self.at

        def put(ref):
            def store(sl, cols, tile):
                ref[sl, cols] = tile.astype(BF)

            return store

        partial(at.p3, put(self.core_out.at[0]))
        self.core[0].start()
        between(0)

        def add_over(sl, cols, tile):
            self.over_out[sl, cols] = (tile + self.core_in[0, sl, cols].astype(F32)).astype(BF)

        self.core[0].wait_recv()
        partial(at.p2, add_over)
        self.over[0].start()
        between(1)
        partial(at.p1, put(self.core_out.at[1]))
        self.core[1].start()
        between(2)
        self.core[1].wait_recv()

        def add_own(sl, cols, tile):
            own[sl, cols] = own[sl, cols] + tile + self.core_in[1, sl, cols].astype(F32)

        partial(at.f, add_own)
        between(3)

    def run_tile(self, compute, tile, own, between=lambda k: None):
        at = self.at

        def one(k, _):
            compute(jnp.where(k == 0, at.p3, jnp.where(k == 1, at.p2, jnp.where(k == 2, at.p1, at.f))))

            @pl.when(k == 0)
            def _():
                self.core_out[0] = tile[...].astype(BF)
                self.core[0].start()

            @pl.when(k == 1)
            def _():
                self.core[0].wait_recv()
                for r in range(2):
                    sl = pl.ds(r * self.chunk, self.chunk)
                    self.over_out[sl, :] = (tile[sl, :] + self.core_in[0, sl, :].astype(F32)).astype(BF)
                self.over[0].start()

            @pl.when(k == 2)
            def _():
                self.core_out[1] = tile[...].astype(BF)
                self.core[1].start()

            @pl.when(k == 3)
            def _():
                self.core[1].wait_recv()
                if own is None:
                    tile[...] = tile[...] + self.core_in[1].astype(F32)
                else:
                    own[...] = own[...] + tile[...] + self.core_in[1].astype(F32)

            between(k)
            return 0

        lax.fori_loop(0, 4, one, 0)

    def second(self):
        self.over[0].wait_send()
        self.over[1].start()

    def arrived(self, r):
        self.over[r].wait_recv()
        return self.over_in[pl.ds(r * self.chunk, self.chunk), :].astype(F32)

    def finish(self):
        for copy in self.core + self.over[1:]:
            copy.wait_send()


class Columns:
    def __init__(self, at, sems, weights, buf, with_own=True):
        rows, width = weights[0].shape
        part = width // 4
        cut = rows // 4
        h = lax.rem(at.s, 4)
        one = h + 1 - 2 * lax.rem(h, 2)
        mates = [at.line(at.s - h + m) for m in (one, lax.rem(h + 2, 4), lax.rem(one + 2, 4))]
        self.near, self.own, self.far, self.side = [], [], [], []
        for k, w in enumerate(weights):
            cols = pl.ds(k * part, part)
            take = lambda f: pl.ds(pl.multiple_of(f * part, 128), part)
            mine = pl.ds(pl.multiple_of(at.f * rows, rows), rows)
            quarter = pl.ds(pl.multiple_of(h * cut, cut), cut)
            mine_cut = pl.ds(pl.multiple_of(at.f * rows + h * cut, cut), cut)
            if with_own:
                self.own.append(pltpu.make_async_copy(w.at[:, take(at.f)], buf.at[mine, cols], sems.take()))
            self.near.append(sems.remote(w.at[:, take(at.p1)], buf.at[mine, cols], at.group(at.p1)))
            for p in (at.p2, at.p3):
                self.far.append(sems.remote(w.at[quarter, take(p)], buf.at[mine_cut, cols], at.group(p)))
                came = buf.at[pl.ds(pl.multiple_of(p * rows + h * cut, cut), cut), cols]
                self.side.append([sems.remote(came, came, mate) for mate in mates])

    def start_far(self):
        for c in self.far:
            c.start()

    def start_near(self):
        for c in self.near + self.own:
            c.start()

    def relay(self, k):
        self.far[k].wait_recv()
        for c in self.side[k]:
            c.start()

    def finish(self):
        for c in self.own + self.near + sum(self.side, []):
            c.wait()
        for c in self.far:
            c.wait_send()


def expm1_neg(v):
    series = v * (1 + v * (1 / 2) * (1 + v * (1 / 3) * (1 + v * (1 / 4) * (1 + v * (1 / 5) * (1 + v * (1 / 6))))))
    return jnp.where(v > -0.25, series, jnp.exp(v) - 1.0)


def decay_rows(param):
    small = jnp.exp(-jnp.abs(param))
    return (
        -RATE_SCALE * (jnp.maximum(-param, 0.0) + jnp.log1p(small)),
        RATE_SCALE * jnp.where(param > 0.0, small, 1.0) / (1.0 + small),
    )


def whole_gain(gain, row):
    return jnp.concatenate([gain[p, row : row + 1, :] for p in range(4)], axis=1)


def swap_rows(src, dst, outer, kind):
    total, width = src.shape
    inner = total // outer

    def one(c, _):
        cols = pl.ds(pl.multiple_of(c * 128, 128), 128)
        v = src[:, cols].reshape(outer, inner, 128)
        dst[:, cols] = jnp.swapaxes(v, 0, 1).reshape(total, 128).astype(kind)
        return 0

    lax.fori_loop(0, width // 128, one, 0)


def forward_branch(x, gain_one, gain_two, taps_w, conv_b, rate_b, inlet_b, decay_p, wr, wl, wo, wg, wi, wu, wv,
                   wgi_o, wuv_o, normed_o, n2_o, middle_o, gate_o, pad_o, conv_o, rate_o, inlet_o, decay_o, states_o,
                   merged_o, ends_o, gain_o, chan_o,
                   wgi, normed, n2, middle, gains, chan, gain, gate, pad, conv, rate, inlet, decay, states, work, merged, ends,
                   tot, core_out, core_in, over_out, over_in, sem, tsend, trecv):
    at = Place()
    here, width = x.shape
    toks = here // 2
    chans = chan.shape[1]
    part = width // 4
    taps = 4
    steps = toks
    group = 8
    halo = (taps - 1) * group
    sems = Sems(sem)
    chan[0:taps, :] = taps_w[...].astype(F32)
    for row, v in enumerate((conv_b, rate_b, inlet_b, decay_p)):
        chan[taps + row : taps + row + 1, :] = v[...].astype(F32).reshape(1, chans)
    for row, v in enumerate((gain_one, gain_two)):
        gains[row : row + 1, :] = v[...].astype(F32).reshape(1, part)
    gains[2:8, :] = jnp.zeros((6, part), F32)
    at.greet()

    shares = [
        sems.remote(gains, gain.at[at.f], at.group(p)) for p in (at.p1, at.p2, at.p3)
    ]
    for c in shares:
        c.start()
    gain[at.f] = gains[...]
    gi = Columns(at, sems, [wg, wi], wgi)
    gi.start_far()
    gi.start_near()
    uv = Columns(at, sems, [wu, wv], wuv_o, False)
    uv.start_near()
    ag1 = Gather(at, sems, normed, toks)
    for c in shares:
        c.wait()
    for r in range(2):
        sl = pl.ds(r * toks, toks)
        v = x[sl, :]
        scale = lax.rsqrt(jnp.mean(v * v, axis=-1, keepdims=True) + EPS_NORM)
        for p in range(4):
            cols = pl.ds(p * part, part)
            normed[rows_at(at.f * 2 + r, toks), cols] = (x[sl, cols] * scale * gain[p, 0:1, :]).astype(BF)
        ag1.send(r)
    for k in range(4):
        gi.relay(k)
    ag1.relay(0)
    uv.start_far()
    ag1.relay(1)
    ag1.near()
    ag1.finish()
    gi.finish()
    saves = [sems.local(normed, normed_o), sems.local(wgi, wgi_o), sems.local(gain, gain_o), sems.local(chan, chan_o)]

    def branch_rows(m, _):
        sl = rows_at(m, here)
        work[sl, :] = mm(normed[sl, :], wgi[:, chans:]).astype(BF).astype(F32)
        return 0

    lax.fori_loop(0, 4, branch_rows, 0)
    swap_rows(work, pad.at[pl.ds(halo, steps * group)], group, F32)
    edge = pad.at[pl.ds(steps * group, halo)]
    next_one = lax.rem(at.s + 1, at.n)
    tail = sems.remote(edge, pad.at[pl.ds(0, halo)], at.line(next_one))

    @pl.when(at.s < at.n - 1)
    def _():
        tail.start()

    @pl.when(at.s == 0)
    def _():
        pad[0:halo, :] = jnp.zeros((halo, chans), F32)

    def gate_rows(m, _):
        sl = rows_at(m, here)
        work[sl, :] = mm(normed[sl, :], wgi[:, :chans])
        return 0

    lax.fori_loop(0, 4, gate_rows, 0)
    swap_rows(work, gate, group, F32)

    @pl.when(at.s > 0)
    def _():
        tail.wait_recv()

    @pl.when(at.s < at.n - 1)
    def _():
        tail.wait_send()


    ends[16:17, :] = decay_rows(chan[7:8, :])[0]

    def gates(b, _):
        for h in range(chans // 128):
            cols = pl.ds(h * 128, 128)
            size = 128
            start = pl.multiple_of(b * size, size)
            sl = pl.ds(start, size)
            total = chan[taps : taps + 1, cols]
            for k in range(taps):
                total = total + chan[k : k + 1, cols] * pad[pl.ds(start + (halo - group * k), size), cols]
            low = total.astype(BF)
            blocks = pl.ds(h * 128, 128)
            r = jax.nn.sigmoid(mm(low, wr[blocks, :]) + chan[5:6, cols])
            i = jax.nn.sigmoid(mm(low, wl[blocks, :]) + chan[6:7, cols])
            ld = r * ends[16:17, cols]
            conv[sl, cols] = low
            low = low.astype(F32)
            decay[sl, cols] = jnp.exp(ld)
            work[sl, cols] = jnp.sqrt(EPS_MULT - expm1_neg(2.0 * ld)) * i * low
            rate[sl, cols] = r
            inlet[sl, cols] = i
        return 0

    lax.fori_loop(0, steps * group // 128, gates, 0)
    saves += [
        sems.local(gate, gate_o), sems.local(pad, pad_o), sems.local(conv, conv_o), sems.local(rate, rate_o),
        sems.local(inlet, inlet_o), sems.local(decay, decay_o),
    ]

    unroll = 8

    def totals(b, carry):
        h, p = carry
        for u in range(unroll):
            sl = pl.ds(pl.multiple_of((b * unroll + u) * group, group), group)
            a = decay[sl, :]
            h = a * h + work[sl, :]
            p = p * a
        return h, p

    zero = jnp.zeros((group, chans), F32)
    h, p = lax.fori_loop(0, steps // unroll, totals, (zero, zero + 1.0))
    ends[0:8, :] = p
    ends[8:16, :] = h

    def total_copy(src, to):
        return pltpu.make_async_remote_copy(
            src_ref=ends.at[pl.ds(0, 16)], dst_ref=tot.at[src], send_sem=tsend.at[to], recv_sem=trecv.at[src],
            device_id=at.line(to), device_id_type=MESH,
        )

    def send_total(j, _):
        total_copy(at.s, j).start()
        return 0

    lax.fori_loop(at.s + 1, at.n, send_total, 0)

    def enter(j, state):
        total_copy(j, j).wait_recv()
        return tot[j, 0:8, :] * state + tot[j, 8:16, :]

    state_in = lax.fori_loop(0, at.s, enter, zero)

    def sent_total(j, _):
        total_copy(at.s, j).wait_send()
        return 0

    lax.fori_loop(at.s + 1, at.n, sent_total, 0)
    ends[16:24, :] = state_in

    def scan(b, h):
        for u in range(unroll):
            sl = pl.ds(pl.multiple_of((b * unroll + u) * group, group), group)
            h = decay[sl, :] * h + work[sl, :]
            states[sl, :] = h
        return h

    lax.fori_loop(0, steps // unroll, scan, state_in)
    saves += [sems.local(states, states_o), sems.local(ends, ends_o)]

    def merge(c, _):
        cols = pl.ds(pl.multiple_of(c * 128, 128), 128)

        def some(b, _):
            sl = rows_at(b, 128)
            work[sl, cols] = states[sl, cols] * gelu_pair(gate[sl, cols])[0]
            return 0

        lax.fori_loop(0, steps * group // 128, some, 0)
        return 0

    lax.fori_loop(0, chans // 128, merge, 0)
    swap_rows(work, merged, steps, BF)
    saves += [sems.local(merged, merged_o)]

    middle[...] = x[...]
    sc = Scatter(at, sems, core_out, core_in, over_out, over_in, toks)

    def partial(o, store):
        def half(r, _):
            sl = rows_at(r, toks)
            tile = mm(merged[rows_at(o * 2 + r, toks), :], wo[...])
            store(sl, slice(None), tile)
            return 0

        lax.fori_loop(0, 2, half, 0)

    def between(k):
        if k >= 2:
            uv.relay(2 * k - 4)
            uv.relay(2 * k - 3)

    sc.run(partial, middle, between)
    sc.second()
    ag2 = Gather(at, sems, n2, toks)
    for r in range(2):
        sl = pl.ds(r * toks, toks)
        v = middle[sl, :] + sc.arrived(r)
        middle[sl, :] = v
        scale = lax.rsqrt(jnp.mean(v * v, axis=-1, keepdims=True) + EPS_NORM)
        for p in range(4):
            cols = pl.ds(p * part, part)
            n2[rows_at(at.f * 2 + r, toks), cols] = (middle[sl, cols] * scale * gain[p, 1:2, :]).astype(BF)
        ag2.send(r)
    saves += [sems.local(middle, middle_o)]
    for r in range(2):
        ag2.relay(r)
    ag2.near()
    ag2.finish()
    sc.finish()
    saves += [sems.local(n2, n2_o)]
    uv.finish()
    for c in saves:
        c.wait()


def call_forward(x, gain_one, gain_two, taps_w, conv_b, rate_b, inlet_b, decay_p, wr, wl, wo, wg, wi, wu, wv):
    here, width = x.shape
    chans = taps_w.shape[1]
    ffl = wu.shape[1] // 4
    every = here * 4
    n = lax.axis_size("seq")
    f32 = lambda *s: jax.ShapeDtypeStruct(s, F32)
    bf = lambda *s: jax.ShapeDtypeStruct(s, BF)
    vf = lambda *s: pltpu.VMEM(s, F32)
    vb = lambda *s: pltpu.VMEM(s, BF)
    outs = [
        bf(width, 2 * chans), bf(width, 2 * ffl), bf(every, width), bf(every, width), f32(here, width),
        f32(every, chans), f32(every + 24, chans), bf(every, chans), f32(every, chans), f32(every, chans),
        f32(every, chans), f32(every, chans), bf(every, chans), f32(24, chans), f32(4, 8, width // 4), f32(8, chans),
    ]
    scratch = [
        vb(width, 2 * chans), vb(every, width), vb(every, width), vf(here, width), vf(8, width // 4), vf(8, chans), vf(4, 8, width // 4),
        vf(every, chans), vf(every + 24, chans), vb(every, chans), vf(every, chans), vf(every, chans),
        vf(every, chans), vf(every, chans), vf(every, chans), vb(every, chans), vf(24, chans),
        vf(n, 16, chans), vb(2, here, width), vb(2, here, width), vb(here, width), vb(here, width),
        pltpu.SemaphoreType.DMA((170,)), pltpu.SemaphoreType.DMA((n,)), pltpu.SemaphoreType.DMA((n,)),
    ]
    return pl.pallas_call(
        forward_branch,
        out_shape=outs,
        in_specs=[VMEM] * 11 + [ANY] * 4,
        out_specs=[ANY] * len(outs),
        scratch_shapes=scratch,
        compiler_params=pltpu.CompilerParams(collective_id=1, has_side_effects=True, vmem_limit_bytes=LIMIT),
        name="forward_branch",
    )(x, gain_one, gain_two, taps_w, conv_b, rate_b, inlet_b, decay_p, wr, wl, wo, wg, wi, wu, wv)


class Hop:
    def __init__(self, at):
        b = at.f * at.n + at.s
        self.to = (lax.div(b, 4), lax.rem(b, 4))
        c = at.s * 4 + at.f
        self.source = (lax.rem(c, at.n), lax.div(c, at.n))
        self.stays = b == c

    def greet(self, barrier):
        @pl.when(jnp.logical_not(self.stays))
        def _():
            for device in (self.to, self.source):
                pl.semaphore_signal(barrier, inc=1, device_id=device, device_id_type=MESH)

        return jnp.where(self.stays, 0, 2)

    def start(self, sems, src, dst):
        far = sems.remote(src, dst, self.to)
        near = pltpu.make_async_copy(src, dst, sems.take())

        @pl.when(self.stays)
        def _():
            near.start()

        @pl.when(jnp.logical_not(self.stays))
        def _():
            far.start()

        return near, far

    def wait(self, pair):
        near, far = pair

        @pl.when(self.stays)
        def _():
            near.wait()

        @pl.when(jnp.logical_not(self.stays))
        def _():
            far.wait()


class Ring:
    def __init__(self, at, grads, slots, send, recv, by_rows):
        self.at, self.grads, self.slots, self.sem, self.rem = at, grads, slots, send, recv
        n = at.n
        self.q = self.place(at.s)
        rows, width = slots.shape[1:]
        self.rows = rows
        if by_rows:
            self.cut = [(pl.ds(i * rows // 4, rows // 4), pl.ds(0, width)) for i in range(4)]
        else:
            self.cut = [(pl.ds(0, rows), pl.ds(i * width // 4, width // 4)) for i in range(4)]
        self.way = (1, -1, 1, -1)
        self.to = {w: at.line(self.owner(lax.rem(self.q + w + n, n))) for w in (1, -1)}

    def place(self, s):
        half = lax.div(s, 2)
        return jnp.where(lax.rem(s, 2) == 0, half, self.at.n - 1 - half)

    def owner(self, q):
        n = self.at.n
        return jnp.where(q < n // 2, 2 * q, 2 * (n - 1 - q) + 1)

    def block(self, i, behind):
        n = self.at.n
        s = self.owner(lax.rem(self.q - self.way[i] * behind + 2 * n, n))
        r, c = self.cut[i]
        return self.grads.at[pl.ds(pl.multiple_of(s * self.rows + r.start, 16), r.size), c]

    def copy(self, i, k, src):
        r, c = self.cut[i]
        return pltpu.make_async_remote_copy(
            src_ref=src, dst_ref=self.slots.at[k, r, c], send_sem=self.sem.at[i, k], recv_sem=self.rem.at[i, k],
            device_id=self.to[self.way[i]], device_id_type=MESH,
        )

    def start(self):
        for i in range(4):
            self.copy(i, 0, self.block(i, 1)).start()

    def summed(self, i, k):
        r, c = self.cut[i]
        slot = self.slots.at[k, r, c]
        self.copy(i, k, slot).wait_recv()
        return slot, slot[...].astype(F32) + self.block(i, k + 2)[...].astype(F32)

    def step(self, k):
        for i in range(4):
            slot, value = self.summed(i, k)
            slot[...] = value.astype(BF)
            self.copy(i, k + 1, slot).start()

    def last(self, out, after=lambda i: None):
        k = self.at.n - 2
        for i in range(4):
            _, value = self.summed(i, k)
            out[self.cut[i]] = value.astype(out.dtype)
            after(i)

    def finish(self):
        def one(k, _):
            for i in range(4):
                r, c = self.cut[i]
                self.copy(i, k, self.slots.at[k, r, c]).wait_send()
            return 0

        lax.fori_loop(0, self.at.n - 1, one, 0)


class Regroup:
    def __init__(self, at, sems, src, dst):
        size = src.shape[0] // at.n
        self.far, self.near = [], []
        for h in range(at.n // 4):
            slot = dst.at[pl.ds(pl.multiple_of((at.f * (at.n // 4) + h) * size, 16), size)]
            block = lambda p: src.at[pl.ds(pl.multiple_of((p + 4 * h) * size, 16), size)]
            for p in (at.p2, at.p3, at.p1):
                self.far.append(sems.remote(block(p), slot, at.group(p)))
            self.near.append(pltpu.make_async_copy(block(at.f), slot, sems.take()))

    def start(self):
        for c in self.far + self.near:
            c.start()

    def wait(self):
        for c in self.far + self.near:
            c.wait()


class Spread:
    def __init__(self, at, sems, src, came):
        self.at, self.src, self.came = at, src, came
        rows = came.shape[1]
        send, recv = [sems.take() for _ in range(4)], [sems.take() for _ in range(4)]
        self.copies = []
        for k in range(1, 4):
            to = lax.rem(at.f + k, 4)
            piece = src.at[pl.ds(pl.multiple_of(to * rows, 16), rows)]
            self.copies.append(
                pltpu.make_async_remote_copy(
                    src_ref=piece, dst_ref=came.at[at.f], send_sem=send[k], recv_sem=recv[k],
                    device_id=at.group(to), device_id_type=MESH,
                )
            )

    def start(self):
        rows = self.came.shape[1]
        for c in self.copies:
            c.start()
        self.came[self.at.f] = self.src[pl.ds(pl.multiple_of(self.at.f * rows, 16), rows), :]

    def wait(self):
        for c in self.copies:
            c.wait()


def mlp(n2_h, wuv_h, wu_h, wv_h, wd_h, middle_h, teacher_h, lengths, gain,
        result_o, gmid_o, gml_o, gain_o, down_o, up_o, value_o,
        n2, wuv, wd, hidden, ge, gdi, gml, middle, own, gout, tile, core_out, core_in, over_out, over_in,
        gwd, gwu, gwv, slots_u, last_u, gain_acc, sem, ring_sem):
    at = Place()
    sems = Sems(sem)
    here, width = middle.shape
    toks = here // 2
    ffl = hidden.shape[1]
    part = width // 4
    col = 384
    loads = [sems.local(n2_h, n2)]
    mine = pl.ds(pl.multiple_of(at.f * part, part), part)
    for k, w in enumerate((wu_h, wv_h)):
        cols = pl.ds(pl.multiple_of(at.f * ffl, 128), ffl)
        loads.append(sems.local(w.at[:, cols], wuv.at[mine, pl.ds(k * ffl, ffl)]))
    for p in (at.p1, at.p2, at.p3):
        rows = pl.ds(pl.multiple_of(p * part, part), part)
        loads.append(sems.local(wuv_h.at[rows], wuv.at[rows]))
    loads.append(sems.local(wd_h, wd))
    loads2 = [sems.local(middle_h, middle), sems.local(middle_h, own), sems.local(teacher_h, gout)]
    at.greet()
    for c in loads + loads2:
        c.wait()

    def forward(o):
        sl = rows_at(o, here)

        def some(c, _):
            cols = pl.ds(pl.multiple_of(c * col, 128), col)
            cols2 = pl.ds(pl.multiple_of(c * col + ffl, 128), col)
            up = mm(n2[sl, :], wuv[:, cols])
            g, d = gelu_pair(mm(n2[sl, :], wuv[:, cols2]))
            hidden[sl, cols] = (g * up).astype(BF)
            ge[sl, cols] = g.astype(BF)
            ge[sl, cols2] = (up * d).astype(BF)
            return 0

        lax.fori_loop(0, ffl // col, some, 0)

        def out(c, _):
            cols = pl.ds(pl.multiple_of(c * 512, 128), 512)
            tile[:, cols] = mm(hidden[sl, :], wd[:, cols])
            return 0

        lax.fori_loop(0, width // 512, out, 0)

    def hidden_rows(o):
        sl = rows_at(o, here)

        def some(c, _):
            cols = pl.ds(pl.multiple_of(c * col, 128), col)
            cols2 = pl.ds(pl.multiple_of(c * col + ffl, 128), col)
            gh = mm_rt(gdi[sl, :], wd[cols, :])
            ge[sl, cols] = (gh * ge[sl, cols].astype(F32)).astype(BF)
            ge[sl, cols2] = (gh * ge[sl, cols2].astype(F32)).astype(BF)
            return 0

        lax.fori_loop(0, ffl // col, some, 0)
        return 0

    sc = Scatter(at, sems, core_out, core_in, over_out, over_in, toks)
    sc.run_tile(forward, tile, own)
    sc.second()
    count = lengths[0]
    for j in range(1, lengths.shape[0]):
        count = count + lengths[j]
    weight = (lengths.shape[0] * toks * at.n) / jnp.full((1, 1), count, jnp.int32).astype(F32)
    place = at.s * toks + lax.broadcasted_iota(jnp.int32, (toks, 1), 0)
    ag = Gather(at, sems, gdi, toks)
    for r in range(2):
        sl = pl.ds(r * toks, toks)
        v = own[sl, :] + sc.arrived(r)
        own[sl, :] = v
        v = jnp.where(place < lengths[at.f * 2 + r], v - gout[sl, :], 0.0) * weight
        gout[sl, :] = v
        gdi[rows_at(at.f * 2 + r, toks), :] = v.astype(BF)
        ag.send(r)
    saves = [sems.local(own, result_o)]
    ag.near()
    lax.fori_loop(0, 2, lambda k, _: hidden_rows(jnp.where(k == 0, at.f, at.p1)), 0)
    for r in range(2):
        ag.relay(r)
    ag.finish()
    sc.finish()
    saves.pop().wait()

    def down_rows(m, _):
        cols = pl.ds(pl.multiple_of(m * 128, 128), 128)
        gwd[rows_at(m, 128), :] = mm_lt(hidden[:, cols], gdi[...]).astype(BF)
        return 0

    def weight_rows(grads, first):
        def one(m, _):
            cols = pl.ds(pl.multiple_of(m * 256, 256), 256)
            grads[rows_at(m, 256), :] = mm_lt(n2[:, cols], ge[:, first : first + ffl]).astype(BF)
            return 0

        return one

    def backward(o):
        sl = rows_at(o, here)

        def out(c, _):
            cols = pl.ds(pl.multiple_of(c * 512, 128), 512)
            tile[:, cols] = mm_rt(ge[sl, :], wuv[cols, :])
            return 0

        lax.fori_loop(0, width // 512, out, 0)

    ring_u = Ring(at, gwu, slots_u, ring_sem.at[0], ring_sem.at[1], True)
    six = width // 256
    lax.fori_loop(0, 2, lambda k, _: hidden_rows(jnp.where(k == 0, at.p2, at.p3)), 0)
    lax.fori_loop(0, six, weight_rows(gwu, 0), 0)
    ring_u.start()
    sc2 = Scatter(at, sems, core_out, core_in, over_out, over_in, toks)

    def between(k):
        @pl.when(k >= 2)
        def _():
            ring_u.step(k - 2)

    sc2.run_tile(backward, tile, None, between)
    sc2.second()
    lax.fori_loop(0, six, weight_rows(gwv, ffl), 0)
    ring_u.step(2)
    lax.fori_loop(0, ffl // 128, down_rows, 0)
    ring_u.step(3)
    saves += [sems.local(gwv, value_o), sems.local(gwd, down_o)]
    ag2 = Gather(at, sems, gml, toks)
    acc = jnp.zeros((1, width), F32)
    for r in range(2):
        sl = pl.ds(r * toks, toks)
        g = tile[sl, :] + sc2.arrived(r)
        v = middle[sl, :]
        s = lax.rsqrt(jnp.mean(v * v, axis=-1, keepdims=True) + EPS_NORM)
        acc = acc + jnp.sum(g * v * s, axis=0, keepdims=True)
        gg = g * whole_gain(gain, 1)
        mean = jnp.mean(gg * v, axis=-1, keepdims=True)
        new = gout[sl, :] + s * gg - v * (s * s * s * mean)
        own[sl, :] = new
        gml[rows_at(at.f * 2 + r, toks), :] = new.astype(BF)
        ag2.send(r)
    gain_acc[...] = jnp.broadcast_to(acc, gain_acc.shape)
    saves += [sems.local(own, gmid_o), sems.local(gain_acc, gain_o)]
    ring_u.step(4)
    ag2.relay(0)
    ring_u.step(5)
    ag2.relay(1)
    ring_u.last(last_u)
    saves += [sems.local(last_u, up_o)]
    ag2.near()
    ag2.finish()
    sc2.finish()
    saves += [sems.local(gml, gml_o)]
    ring_u.finish()
    for c in saves:
        c.wait()


def call_mlp(n2, wuv, wu, wv, wd, middle, teacher, lengths, gain):
    every, width = n2.shape
    here = middle.shape[0]
    ffl = wd.shape[0]
    n = lax.axis_size("seq")
    f32 = lambda *s: jax.ShapeDtypeStruct(s, F32)
    bf = lambda *s: jax.ShapeDtypeStruct(s, BF)
    vf = lambda *s: pltpu.VMEM(s, F32)
    vb = lambda *s: pltpu.VMEM(s, BF)
    outs = [
        f32(here, width), f32(here, width), bf(every, width), f32(8, width), bf(ffl, width),
        bf(width // n, ffl), bf(width, ffl),
    ]
    scratch = [
        vb(every, width), vb(width, 2 * ffl), vb(ffl, width), vb(every, ffl), vb(every, 2 * ffl), vb(every, width),
        vb(every, width), vf(here, width), vf(here, width), vf(here, width), vf(here, width),
        vb(2, here, width), vb(2, here, width), vb(here, width), vb(here, width),
        vb(ffl, width), vb(width, ffl), vb(width, ffl), vb(n - 1, width // n, ffl),
        vb(width // n, ffl), vf(8, width),
        pltpu.SemaphoreType.DMA((100,)), pltpu.SemaphoreType.DMA((2, 4, n - 1)),
    ]
    return pl.pallas_call(
        mlp,
        out_shape=outs,
        in_specs=[ANY] * 7 + [pl.BlockSpec(memory_space=pltpu.SMEM), VMEM],
        out_specs=[ANY] * len(outs),
        scratch_shapes=scratch,
        compiler_params=pltpu.CompilerParams(collective_id=2, has_side_effects=True, vmem_limit_bytes=LIMIT),
        name="mlp",
    )(n2, wuv, wu, wv, wd, middle, teacher, lengths, gain)


class Line:
    def __init__(self, at, src, tot, send, recv):
        self.at, self.src, self.tot, self.send_sem, self.recv_sem = at, src, tot, send, recv

    def copy(self, slot, to):
        return pltpu.make_async_remote_copy(
            src_ref=self.src, dst_ref=self.tot.at[slot], send_sem=self.send_sem.at[to], recv_sem=self.recv_sem.at[slot],
            device_id=self.at.line(to), device_id_type=MESH,
        )

    def send(self, first, end):
        def one(j, _):
            @pl.when(j != self.at.s)
            def _():
                self.copy(self.at.s, j).start()

            return 0

        lax.fori_loop(first, end, one, 0)

    def sent(self, first, end):
        def one(j, _):
            @pl.when(j != self.at.s)
            def _():
                self.copy(self.at.s, j).wait_send()

            return 0

        lax.fori_loop(first, end, one, 0)

    def wait(self, j):
        self.copy(j, j).wait_recv()


def branch_back(chan, wr, wl, gain, gain2,
                gml_h, merged_h, wo_h, wgi_h, normed_h, gate_h, pad_h, conv_h, rate_h, inlet_h, decay_h, states_h, ends_h,
                gwd_h, x_h, gmid_h, up_h, value_h,
                ginput_o, up_o, value_o, down_o, gate_o, input_o, out_o, rate_o, inlet_o, chan_o, gains_o,
                gml, merged, wo, wgi, gate, pad, conv, rate, inlet, decay, states, ends, gwd, gwv, own,
                work, gconv, pair, heads_r, heads_l, acc, tile, core_in, over_out, over_in,
                go, ggi, slots_d, slots_v, slots_o, slots_g, last_u, last_o, last_g, came_u, came_v, came_o, came_g,
                passed, tot, small, small_in, small_sum, group_in, gains, slope8,
                sem, ring_sem, line_sem):
    at = Place()
    sems = Sems(sem)
    here, width = own.shape
    toks = here // 2
    chans = chan.shape[1]
    group, taps = 8, 4
    steps = toks
    every = steps * group
    halo = (taps - 1) * group
    n = at.n
    ffl = came_u.shape[2]
    early = [
        sems.local(value_h, gwv), sems.local(up_h, last_u), sems.local(gml_h, gml),
        sems.local(wo_h.at[pl.ds(0, here)], wo.at[0]), sems.local(wo_h.at[pl.ds(here, here)], wo.at[1]),
    ]
    second = [sems.local(gate_h, gate), sems.local(states_h, states.at[pl.ds(group, every)]), sems.local(ends_h, ends)]
    third = [sems.local(decay_h, decay), sems.local(merged_h, merged)]
    fourth = [
        sems.local(a, b)
        for a, b in ((pad_h, pad), (conv_h, conv), (rate_h, rate), (inlet_h, inlet), (wgi_h, wgi), (gmid_h, own))
    ]
    hop = Hop(at)
    at.greet(hop)
    ring_d = Ring(at, gwd, slots_d, ring_sem.at[0], ring_sem.at[1], False)
    ring_v = Ring(at, gwv, slots_v, ring_sem.at[6], ring_sem.at[7], True)
    ring_o = Ring(at, go, slots_o, ring_sem.at[2], ring_sem.at[3], True)
    ring_g = Ring(at, ggi, slots_g, ring_sem.at[4], ring_sem.at[5], True)
    early[0].wait()
    ring_v.start()
    for c in early[1:]:
        c.wait()
    regroup = Regroup(at, sems, gwd_h, gwd)
    spread_u = Spread(at, sems, last_u, came_u)
    spread_u.start()
    regroup.start()

    def staged(came, first, size, outs, base=0):
        rows = came.shape[1]
        for f in range(4):
            at_col = f * size
            done = 0
            while done < size:
                block, col = divmod(at_col + done, width)
                step = min(size - done, width - col)
                tile[base + block * rows : base + (block + 1) * rows, col : col + step] = came[
                    f, :, first + done : first + done + step
                ].astype(F32)
                done += step
        copies, done = [], 0
        while done < 4 * size:
            step = min(width, 4 * size - done)
            copies.append(
                sems.local(tile.at[pl.ds(base + done // width * rows, rows), pl.ds(0, step)], outs.at[:, pl.ds(done, step)])
            )
            done += step
        return copies

    def merged_rows(m, _):
        sl = rows_at(m, here)
        for h in range(2):
            work[sl, pl.ds(h * here, here)] = mm_rt(gml[sl, :], wo[h])
        return 0

    lax.fori_loop(0, 4, merged_rows, 0)
    for c in second:
        c.wait()
    states[0:group, :] = ends[16:24, :]

    def split(c, _):
        cols = pl.ds(pl.multiple_of(c * 128, 128), 128)
        g = jnp.swapaxes(work[:, cols].reshape(group, steps, 128), 0, 1).reshape(every, 128)
        act, slope = gelu_pair(gate[:, cols])
        gate[:, cols] = g * act
        down = g * states[pl.ds(group, every), cols] * slope
        pair[:, cols] = jnp.swapaxes(down.reshape(steps, group, 128), 0, 1).reshape(every, 128).astype(BF)
        return 0

    lax.fori_loop(0, chans // 128, split, 0)
    ring_v.step(0)
    for c in third:
        c.wait()
    unroll = 8
    blocks = steps // unroll

    def totals(b, carry):
        for u in range(unroll):
            sl = pl.ds(pl.multiple_of((steps - 1 - (b * unroll + u)) * group, group), group)
            carry = decay[sl, :] * (gate[sl, :] + carry)
        return carry

    zero = jnp.zeros((group, chans), F32)
    passed[0:8, :] = ends[0:8, :]
    passed[8:16, :] = lax.fori_loop(0, blocks, totals, zero)
    line = Line(at, passed, tot, line_sem.at[0], line_sem.at[1])
    line.send(0, at.s)

    def out_rows(m, _):
        cols = pl.ds(pl.multiple_of(m * 256, 256), 256)
        go[rows_at(m, 256), 0:width] = mm_lt(merged[:, cols], gml[...]).astype(BF)
        return 0

    lax.fori_loop(0, chans // 256, out_rows, 0)
    normed, core_out = gml, wo
    fourth.append(sems.local(normed_h, normed))

    def enter(k, state):
        j = n - 1 - k
        line.wait(j)
        return tot[j, 0:8, :] * state + tot[j, 8:16, :]

    carry_in = lax.fori_loop(0, n - 1 - at.s, enter, zero)
    line.sent(0, at.s)

    def scan(b, carry):
        for u in range(unroll):
            sl = pl.ds(pl.multiple_of((steps - 1 - (b * unroll + u)) * group, group), group)
            adjoint = gate[sl, :] + carry
            gate[sl, :] = adjoint
            carry = decay[sl, :] * adjoint
        return carry

    lax.fori_loop(0, blocks, scan, carry_in)
    ring_v.step(1)
    spread_u.wait()
    staging = staged(came_u, 0, ffl, up_o)
    for c in fourth:
        c.wait()
    heads_r[...] = jnp.zeros_like(heads_r)
    heads_l[...] = jnp.zeros_like(heads_l)
    acc[...] = jnp.zeros_like(acc)
    edge = sems.remote(
        gconv.at[pl.ds(0, halo)], gconv.at[pl.ds(every, halo)], at.line(lax.rem(at.s + n - 1, n))
    )

    slope8[0:1, :], slope8[1:2, :] = decay_rows(chan[7:8, :])

    def gates(b, _):
        size = 128
        start = pl.multiple_of(b * size, size)
        sl = pl.ds(start, size)
        for h in range(chans // 128):
            cols = pl.ds(h * 128, 128)
            sp8 = slope8[0:1, cols]
            r, i, dec, adj = rate[sl, cols], inlet[sl, cols], decay[sl, cols], gate[sl, cols]
            low_bf = conv[sl, cols]
            low = low_bf.astype(F32)
            factor = jnp.sqrt(EPS_MULT - expm1_neg(2.0 * (r * sp8)))
            ai = adj * i
            af = adj * factor
            gld = adj * states[sl, cols] * dec - ai * low * (dec * dec) / factor
            gldr = gld * r
            grate = gldr * sp8 * (1.0 - r)
            ginl = af * low * i * (1.0 - i)
            grl, gil = grate.astype(BF), ginl.astype(BF)
            hb = pl.ds(h * 128, 128)
            gc = af * i + mm_rt(grl, wr[hb, :]) + mm_rt(gil, wl[hb, :])
            heads_r[hb, :] += mm_lt(low_bf, grl)
            heads_l[hb, :] += mm_lt(low_bf, gil)
            gconv[sl, cols] = gc
            fold = lambda v: jnp.sum(v.reshape(size // 8, 8, 128), axis=0)
            for k in range(taps):
                acc[k, :, cols] += fold(gc * pad[pl.ds(start + (halo - group * k), size), cols])
            acc[4, :, cols] += fold(gc)
            acc[5, :, cols] += fold(grate)
            acc[6, :, cols] += fold(ginl)
            acc[7, :, cols] += fold(gldr)

        @pl.when(jnp.logical_and(b == 0, at.s > 0))
        def _():
            edge.start()

        return 0

    lax.fori_loop(0, every // 128, gates, 0)

    @pl.when(at.s == n - 1)
    def _():
        gconv[pl.ds(every, halo), :] = jnp.zeros((halo, chans), F32)

    thirds = width // chans
    inputs = [
        sems.local(x_h.at[:, pl.ds(k * chans, chans)], pad.at[pl.ds(k * here, here)]) for k in range(thirds)
    ]
    go[:, width : width + 128] = heads_r[...].astype(BF)
    go[:, width + 128 :] = heads_l[...].astype(BF)
    ring_o.start()
    ring_v.step(2)
    for k in range(8):
        small[k : k + 1, :] = jnp.sum(acc[k], axis=0, keepdims=True)
    small[7:8, :] = small[7:8, :] * slope8[1:2, :]

    @pl.when(at.s < n - 1)
    def _():
        edge.wait_recv()

    @pl.when(at.s > 0)
    def _():
        edge.wait_send()

    def taps_back(b, _):
        start = pl.multiple_of(b * 128, 128)
        for h in range(chans // 128):
            cols = pl.ds(h * 128, 128)
            total = chan[0:1, cols] * gconv[pl.ds(start, 128), cols]
            for k in range(1, taps):
                total = total + chan[k : k + 1, cols] * gconv[pl.ds(start + group * k, 128), cols]
            work[pl.ds(start, 128), cols] = total
        return 0

    lax.fori_loop(0, every // 128, taps_back, 0)
    swap_rows(work, pair.at[:, pl.ds(chans, chans)], steps, BF)
    ring_v.step(3)

    def normed_rows(m, _):
        cols = pl.ds(pl.multiple_of(m * 256, 256), 256)
        ggi[rows_at(m, 256), :] = mm_lt(normed[:, cols], pair[...]).astype(BF)
        return 0

    lax.fori_loop(0, width // 256, normed_rows, 0)
    ring_g.start()
    for c in staging:
        c.wait()

    def back(o):
        sl = rows_at(o, here)

        def some(c, _):
            cols = pl.ds(pl.multiple_of(c * 512, 128), 512)
            tile[:, cols] = mm_rt(pair[sl, :], wgi[cols, :])
            return 0

        lax.fori_loop(0, width // 512, some, 0)

    sc = Scatter(at, sems, core_out, core_in, over_out, over_in, toks)

    def between(k):
        for j, ring, step in ((1, ring_v, 4), (2, ring_o, 0), (3, ring_v, 5)):

            @pl.when(k == j)
            def _():
                ring.step(step)

    sc.run_tile(back, tile, None, between)
    sc.second()
    ring_g.step(0)
    spread_v = Spread(at, sems, last_u, came_v)
    ring_v.last(last_u)
    spread_v.start()
    regroup.wait()
    ring_d.start()
    ring_o.step(1)
    ring_g.step(1)
    gain1 = jnp.zeros((1, width), F32)
    for c in inputs:
        c.wait()
    for r in range(2):
        sl = pl.ds(r * toks, toks)
        g = tile[sl, :] + sc.arrived(r)
        v = jnp.concatenate([pad[pl.ds(k * here + r * toks, toks), :] for k in range(thirds)], axis=1)
        s = lax.rsqrt(jnp.mean(v * v, axis=-1, keepdims=True) + EPS_NORM)
        gain1 = gain1 + jnp.sum(g * v * s, axis=0, keepdims=True)
        gg = g * whole_gain(gain, 0)
        mean = jnp.mean(gg * v, axis=-1, keepdims=True)
        own[sl, :] = own[sl, :] + s * gg - v * (s * s * s * mean)
    saves = [sems.local(own, ginput_o)]
    ring_d.step(0)
    ring_g.step(2)
    ring_o.step(2)
    for k in range(3):
        small[8 + k : 9 + k, :] = gain1[:, k * chans : (k + 1) * chans]
        small[11 + k : 12 + k, :] = gain2[0:1, k * chans : (k + 1) * chans]
    small[14:16, :] = jnp.zeros((2, chans), F32)
    share = Line(at, small, small_in, line_sem.at[2], line_sem.at[3])
    share.send(0, n)
    ring_d.step(1)
    spread_v.wait()
    saves += staged(came_v, 0, ffl, value_o)
    ring_g.step(3)
    ring_o.step(3)
    ring_d.step(2)
    small_in[at.s] = small[...]

    def arrive(j, total):
        @pl.when(j != at.s)
        def _():
            share.wait(j)

        return total + small_in[j]

    small_sum[...] = lax.fori_loop(0, n, arrive, jnp.zeros(small.shape, F32))
    ring_g.step(4)
    ring_o.step(4)
    ring_d.step(3)
    hops = [hop.start(sems, small_sum.at[pl.ds(0, 8)], chan_o)]
    lower = small_sum.at[pl.ds(8, 8)]
    around = [sems.remote(lower, group_in.at[at.f], at.group(p)) for p in (at.p1, at.p2, at.p3)]
    for c in around:
        c.start()
    group_in[at.f] = small_sum[8:16, :]
    ring_g.step(5)
    ring_o.step(5)
    ring_d.step(4)
    spread_g = Spread(at, sems, last_g, came_g)
    ring_g.last(last_g)
    spread_g.start()
    ring_o.last(last_o)
    hops.append(hop.start(sems, last_o, came_o))
    for c in saves:
        c.wait()
    ring_d.step(5)
    ring_d.last(tile)
    saves = [sems.local(tile.at[pl.ds(0, gwd.shape[0] // n)], down_o)]
    hop.wait(hops[1])
    crow = came_o.shape[0]
    for k in range(thirds + 1):
        size = min(chans, came_o.shape[1] - k * chans)
        rate[k * crow : (k + 1) * crow, 0:size] = came_o[:, k * chans : k * chans + size].astype(F32)
    saves += [
        sems.local(rate.at[pl.ds(k * crow, crow)], out_o.at[:, pl.ds(k * chans, chans)]) for k in range(thirds)
    ]
    saves += [
        sems.local(rate.at[pl.ds(thirds * crow, crow), pl.ds(k * 128, 128)], o) for k, o in enumerate((rate_o, inlet_o))
    ]
    for c in around:
        c.wait()
    gains[...] = group_in[0] + group_in[1] + group_in[2] + group_in[3]
    saves += [sems.local(gains, gains_o)]
    share.sent(0, n)
    sc.finish()
    for r in (ring_v, ring_d, ring_o, ring_g):
        r.finish()
    spread_g.wait()
    for c in saves:
        c.wait()
    saves = staged(came_g, 0, chans, gate_o) + staged(came_g, chans, chans, input_o, here // 2)
    hop.wait(hops[0])
    for c in saves:
        c.wait()


def call_back(chan, wr, wl, gain, gain2, gml, merged, wo, wgi, normed, gate, pad, conv, rate, inlet, decay, states, ends, gwd, x, gmid, up, value):
    every, width = gml.shape
    here = x.shape[0]
    chans = chan.shape[1]
    ffl = gwd.shape[0]
    n = lax.axis_size("seq")
    f32 = lambda *s: jax.ShapeDtypeStruct(s, F32)
    vf = lambda *s: pltpu.VMEM(s, F32)
    vb = lambda *s: pltpu.VMEM(s, BF)
    rows, crow = width // n, chans // n
    outs = [
        f32(here, width), f32(rows // 4, 4 * ffl), f32(rows // 4, 4 * ffl), f32(ffl // n, width), f32(rows // 4, 4 * chans), f32(rows // 4, 4 * chans), f32(crow, width),
        f32(crow, 128), f32(crow, 128), f32(8, chans), f32(8, chans),
    ]
    scratch = [
        vb(every, width), vb(every, chans), vb(2, here, width), vb(width, 2 * chans),
        vf(every, chans), vf(every + 24, chans), vb(every, chans), vf(every, chans), vf(every, chans), vf(every, chans),
        vf(every + 8, chans), vf(24, chans), vb(ffl, width), vb(width, ffl), vf(here, width),
        vf(every, chans), vf(every + 24, chans), vb(every, 2 * chans), vf(chans, 128), vf(chans, 128), vf(8, 8, chans),
        vf(here, width), vb(2, here, width), vb(here, width), vb(here, width),
        vb(chans, width + 256), vb(width, 2 * chans), vb(n - 1, ffl // n, width), vb(n - 1, rows, ffl), vb(n - 1, crow, width + 256), vb(n - 1, rows, 2 * chans),
        vb(rows, ffl), vb(crow, width + 256), vb(rows, 2 * chans), vb(4, rows // 4, ffl), vb(4, rows // 4, ffl),
        vb(crow, width + 256), vb(4, rows // 4, 2 * chans),
        vf(16, chans), vf(n, 16, chans), vf(16, chans), vf(n, 16, chans), vf(16, chans), vf(4, 8, chans), vf(8, chans), vf(8, chans),
        pltpu.SemaphoreType.DMA((120,)), pltpu.SemaphoreType.DMA((8, 4, n - 1)), pltpu.SemaphoreType.DMA((4, n)),
    ]
    return pl.pallas_call(
        branch_back,
        out_shape=outs,
        in_specs=[VMEM] * 5 + [ANY] * 18,
        out_specs=[ANY] * len(outs),
        scratch_shapes=scratch,
        compiler_params=pltpu.CompilerParams(collective_id=3, has_side_effects=True, vmem_limit_bytes=LIMIT),
        name="branch_back",
    )(chan, wr, wl, gain, gain2, gml, merged, wo, wgi, normed, gate, pad, conv, rate, inlet, decay, states, ends, gwd, x, gmid, up, value)


def collect(chan, gains, *refs):
    count = (len(refs) - 1 - 7) // 3
    sources, results, small = refs[:count], refs[count : 2 * count], refs[2 * count : 2 * count + 7]
    held, sem = refs[2 * count + 7 : -1], refs[-1]
    loads = [pltpu.make_async_copy(a, b, sem.at[0, k]) for k, (a, b) in enumerate(zip(sources, held))]
    copies = [pltpu.make_async_copy(a, b, sem.at[1, k]) for k, (a, b) in enumerate(zip(held, results))]
    for c in loads:
        c.start()
    for a, b in zip(loads, copies):
        a.wait()
        b.start()
    taps_o, bias_o, rate_o, inlet_o, decay_o, one_o, two_o = small
    n = lax.axis_size("seq")
    place = lax.axis_index("seq") * 4 + lax.axis_index("fsdp")
    per, chans = taps_o.shape[1], chan.shape[1]
    mine = pltpu.roll(chan[...], lax.rem(chans - lax.rem(place, n) * per, chans), 1)[:, :per]
    taps_o[...] = mine[0:4, :]
    for k, o in enumerate((bias_o, rate_o, inlet_o, decay_o)):
        o[...] = mine[4 + k : 5 + k, :].reshape(per)
    per = one_o.shape[0]
    thirds = 4 * n * per // chans
    for row, o in enumerate((one_o, two_o)):
        line = jnp.concatenate([gains[row * thirds + k : row * thirds + k + 1, :] for k in range(thirds)], axis=1)
        line = jnp.broadcast_to(line, (8, thirds * chans))
        line = pltpu.roll(line, lax.rem(thirds * chans - place * per, thirds * chans), 1)
        o[...] = line[0:1, :per].reshape(per)
    for c in copies:
        c.wait()


def call_collect(chan, gains, big):
    n = lax.axis_size("seq")
    chans = chan.shape[1]
    f32 = lambda *s: jax.ShapeDtypeStruct(s, F32)
    per, own = chans // n, big[0].shape[1] // (4 * n)
    outs = [f32(*v.shape) for v in big] + [f32(4, per)] + [f32(per)] * 4 + [f32(own)] * 2
    return pl.pallas_call(
        collect,
        out_shape=outs,
        in_specs=[VMEM] * 2 + [ANY] * len(big),
        out_specs=[ANY] * len(big) + [VMEM] * 7,
        scratch_shapes=[pltpu.VMEM(v.shape, F32) for v in big] + [pltpu.SemaphoreType.DMA((2, len(big)))],
        compiler_params=pltpu.CompilerParams(has_side_effects=True, vmem_limit_bytes=LIMIT),
        name="collect",
    )(chan, gains, *big)


def body(
    block_input, teacher, valid_lengths, norm_gain, w_gate, w_input, conv_weight, conv_bias,
    w_rate, bias_rate, w_inlet, bias_inlet, decay_param, w_out, mlp_gain, w_up, w_value, w_down,
):
    n_seq, n_fs = lax.axis_size("seq"), lax.axis_size(GROUP)
    si, fi = lax.axis_index("seq"), lax.axis_index(GROUP)
    rows_dev, toks, width = block_input.shape
    rows = rows_dev * n_fs
    here = rows_dev * toks
    chans = conv_bias.shape[0]
    hb = w_rate.shape[1]
    heads = chans // hb
    taps = conv_weight.shape[0]

    cw = conv_weight.astype(F32)
    x = block_input.reshape(here, width)
    (wgi, wuv, normed, n2, middle, gate_tm, pad_tm, conv_tm, rate_tm, inlet_tm, decay_tm, states_tm, merged, ends, gain, chan) = call_forward(
        x, norm_gain, mlp_gain, conv_weight, conv_bias, bias_rate, bias_inlet, decay_param, w_rate, w_inlet, w_out, w_gate, w_input, w_up, w_value)
    lens = lax.dynamic_slice_in_dim(valid_lengths, fi * rows_dev, rows_dev)
    pos = si * toks + jnp.arange(toks, dtype=jnp.int32)
    mask = (pos[None, :] < lens[:, None]).reshape(here, 1)
    slots = valid_lengths.shape[0] * toks * n_seq
    count = jnp.sum(valid_lengths).astype(F32)
    if all((v // n_seq) % 64 == 0 for v in (width, chans)):
        result, grad_middle, gml, gain2, g_down, up_part, value_part = call_mlp(
            n2, wuv, w_up, w_value, w_down, middle, teacher.reshape(here, width), valid_lengths, gain)
        grad_input, up_sum, value_sum, down_sum, gate_sum, input_sum, out_sum, rate_sum, inlet_sum, ch, gn = call_back(
            chan, w_rate, w_inlet, gain, gain2, gml, merged, w_out, wgi, normed, gate_tm, pad_tm,
            conv_tm, rate_tm, inlet_tm, decay_tm, states_tm, ends, g_down, x, grad_middle, up_part, value_part)
        (result, grad_input, up_sum, value_sum, down_sum, gate_sum, input_sum, out_sum, rate_sum, inlet_sum,
         s_taps, s_bias, s_rate, s_inlet, s_decay, s_one, s_two) = call_collect(
            ch, gn, [result, grad_input, up_sum, value_sum, down_sum, gate_sum, input_sum, out_sum, rate_sum, inlet_sum])
        return (
            result.reshape(block_input.shape), grad_input.reshape(block_input.shape), s_one, gate_sum, input_sum,
            s_taps, s_bias, rate_sum, s_rate, inlet_sum, s_inlet, s_decay, out_sum, s_two, up_sum, value_sum, down_sum,
        )

    sp = jax.nn.softplus(-decay_param.astype(F32))
    heads_shape = (heads, hb, hb)
    wr, wl = w_rate.reshape(heads_shape), w_inlet.reshape(heads_shape)
    wg, wi = wgi[:, :chans], wgi[:, chans:]
    ffl = w_down.shape[0]
    own = jnp.concatenate([lax.dynamic_slice_in_dim(w, fi * ffl, ffl, 1) for w in (w_up, w_value)], 1)
    wuv = lax.dynamic_update_slice_in_dim(wuv, own, fi * (width // n_fs), 0)
    wu, wv = wuv[:, :ffl], wuv[:, ffl:]
    gain_one, gain_two = gain[:, 0].reshape(-1), gain[:, 1].reshape(-1)
    s1 = lax.rsqrt(jnp.mean(x * x, axis=-1, keepdims=True) + EPS_NORM)
    s2 = lax.rsqrt(jnp.mean(middle * middle, axis=-1, keepdims=True) + EPS_NORM)
    tok = lambda v: v.reshape(-1, rows, chans).swapaxes(0, 1)
    padded, clf, r, i, decay, states = tok(pad_tm), tok(conv_tm), tok(rate_tm), tok(inlet_tm), tok(decay_tm), tok(states_tm)
    conv_low, clf = clf, clf.astype(F32)
    heads_in = conv_low.reshape(rows * toks, heads, hb)
    gate_pre = tok(gate_tm).reshape(-1, chans)
    gg, gd = gelu_pair(gate_pre)
    cum_end, state_in = ends[:8], ends[16:24]
    prev = jnp.concatenate([state_in[:, None], states[:, :-1]], axis=1)
    ld = -RATE_SCALE * r * sp
    factor = jnp.sqrt(EPS_MULT - jnp.expm1(2.0 * ld))
    up = mm(n2, wu)
    value = mm(n2, wv)
    vg, vd = gelu_pair(value)
    hidden = (vg * up).astype(BF)
    result = middle + rs(mm(hidden, w_down))
    grad_out = jnp.where(mask, result - teacher.reshape(here, width), 0.0) * (slots / count)
    gdi = ag(grad_out.astype(BF))
    g_down = mm_lt(hidden, gdi)
    gh = mm_rt(gdi, w_down)
    gu = (gh * vg).astype(BF)
    gv = (gh * up * vd).astype(BF)
    g_up = mm_lt(n2, gu)
    g_value = mm_lt(n2, gv)
    gn2 = rs(mm_rt(gu, wu) + mm_rt(gv, wv))
    gm_norm, gain2 = rms_back(middle, s2, gain_two, gn2)
    grad_middle = grad_out + gm_norm
    gml = ag(grad_middle.astype(BF))
    g_out = mm_lt(merged, gml)
    gmer = mm_rt(gml, w_out)
    gst = (gmer * gg).reshape(rows, toks, chans)
    ggate = (gmer * states.reshape(-1, chans) * gd).astype(BF)
    nextd = jnp.concatenate([decay[:, 1:], jnp.ones((rows, 1, chans), F32)], axis=1)
    carry, ladj = lax.associative_scan(linear_step, (nextd, gst), axis=1, reverse=True)
    tot2 = lax.all_gather(jnp.stack([cum_end, decay[:, 0] * ladj[:, 0]]), "seq")
    adj_in = jnp.zeros((rows, chans), F32)
    for j in reversed(range(n_seq)):
        adj_in = jnp.where(j > si, tot2[j, 0] * adj_in + tot2[j, 1], adj_in)
    adj = ladj + carry * adj_in[:, None]
    gdec = adj * prev
    gfac = adj * i * clf
    gld = gdec * decay - gfac * (decay * decay) / factor
    grate = gld * (-RATE_SCALE * sp) * r * (1.0 - r)
    ginl = adj * factor * clf * i * (1.0 - i)
    gdp = jnp.sum(gld * r, axis=(0, 1)) * RATE_SCALE * jax.nn.sigmoid(-decay_param.astype(F32))
    gcd = adj * factor * i
    grb, gib = jnp.sum(grate, (0, 1)), jnp.sum(ginl, (0, 1))
    grl, gil = grate.astype(BF).reshape(-1, heads, hb), ginl.astype(BF).reshape(-1, heads, hb)
    gwr = jnp.einsum("nhi,nhj->hij", heads_in, grl, preferred_element_type=F32).reshape(chans, hb)
    gwi = jnp.einsum("nhi,nhj->hij", heads_in, gil, preferred_element_type=F32).reshape(chans, hb)
    bk = lambda a, w: jnp.einsum("nhj,hij->nhi", a, w, preferred_element_type=F32).reshape(rows, toks, chans)
    gconv = gcd + bk(grl, wr) + bk(gil, wl)
    gcw = jnp.stack([jnp.sum(gconv * padded[:, taps - 1 - k: taps - 1 - k + toks], (0, 1)) for k in range(taps)])
    gcb = jnp.sum(gconv, (0, 1))
    gpad = jnp.zeros((rows, toks + taps - 1, chans), F32)
    for k in range(taps):
        gpad = gpad.at[:, taps - 1 - k: taps - 1 - k + toks].add(cw[k] * gconv)
    edge = shifted(gpad[:, : taps - 1], "seq", -1)
    gbr = gpad[:, taps - 1:].at[:, toks - (taps - 1):].add(edge).reshape(-1, chans).astype(BF)
    g_gate = mm_lt(normed, ggate)
    g_input = mm_lt(normed, gbr)
    gn1 = rs(mm_rt(ggate, wg) + mm_rt(gbr, wi))
    gi_norm, gain1 = rms_back(x, s1, gain_one, gn1)
    grad_input = grad_middle + gi_norm

    chan = jnp.concatenate([gcw, gcb[None], grb[None], gib[None], gdp[None]], 0)
    per = chans // n_seq
    chan = chan.reshape(8, n_seq, per).transpose(1, 0, 2).reshape(n_seq, 8 * per)
    blk = jnp.zeros((n_fs, n_seq, 8 * per), F32).at[fi].set(chan).reshape(n_fs * n_seq, 8 * per)
    gw = jnp.stack([gain1, gain2]).reshape(2, n_fs * n_seq, -1).transpose(1, 0, 2).reshape(n_fs * n_seq, -1)
    small = lax.psum_scatter(jnp.concatenate([blk, gw], 1), BOTH, scatter_dimension=0, tiled=True)[0]
    ch = small[: 8 * per].reshape(8, per)
    gn = small[8 * per:].reshape(2, -1)
    og = grads_rows(jnp.concatenate([g_out, gwr, gwi], 1))
    return (
        result.reshape(block_input.shape), grad_input.reshape(block_input.shape), gn[0],
        grads_cols(g_gate), grads_cols(g_input), ch[:4], ch[4], og[:, width: width + hb], ch[5],
        og[:, width + hb:], ch[6], ch[7], og[:, :width], gn[1], grads_cols(g_up), grads_cols(g_value), grads_rows(g_down),
    )


def solution(mesh):
    rowsh, vec, mat = P("fsdp", "seq", None), P("fsdp"), P("fsdp", None)
    ov, om = P(BOTH), P(BOTH, None)
    return jax.shard_map(
        body,
        mesh=mesh,
        in_specs=(rowsh, rowsh, P(), vec, mat, mat, P(None, "fsdp"), vec, mat, vec, mat, vec, vec, mat, vec, mat, mat, mat),
        out_specs=(rowsh, rowsh, ov, om, om, P(None, BOTH), ov, om, ov, om, ov, ov, om, ov, om, om, om),
        check_vma=False,
    )
```

```python
import jax
import jax.numpy as jnp
from jax import lax
from jax.sharding import PartitionSpec as P
from jax.experimental import pallas as pl
from jax.experimental.pallas import tpu as pltpu

EPS_NORM = 1e-06
EPS_MULT = 0.0001
RATE_SCALE = 8.0
BF = jnp.bfloat16
F32 = jnp.float32
GROUP = "fsdp"
BOTH = ("seq", "fsdp")


def mm(left, right):
    return jnp.dot(left, right, preferred_element_type=F32)


def mm_lt(left, right):
    return lax.dot_general(left, right, (((0,), (0,)), ((), ())), preferred_element_type=F32)


def mm_rt(left, right):
    return lax.dot_general(left, right, (((1,), (1,)), ((), ())), preferred_element_type=F32)


def gelu_pair(v):
    c = 0.7978845608028654
    a = 0.044715
    u = c * (v + a * v * v * v)
    t = jnp.tanh(u)
    g = 0.5 * v * (1.0 + t)
    d = 0.5 * (1.0 + t) + 0.5 * v * (1.0 - t * t) * c * (1.0 + 3.0 * a * v * v)
    return g, d


def linear_step(first_pair, second_pair):
    return (first_pair[0] * second_pair[0], second_pair[1] + second_pair[0] * first_pair[1])


def rms(v, g):
    s = lax.rsqrt(jnp.mean(v * v, axis=-1, keepdims=True) + EPS_NORM)
    return (v * s * g).astype(BF), s


def rms_back(v, s, g, grad):
    gg = grad * g
    gain = jnp.sum(grad * v * s, axis=0)
    return s * gg - v * (s * s * s) * jnp.mean(gg * v, axis=-1, keepdims=True), gain


def ag(a):
    return lax.all_gather(a, GROUP, axis=0, tiled=True)


def rs(a):
    return lax.psum_scatter(a.astype(BF), GROUP, scatter_dimension=0, tiled=True).astype(F32)


def grads_cols(g):
    part = lax.psum_scatter(g.astype(BF), "seq", scatter_dimension=0, tiled=True)
    return lax.all_to_all(part, GROUP, split_axis=0, concat_axis=1, tiled=True).astype(F32)


def grads_rows(g):
    n, m = lax.axis_size("seq"), lax.axis_size(GROUP)
    part = lax.psum_scatter(g.astype(BF), "seq", scatter_dimension=0, tiled=True)
    pairs = [(j * m + f, f * n + j) for j in range(n) for f in range(m)]
    return lax.ppermute(part, BOTH, pairs).astype(F32)


def shifted(shard, axis, by):
    length = lax.axis_size(axis)
    pairs = [(i, i + by) for i in range(length) if 0 <= i + by < length]
    return lax.ppermute(shard, axis, pairs)


MESH = pl.DeviceIdType.MESH
VMEM = pl.BlockSpec(memory_space=pltpu.VMEM)
ANY = pl.BlockSpec(memory_space=pl.ANY)
LIMIT = 63 * 2**20


def ds(start, size):
    if not isinstance(start, int):
        start = pl.multiple_of(start, size if size % 128 else 128)
    return pl.ds(start, size)


def rows_at(block, size):
    return pl.ds(pl.multiple_of(block * size, size), size)


class Place:
    def __init__(self):
        self.n = lax.axis_size("seq")
        self.s, self.f = lax.axis_index("seq"), lax.axis_index("fsdp")
        f = self.f
        self.p1 = f + 1 - 2 * lax.rem(f, 2)
        self.p2 = lax.rem(f + 2, 4)
        self.p3 = lax.rem(self.p1 + 2, 4)
        self.sx = self.s + 1 - 2 * lax.rem(self.s, 2)

    def group(self, f):
        return (self.s, f)

    def line(self, s):
        return (s, self.f)

    def greet(self, hop=None):
        barrier = pltpu.get_barrier_semaphore()
        for f in (self.p1, self.p2, self.p3):
            pl.semaphore_signal(barrier, inc=1, device_id=self.group(f), device_id_type=MESH)

        def one(j, _):
            pl.semaphore_signal(
                barrier, inc=1, device_id=self.line(lax.rem(self.s + j, self.n)), device_id_type=MESH
            )
            return 0

        lax.fori_loop(1, self.n, one, 0)
        pl.semaphore_wait(barrier, 3 + self.n - 1 + (0 if hop is None else hop.greet(barrier)))


class Sems:
    def __init__(self, ref):
        self.ref, self.used = ref, 0

    def take(self):
        self.used += 1
        return self.ref.at[self.used - 1]

    def remote(self, src, dst, device):
        return pltpu.make_async_remote_copy(
            src_ref=src, dst_ref=dst, send_sem=self.take(), recv_sem=self.take(),
            device_id=device, device_id_type=MESH,
        )

    def local(self, src, dst):
        copy = pltpu.make_async_copy(src, dst, self.take())
        copy.start()
        return copy


class Gather:
    def __init__(self, at, sems, buf, chunk):
        self.at, self.buf, self.chunk = at, buf, chunk
        mine = lambda f, r: buf.at[rows_at(f * 2 + r, chunk)]
        self.core = [sems.remote(mine(at.f, r), mine(at.f, r), at.group(at.p1)) for r in range(2)]
        self.over = [sems.remote(mine(at.f, r), mine(at.f, r), at.group(at.p2)) for r in range(2)]
        self.pass_on = [sems.remote(mine(at.p2, r), mine(at.p2, r), at.group(at.p1)) for r in range(2)]

    def send(self, r):
        self.over[r].start()
        self.core[r].start()

    def relay(self, r):
        self.over[r].wait_recv()
        self.pass_on[r].start()

    def near(self):
        for r in range(2):
            self.core[r].wait_recv()

    def finish(self):
        for r in range(2):
            self.core[r].wait_send()
            self.over[r].wait_send()
            self.pass_on[r].wait()


class Scatter:
    def __init__(self, at, sems, core_out, core_in, over_out, over_in, chunk):
        self.at, self.chunk = at, chunk
        self.core_out, self.core_in, self.over_out, self.over_in = core_out, core_in, over_out, over_in
        self.core = [sems.remote(core_out.at[k], core_in.at[k], at.group(at.p1)) for k in range(2)]
        self.over = [
            sems.remote(
                over_out.at[pl.ds(r * chunk, chunk)], over_in.at[pl.ds(r * chunk, chunk)], at.group(at.p2)
            )
            for r in range(2)
        ]

    def run(self, partial, own, between=lambda k: None):
        at = self.at

        def put(ref):
            def store(sl, cols, tile):
                ref[sl, cols] = tile.astype(BF)

            return store

        partial(at.p3, put(self.core_out.at[0]))
        self.core[0].start()
        between(0)

        def add_over(sl, cols, tile):
            self.over_out[sl, cols] = (tile + self.core_in[0, sl, cols].astype(F32)).astype(BF)

        self.core[0].wait_recv()
        partial(at.p2, add_over)
        self.over[0].start()
        between(1)
        partial(at.p1, put(self.core_out.at[1]))
        self.core[1].start()
        between(2)
        self.core[1].wait_recv()

        def add_own(sl, cols, tile):
            own[sl, cols] = own[sl, cols] + tile + self.core_in[1, sl, cols].astype(F32)

        partial(at.f, add_own)
        between(3)

    def run_tile(self, compute, tile, own, between=lambda k: None):
        at = self.at

        def one(k, _):
            compute(jnp.where(k == 0, at.p3, jnp.where(k == 1, at.p2, jnp.where(k == 2, at.p1, at.f))))

            @pl.when(k == 0)
            def _():
                self.core_out[0] = tile[...].astype(BF)
                self.core[0].start()

            @pl.when(k == 1)
            def _():
                self.core[0].wait_recv()
                for r in range(2):
                    sl = pl.ds(r * self.chunk, self.chunk)
                    self.over_out[sl, :] = (tile[sl, :] + self.core_in[0, sl, :].astype(F32)).astype(BF)
                self.over[0].start()

            @pl.when(k == 2)
            def _():
                self.core_out[1] = tile[...].astype(BF)
                self.core[1].start()

            @pl.when(k == 3)
            def _():
                self.core[1].wait_recv()
                if own is None:
                    tile[...] = tile[...] + self.core_in[1].astype(F32)
                else:
                    own[...] = own[...] + tile[...] + self.core_in[1].astype(F32)

            between(k)
            return 0

        lax.fori_loop(0, 4, one, 0)

    def second(self):
        self.over[0].wait_send()
        self.over[1].start()

    def arrived(self, r):
        self.over[r].wait_recv()
        return self.over_in[pl.ds(r * self.chunk, self.chunk), :].astype(F32)

    def finish(self):
        for copy in self.core + self.over[1:]:
            copy.wait_send()


class Columns:
    def __init__(self, at, sems, weights, buf, with_own=True):
        rows, width = weights[0].shape
        part = width // 4
        cut = rows // 4
        h = lax.rem(at.s, 4)
        one = h + 1 - 2 * lax.rem(h, 2)
        mates = [at.line(at.s - h + m) for m in (one, lax.rem(h + 2, 4), lax.rem(one + 2, 4))]
        self.near, self.own, self.far, self.side = [], [], [], []
        for k, w in enumerate(weights):
            cols = pl.ds(k * part, part)
            take = lambda f: pl.ds(pl.multiple_of(f * part, 128), part)
            mine = pl.ds(pl.multiple_of(at.f * rows, rows), rows)
            quarter = pl.ds(pl.multiple_of(h * cut, cut), cut)
            mine_cut = pl.ds(pl.multiple_of(at.f * rows + h * cut, cut), cut)
            if with_own:
                self.own.append(pltpu.make_async_copy(w.at[:, take(at.f)], buf.at[mine, cols], sems.take()))
            self.near.append(sems.remote(w.at[:, take(at.p1)], buf.at[mine, cols], at.group(at.p1)))
            for p in (at.p2, at.p3):
                self.far.append(sems.remote(w.at[quarter, take(p)], buf.at[mine_cut, cols], at.group(p)))
                came = buf.at[pl.ds(pl.multiple_of(p * rows + h * cut, cut), cut), cols]
                self.side.append([sems.remote(came, came, mate) for mate in mates])

    def start_far(self, first=0, end=4):
        for c in self.far[first:end]:
            c.start()

    def start_near(self):
        for c in self.near + self.own:
            c.start()

    def relay(self, k):
        self.far[k].wait_recv()
        for c in self.side[k]:
            c.start()

    def finish(self):
        for c in self.own + self.near + sum(self.side, []):
            c.wait()
        for c in self.far:
            c.wait_send()


def expm1_neg(v):
    series = v * (1 + v * (1 / 2) * (1 + v * (1 / 3) * (1 + v * (1 / 4) * (1 + v * (1 / 5) * (1 + v * (1 / 6))))))
    return jnp.where(v > -0.25, series, jnp.exp(v) - 1.0)


def decay_rows(param):
    small = jnp.exp(-jnp.abs(param))
    return (
        -RATE_SCALE * (jnp.maximum(-param, 0.0) + jnp.log1p(small)),
        RATE_SCALE * jnp.where(param > 0.0, small, 1.0) / (1.0 + small),
    )


def whole_gain(gain, row):
    return jnp.concatenate([gain[p, row : row + 1, :] for p in range(4)], axis=1)


def swap_rows(src, dst, outer, kind):
    total, width = src.shape
    inner = total // outer

    def one(c, _):
        cols = pl.ds(pl.multiple_of(c * 128, 128), 128)
        v = src[:, cols].reshape(outer, inner, 128)
        dst[:, cols] = jnp.swapaxes(v, 0, 1).reshape(total, 128).astype(kind)
        return 0

    lax.fori_loop(0, width // 128, one, 0)


def forward_branch(x, gain_one, gain_two, taps_w, conv_b, rate_b, inlet_b, decay_p, wr, wl, wo_h, wg, wi, wu, wv,
                   wgi_o, wuv_o, normed_o, n2_o, middle_o, gate_o, pad_o, conv_o, rate_o, inlet_o, decay_o, states_o,
                   merged_o, ends_o, gain_o, chan_o,
                   wo, wgi, normed, n2, middle, gains, chan, gain, gate, pad, conv, rate, inlet, decay, states, work, merged, ends,
                   tot, core_out, core_in, over_out, over_in, sem, tsend, trecv):
    at = Place()
    here, width = x.shape
    toks = here // 2
    chans = chan.shape[1]
    part = width // 4
    taps = 4
    steps = toks
    group = 8
    halo = (taps - 1) * group
    sems = Sems(sem)
    late = sems.local(wo_h, wo)
    chan[0:taps, :] = taps_w[...].astype(F32)
    for row, v in enumerate((conv_b, rate_b, inlet_b, decay_p)):
        chan[taps + row : taps + row + 1, :] = v[...].astype(F32).reshape(1, chans)
    for row, v in enumerate((gain_one, gain_two)):
        gains[row : row + 1, :] = v[...].astype(F32).reshape(1, part)
    gains[2:8, :] = jnp.zeros((6, part), F32)
    at.greet()

    shares = [
        sems.remote(gains, gain.at[at.f], at.group(p)) for p in (at.p1, at.p2, at.p3)
    ]
    for c in shares:
        c.start()
    gain[at.f] = gains[...]
    gi = Columns(at, sems, [wg, wi], wgi)
    gi.start_far()
    gi.start_near()
    uv = Columns(at, sems, [wu, wv], wuv_o, False)
    uv.start_near()
    ag1 = Gather(at, sems, normed, toks)
    scales = []
    for r in range(2):
        v = x[pl.ds(r * toks, toks), :]
        scales.append(lax.rsqrt(jnp.mean(v * v, axis=-1, keepdims=True) + EPS_NORM))
    for c in shares:
        c.wait()
    for r in range(2):
        sl = pl.ds(r * toks, toks)
        scale = scales[r]
        for p in range(4):
            cols = pl.ds(p * part, part)
            normed[rows_at(at.f * 2 + r, toks), cols] = (x[sl, cols] * scale * gain[p, 0:1, :]).astype(BF)
        ag1.send(r)
    for k in range(4):
        gi.relay(k)
    ag1.relay(0)
    uv.start_far()
    ag1.relay(1)
    ag1.near()
    ag1.finish()
    gi.finish()
    saves = [sems.local(normed, normed_o), sems.local(wgi, wgi_o), sems.local(gain, gain_o), sems.local(chan, chan_o)]

    def branch_rows(m, _):
        sl = rows_at(m, here)
        work[sl, :] = mm(normed[sl, :], wgi[:, chans:]).astype(BF).astype(F32)
        return 0

    lax.fori_loop(0, 4, branch_rows, 0)
    swap_rows(work, pad.at[pl.ds(halo, steps * group)], group, F32)
    edge = pad.at[pl.ds(steps * group, halo)]
    next_one = lax.rem(at.s + 1, at.n)
    tail = sems.remote(edge, pad.at[pl.ds(0, halo)], at.line(next_one))

    @pl.when(at.s < at.n - 1)
    def _():
        tail.start()

    @pl.when(at.s == 0)
    def _():
        pad[0:halo, :] = jnp.zeros((halo, chans), F32)

    def gate_rows(m, _):
        sl = rows_at(m, here)
        work[sl, :] = mm(normed[sl, :], wgi[:, :chans])
        return 0

    lax.fori_loop(0, 4, gate_rows, 0)
    swap_rows(work, gate, group, F32)

    @pl.when(at.s > 0)
    def _():
        tail.wait_recv()

    @pl.when(at.s < at.n - 1)
    def _():
        tail.wait_send()


    ends[16:17, :] = decay_rows(chan[7:8, :])[0]

    def gates(b, _):
        for h in range(chans // 128):
            cols = pl.ds(h * 128, 128)
            size = 128
            start = pl.multiple_of(b * size, size)
            sl = pl.ds(start, size)
            total = chan[taps : taps + 1, cols]
            for k in range(taps):
                total = total + chan[k : k + 1, cols] * pad[pl.ds(start + (halo - group * k), size), cols]
            low = total.astype(BF)
            blocks = pl.ds(h * 128, 128)
            r = jax.nn.sigmoid(mm(low, wr[blocks, :]) + chan[5:6, cols])
            i = jax.nn.sigmoid(mm(low, wl[blocks, :]) + chan[6:7, cols])
            ld = r * ends[16:17, cols]
            conv[sl, cols] = low
            low = low.astype(F32)
            decay[sl, cols] = jnp.exp(ld)
            work[sl, cols] = jnp.sqrt(EPS_MULT - expm1_neg(2.0 * ld)) * i * low
            rate[sl, cols] = r
            inlet[sl, cols] = i
        return 0

    lax.fori_loop(0, steps * group // 128, gates, 0)
    saves += [
        sems.local(gate, gate_o), sems.local(pad, pad_o), sems.local(conv, conv_o), sems.local(rate, rate_o),
        sems.local(inlet, inlet_o), sems.local(decay, decay_o),
    ]

    unroll = 8

    def totals(b, carry):
        h, p = carry
        for u in range(unroll):
            sl = pl.ds(pl.multiple_of((b * unroll + u) * group, group), group)
            a = decay[sl, :]
            h = a * h + work[sl, :]
            p = p * a
        return h, p

    zero = jnp.zeros((group, chans), F32)
    h, p = lax.fori_loop(0, steps // unroll, totals, (zero, zero + 1.0))
    ends[0:8, :] = p
    ends[8:16, :] = h

    def total_copy(src, to):
        return pltpu.make_async_remote_copy(
            src_ref=ends.at[pl.ds(0, 16)], dst_ref=tot.at[src], send_sem=tsend.at[to], recv_sem=trecv.at[src],
            device_id=at.line(to), device_id_type=MESH,
        )

    def send_total(j, _):
        total_copy(at.s, j).start()
        return 0

    lax.fori_loop(at.s + 1, at.n, send_total, 0)

    def enter(j, state):
        total_copy(j, j).wait_recv()
        return tot[j, 0:8, :] * state + tot[j, 8:16, :]

    state_in = lax.fori_loop(0, at.s, enter, zero)

    def sent_total(j, _):
        total_copy(at.s, j).wait_send()
        return 0

    lax.fori_loop(at.s + 1, at.n, sent_total, 0)
    uv.relay(0)
    uv.relay(1)
    ends[16:24, :] = state_in

    def scan(b, h):
        for u in range(unroll):
            sl = pl.ds(pl.multiple_of((b * unroll + u) * group, group), group)
            h = decay[sl, :] * h + work[sl, :]
            states[sl, :] = h
        return h

    lax.fori_loop(0, steps // unroll, scan, state_in)
    saves += [sems.local(states, states_o), sems.local(ends, ends_o)]

    def merge(c, _):
        cols = pl.ds(pl.multiple_of(c * 128, 128), 128)

        def some(b, _):
            sl = rows_at(b, 128)
            work[sl, cols] = states[sl, cols] * gelu_pair(gate[sl, cols])[0]
            return 0

        lax.fori_loop(0, steps * group // 128, some, 0)
        return 0

    lax.fori_loop(0, chans // 128, merge, 0)
    swap_rows(work, merged, steps, BF)
    saves += [sems.local(merged, merged_o)]

    middle[...] = x[...]
    late.wait()
    sc = Scatter(at, sems, core_out, core_in, over_out, over_in, toks)

    def partial(o, store):
        def half(r, _):
            sl = rows_at(r, toks)
            tile = mm(merged[rows_at(o * 2 + r, toks), :], wo[...])
            store(sl, slice(None), tile)
            return 0

        lax.fori_loop(0, 2, half, 0)

    def between(k):
        if k == 2:
            uv.relay(2)
            uv.relay(3)

    sc.run(partial, middle, between)
    sc.second()
    ag2 = Gather(at, sems, n2, toks)
    for r in range(2):
        sl = pl.ds(r * toks, toks)
        v = middle[sl, :] + sc.arrived(r)
        middle[sl, :] = v
        scale = lax.rsqrt(jnp.mean(v * v, axis=-1, keepdims=True) + EPS_NORM)
        for p in range(4):
            cols = pl.ds(p * part, part)
            n2[rows_at(at.f * 2 + r, toks), cols] = (middle[sl, cols] * scale * gain[p, 1:2, :]).astype(BF)
        ag2.send(r)
    saves += [sems.local(middle, middle_o)]
    for r in range(2):
        ag2.relay(r)
    ag2.near()
    ag2.finish()
    sc.finish()
    saves += [sems.local(n2, n2_o)]
    uv.finish()
    for c in saves:
        c.wait()


def call_forward(x, gain_one, gain_two, taps_w, conv_b, rate_b, inlet_b, decay_p, wr, wl, wo, wg, wi, wu, wv):
    here, width = x.shape
    chans = taps_w.shape[1]
    ffl = wu.shape[1] // 4
    every = here * 4
    n = lax.axis_size("seq")
    f32 = lambda *s: jax.ShapeDtypeStruct(s, F32)
    bf = lambda *s: jax.ShapeDtypeStruct(s, BF)
    vf = lambda *s: pltpu.VMEM(s, F32)
    vb = lambda *s: pltpu.VMEM(s, BF)
    outs = [
        bf(width, 2 * chans), bf(width, 2 * ffl), bf(every, width), bf(every, width), f32(here, width),
        f32(every, chans), f32(every + 24, chans), bf(every, chans), f32(every, chans), f32(every, chans),
        f32(every, chans), f32(every, chans), bf(every, chans), f32(24, chans), f32(4, 8, width // 4), f32(8, chans),
    ]
    scratch = [
        vb(chans, width), vb(width, 2 * chans), vb(every, width), vb(every, width), vf(here, width), vf(8, width // 4), vf(8, chans), vf(4, 8, width // 4),
        vf(every, chans), vf(every + 24, chans), vb(every, chans), vf(every, chans), vf(every, chans),
        vf(every, chans), vf(every, chans), vf(every, chans), vb(every, chans), vf(24, chans),
        vf(n, 16, chans), vb(2, here, width), vb(2, here, width), vb(here, width), vb(here, width),
        pltpu.SemaphoreType.DMA((170,)), pltpu.SemaphoreType.DMA((n,)), pltpu.SemaphoreType.DMA((n,)),
    ]
    return pl.pallas_call(
        forward_branch,
        out_shape=outs,
        in_specs=[VMEM] * 10 + [ANY] * 5,
        out_specs=[ANY] * len(outs),
        scratch_shapes=scratch,
        compiler_params=pltpu.CompilerParams(collective_id=1, has_side_effects=True, vmem_limit_bytes=LIMIT),
        name="forward_branch",
    )(x, gain_one, gain_two, taps_w, conv_b, rate_b, inlet_b, decay_p, wr, wl, wo, wg, wi, wu, wv)


class Hop:
    def __init__(self, at):
        b = at.f * at.n + at.s
        self.to = (lax.div(b, 4), lax.rem(b, 4))
        c = at.s * 4 + at.f
        self.source = (lax.rem(c, at.n), lax.div(c, at.n))
        self.stays = b == c

    def greet(self, barrier):
        @pl.when(jnp.logical_not(self.stays))
        def _():
            for device in (self.to, self.source):
                pl.semaphore_signal(barrier, inc=1, device_id=device, device_id_type=MESH)

        return jnp.where(self.stays, 0, 2)

    def start(self, sems, src, dst):
        far = sems.remote(src, dst, self.to)
        near = pltpu.make_async_copy(src, dst, sems.take())

        @pl.when(self.stays)
        def _():
            near.start()

        @pl.when(jnp.logical_not(self.stays))
        def _():
            far.start()

        return near, far

    def wait(self, pair):
        near, far = pair

        @pl.when(self.stays)
        def _():
            near.wait()

        @pl.when(jnp.logical_not(self.stays))
        def _():
            far.wait()


class Ring:
    def __init__(self, at, grads, slots, send, recv, by_rows):
        self.at, self.grads, self.slots, self.sem, self.rem = at, grads, slots, send, recv
        n = at.n
        self.q = self.place(at.s)
        rows, width = slots.shape[1:]
        self.rows = rows
        if by_rows:
            self.cut = [(pl.ds(i * rows // 4, rows // 4), pl.ds(0, width)) for i in range(4)]
        else:
            self.cut = [(pl.ds(0, rows), pl.ds(i * width // 4, width // 4)) for i in range(4)]
        self.way = (1, -1, 1, -1)
        self.to = {w: at.line(self.owner(lax.rem(self.q + w + n, n))) for w in (1, -1)}

    def place(self, s):
        half = lax.div(s, 2)
        return jnp.where(lax.rem(s, 2) == 0, half, self.at.n - 1 - half)

    def owner(self, q):
        n = self.at.n
        return jnp.where(q < n // 2, 2 * q, 2 * (n - 1 - q) + 1)

    def block(self, i, behind):
        n = self.at.n
        s = self.owner(lax.rem(self.q - self.way[i] * behind + 2 * n, n))
        r, c = self.cut[i]
        return self.grads.at[pl.ds(pl.multiple_of(s * self.rows + r.start, 16), r.size), c]

    def copy(self, i, k, src):
        r, c = self.cut[i]
        return pltpu.make_async_remote_copy(
            src_ref=src, dst_ref=self.slots.at[k, r, c], send_sem=self.sem.at[i, k], recv_sem=self.rem.at[i, k],
            device_id=self.to[self.way[i]], device_id_type=MESH,
        )

    def start(self):
        for i in range(4):
            self.copy(i, 0, self.block(i, 1)).start()

    def summed(self, i, k):
        r, c = self.cut[i]
        slot = self.slots.at[k, r, c]
        self.copy(i, k, slot).wait_recv()
        return slot, slot[...].astype(F32) + self.block(i, k + 2)[...].astype(F32)

    def step(self, k):
        for i in range(4):
            slot, value = self.summed(i, k)
            slot[...] = value.astype(BF)
            self.copy(i, k + 1, slot).start()

    def last(self, out, store=None):
        k = self.at.n - 2
        for i in range(4):
            _, value = self.summed(i, k)
            if store is None:
                out[self.cut[i]] = value.astype(out.dtype)
            else:
                store(i, value)

    def finish(self):
        def one(k, _):
            for i in range(4):
                r, c = self.cut[i]
                self.copy(i, k, self.slots.at[k, r, c]).wait_send()
            return 0

        lax.fori_loop(0, self.at.n - 1, one, 0)


class Regroup:
    def __init__(self, at, sems, src, dst, parts=None):
        size = src.shape[0] // at.n
        self.far, self.near = [], []
        for h in parts or range(at.n // 4):
            slot = dst.at[pl.ds(pl.multiple_of((at.f * (at.n // 4) + h) * size, 16), size)]
            block = lambda p: src.at[pl.ds(pl.multiple_of((p + 4 * h) * size, 16), size)]
            for p in (at.p2, at.p3, at.p1):
                self.far.append(sems.remote(block(p), slot, at.group(p)))
            self.near.append(pltpu.make_async_copy(block(at.f), slot, sems.take()))

    def start(self):
        for c in self.far + self.near:
            c.start()

    def wait(self):
        for c in self.far + self.near:
            c.wait()


class Spread:
    def __init__(self, at, sems, src, came):
        self.at, self.src, self.came = at, src, came
        rows = came.shape[1]
        send, recv = [sems.take() for _ in range(4)], [sems.take() for _ in range(4)]
        self.copies = []
        for k in range(1, 4):
            to = lax.rem(at.f + k, 4)
            piece = src.at[pl.ds(pl.multiple_of(to * rows, 16), rows)]
            self.copies.append(
                pltpu.make_async_remote_copy(
                    src_ref=piece, dst_ref=came.at[at.f], send_sem=send[k], recv_sem=recv[k],
                    device_id=at.group(to), device_id_type=MESH,
                )
            )

    def start(self):
        rows = self.came.shape[1]
        for c in self.copies:
            c.start()
        self.came[self.at.f] = self.src[pl.ds(pl.multiple_of(self.at.f * rows, 16), rows), :]

    def wait(self):
        for c in self.copies:
            c.wait()


def mlp(n2_h, wuv_h, wu_h, wv_h, wd_h, middle_h, teacher_h, lengths, gain,
        result_o, gmid_o, gml_o, gain_o, down_o, up_o, value_o,
        n2, wuv, wd, hidden, ge, gdi, gml, middle, own, gout, tile, core_out, core_in, over_out, over_in,
        gwd, gwu, gwv, acc_u, slots_u, last_u, gain_acc, sem, ring_sem):
    at = Place()
    sems = Sems(sem)
    here, width = middle.shape
    toks = here // 2
    ffl = hidden.shape[1]
    part = width // 4
    col = 384
    loads = [sems.local(n2_h, n2)]
    mine = pl.ds(pl.multiple_of(at.f * part, part), part)
    for k, w in enumerate((wu_h, wv_h)):
        cols = pl.ds(pl.multiple_of(at.f * ffl, 128), ffl)
        loads.append(sems.local(w.at[:, cols], wuv.at[mine, pl.ds(k * ffl, ffl)]))
    for p in (at.p1, at.p2, at.p3):
        rows = pl.ds(pl.multiple_of(p * part, part), part)
        loads.append(sems.local(wuv_h.at[rows], wuv.at[rows]))
    late = sems.local(wd_h, wd)
    loads2 = [sems.local(middle_h, middle), sems.local(middle_h, own), sems.local(teacher_h, gout)]
    at.greet()
    for c in loads:
        c.wait()

    def forward(o):
        sl = rows_at(o, here)

        def some(c, _):
            cols = pl.ds(pl.multiple_of(c * col, 128), col)
            cols2 = pl.ds(pl.multiple_of(c * col + ffl, 128), col)
            up = mm(n2[sl, :], wuv[:, cols])
            g, d = gelu_pair(mm(n2[sl, :], wuv[:, cols2]))
            hidden[sl, cols] = (g * up).astype(BF)
            ge[sl, cols] = g.astype(BF)
            ge[sl, cols2] = (up * d).astype(BF)
            return 0

        lax.fori_loop(0, ffl // col, some, 0)

        @pl.when(o == at.p3)
        def _():
            late.wait()

        def out(c, _):
            cols = pl.ds(pl.multiple_of(c * 512, 128), 512)
            tile[:, cols] = mm(hidden[sl, :], wd[:, cols])
            return 0

        lax.fori_loop(0, width // 512, out, 0)

    def hidden_rows(o):
        sl = rows_at(o, here)

        def some(c, _):
            cols = pl.ds(pl.multiple_of(c * col, 128), col)
            cols2 = pl.ds(pl.multiple_of(c * col + ffl, 128), col)
            gh = mm_rt(gdi[sl, :], wd[cols, :])
            ge[sl, cols] = (gh * ge[sl, cols].astype(F32)).astype(BF)
            ge[sl, cols2] = (gh * ge[sl, cols2].astype(F32)).astype(BF)
            return 0

        lax.fori_loop(0, ffl // col, some, 0)
        return 0

    sc = Scatter(at, sems, core_out, core_in, over_out, over_in, toks)

    def between(k):
        @pl.when(k == 2)
        def _():
            for c in loads2:
                c.wait()

    sc.run_tile(forward, tile, own, between)
    sc.second()
    count = lengths[0]
    for j in range(1, lengths.shape[0]):
        count = count + lengths[j]
    weight = (lengths.shape[0] * toks * at.n) / jnp.full((1, 1), count, jnp.int32).astype(F32)
    place = at.s * toks + lax.broadcasted_iota(jnp.int32, (toks, 1), 0)
    ag = Gather(at, sems, gdi, toks)
    for r in range(2):
        sl = pl.ds(r * toks, toks)
        v = own[sl, :] + sc.arrived(r)
        own[sl, :] = v
        v = jnp.where(place < lengths[at.f * 2 + r], v - gout[sl, :], 0.0) * weight
        gout[sl, :] = v
        gdi[rows_at(at.f * 2 + r, toks), :] = v.astype(BF)
        ag.send(r)
    saves = [sems.local(own, result_o)]
    ag.near()
    lax.fori_loop(0, 2, lambda k, _: hidden_rows(jnp.where(k == 0, at.f, at.p1)), 0)
    chip = pl.ds(pl.multiple_of(lax.div(at.f, 2) * 2 * here, 2 * here), 2 * here)
    other = pl.ds(pl.multiple_of((1 - lax.div(at.f, 2)) * 2 * here, 2 * here), 2 * here)
    pair = 2 * (width // at.n)

    def up_near(m, _):
        rows = pl.ds(pl.multiple_of(m * pair, 128), pair)
        acc_u[rows, :] = mm_lt(n2[chip, rows], ge[chip, 0:ffl])
        return 0

    lax.fori_loop(0, width // pair, up_near, 0)
    for r in range(2):
        ag.relay(r)
    ag.finish()
    sc.finish()
    saves.pop().wait()

    def down_rows(m, _):
        cols = pl.ds(pl.multiple_of(m * 128, 128), 128)
        gwd[rows_at(m, 128), :] = mm_lt(hidden[:, cols], gdi[...]).astype(BF)
        return 0

    def weight_rows(grads, first):
        def one(m, _):
            cols = pl.ds(pl.multiple_of(m * 256, 256), 256)
            grads[rows_at(m, 256), :] = mm_lt(n2[:, cols], ge[:, first : first + ffl]).astype(BF)
            return 0

        return one

    def backward(o):
        sl = rows_at(o, here)

        def out(c, _):
            cols = pl.ds(pl.multiple_of(c * 512, 128), 512)
            tile[:, cols] = mm_rt(ge[sl, :], wuv[cols, :])
            return 0

        lax.fori_loop(0, width // 512, out, 0)

    ring_u = Ring(at, gwu, slots_u, ring_sem.at[0], ring_sem.at[1], True)
    six = width // 256
    lax.fori_loop(0, 2, lambda k, _: hidden_rows(jnp.where(k == 0, at.p2, at.p3)), 0)
    def up_far(m):
        rows = pl.ds(pl.multiple_of(m * pair, 128), pair)
        gwu[rows, :] = (acc_u[rows, :] + mm_lt(n2[other, rows], ge[other, 0:ffl])).astype(BF)
        return 0

    sc2 = Scatter(at, sems, core_out, core_in, over_out, over_in, toks)

    def between(k):
        @pl.when(k == 1)
        def _():
            z = lax.div(at.s, 2)
            behind = lax.div(ring_u.owner(lax.rem(ring_u.q + at.n - 1, at.n)), 2)
            ahead = lax.div(ring_u.owner(lax.rem(ring_u.q + 1, at.n)), 2)
            lax.fori_loop(0, 2, lambda k, _: up_far(jnp.where(k == 0, behind, ahead)), 0)
            ring_u.start()
            at_end = jnp.logical_or(z == 0, z == 3)
            rest = lambda p: jnp.where(at_end, lax.rem(p + 2, 4), p + 1 - 2 * lax.rem(p, 2))
            lax.fori_loop(0, 2, lambda k, _: up_far(jnp.where(k == 0, rest(behind), rest(ahead))), 0)

        @pl.when(k == 3)
        def _():
            ring_u.step(0)

    sc2.run_tile(backward, tile, None, between)
    sc2.second()
    lax.fori_loop(0, six, weight_rows(gwv, ffl), 0)
    ring_u.step(1)
    lax.fori_loop(0, ffl // 128, down_rows, 0)
    ring_u.step(2)
    saves += [sems.local(gwv, value_o), sems.local(gwd, down_o)]
    ag2 = Gather(at, sems, gml, toks)
    acc = jnp.zeros((1, width), F32)
    for r in range(2):
        sl = pl.ds(r * toks, toks)
        g = tile[sl, :] + sc2.arrived(r)
        v = middle[sl, :]
        s = lax.rsqrt(jnp.mean(v * v, axis=-1, keepdims=True) + EPS_NORM)
        acc = acc + jnp.sum(g * v * s, axis=0, keepdims=True)
        gg = g * whole_gain(gain, 1)
        mean = jnp.mean(gg * v, axis=-1, keepdims=True)
        new = gout[sl, :] + s * gg - v * (s * s * s * mean)
        own[sl, :] = new
        gml[rows_at(at.f * 2 + r, toks), :] = new.astype(BF)
        ag2.send(r)
    gain_acc[...] = jnp.broadcast_to(acc, gain_acc.shape)
    saves += [sems.local(own, gmid_o), sems.local(gain_acc, gain_o)]
    ring_u.step(3)
    ring_u.step(4)
    ag2.relay(0)
    ring_u.step(5)
    ag2.relay(1)
    ring_u.last(last_u)
    saves += [sems.local(last_u, up_o)]
    ag2.near()
    ag2.finish()
    sc2.finish()
    saves += [sems.local(gml, gml_o)]
    ring_u.finish()
    for c in saves:
        c.wait()


def call_mlp(n2, wuv, wu, wv, wd, middle, teacher, lengths, gain):
    every, width = n2.shape
    here = middle.shape[0]
    ffl = wd.shape[0]
    n = lax.axis_size("seq")
    f32 = lambda *s: jax.ShapeDtypeStruct(s, F32)
    bf = lambda *s: jax.ShapeDtypeStruct(s, BF)
    vf = lambda *s: pltpu.VMEM(s, F32)
    vb = lambda *s: pltpu.VMEM(s, BF)
    outs = [
        f32(here, width), f32(here, width), bf(every, width), f32(8, width), bf(ffl, width),
        bf(width // n, ffl), bf(width, ffl),
    ]
    scratch = [
        vb(every, width), vb(width, 2 * ffl), vb(ffl, width), vb(every, ffl), vb(every, 2 * ffl), vb(every, width),
        vb(every, width), vf(here, width), vf(here, width), vf(here, width), vf(here, width),
        vb(2, here, width), vb(2, here, width), vb(here, width), vb(here, width),
        vb(ffl, width), vb(width, ffl), vb(width, ffl), vf(width, ffl), vb(n - 1, width // n, ffl),
        vb(width // n, ffl), vf(8, width),
        pltpu.SemaphoreType.DMA((100,)), pltpu.SemaphoreType.DMA((2, 4, n - 1)),
    ]
    return pl.pallas_call(
        mlp,
        out_shape=outs,
        in_specs=[ANY] * 7 + [pl.BlockSpec(memory_space=pltpu.SMEM), VMEM],
        out_specs=[ANY] * len(outs),
        scratch_shapes=scratch,
        compiler_params=pltpu.CompilerParams(collective_id=2, has_side_effects=True, vmem_limit_bytes=LIMIT),
        name="mlp",
    )(n2, wuv, wu, wv, wd, middle, teacher, lengths, gain)


class Line:
    def __init__(self, at, src, tot, send, recv):
        self.at, self.src, self.tot, self.send_sem, self.recv_sem = at, src, tot, send, recv

    def copy(self, slot, to):
        return pltpu.make_async_remote_copy(
            src_ref=self.src, dst_ref=self.tot.at[slot], send_sem=self.send_sem.at[to], recv_sem=self.recv_sem.at[slot],
            device_id=self.at.line(to), device_id_type=MESH,
        )

    def send(self, first, end):
        def one(j, _):
            @pl.when(j != self.at.s)
            def _():
                self.copy(self.at.s, j).start()

            return 0

        lax.fori_loop(first, end, one, 0)

    def sent(self, first, end):
        def one(j, _):
            @pl.when(j != self.at.s)
            def _():
                self.copy(self.at.s, j).wait_send()

            return 0

        lax.fori_loop(first, end, one, 0)

    def wait(self, j):
        self.copy(j, j).wait_recv()


def branch_back(chan, wr, wl, gain, gain2,
                gml_h, merged_h, wo_h, wgi_h, normed_h, gate_h, pad_h, conv_h, rate_h, inlet_h, decay_h, states_h, ends_h,
                gwd_h, x_h, gmid_h, up_h, value_h,
                ginput_o, up_o, value_o, down_o, gate_o, input_o, out_o, rate_o, inlet_o, chan_o, gains_o,
                gml, merged, wo, wgi, gate, pad, conv, rate, inlet, decay, states, ends, gwd, gwv, own,
                work, gconv, pair, heads_r, heads_l, acc, tile, core_in, over_out, over_in,
                go, ggi, slots_d, slots_v, slots_o, slots_g, last_u, came_u, came_v, go_own,
                passed, tot, small, small_in, small_sum, group_in, gains, slope8,
                sem, ring_sem, line_sem):
    at = Place()
    sems = Sems(sem)
    here, width = own.shape
    toks = here // 2
    chans = chan.shape[1]
    group, taps = 8, 4
    steps = toks
    every = steps * group
    halo = (taps - 1) * group
    n = at.n
    ffl = came_u.shape[2]
    early = [
        sems.local(value_h, gwv), sems.local(up_h, last_u), sems.local(gml_h, gml),
        sems.local(wo_h.at[pl.ds(0, here)], wo.at[0]), sems.local(wo_h.at[pl.ds(here, here)], wo.at[1]),
    ]
    second = [sems.local(gate_h, gate), sems.local(states_h, states.at[pl.ds(group, every)]), sems.local(ends_h, ends)]
    third = [sems.local(decay_h, decay), sems.local(merged_h, merged)]
    fourth = [
        sems.local(a, b)
        for a, b in ((pad_h, pad), (conv_h, conv), (rate_h, rate), (inlet_h, inlet), (wgi_h, wgi), (gmid_h, own))
    ]
    hop = Hop(at)
    at.greet(hop)
    ring_d = Ring(at, gwd, slots_d, ring_sem.at[0], ring_sem.at[1], False)
    ring_v = Ring(at, gwv, slots_v, ring_sem.at[6], ring_sem.at[7], True)
    ring_o = Ring(at, go_own, slots_o, ring_sem.at[2], ring_sem.at[3], True)
    ring_g = Ring(at, ggi, slots_g, ring_sem.at[4], ring_sem.at[5], True)
    early[0].wait()
    ring_v.start()
    for c in early[1:]:
        c.wait()
    regroup = [Regroup(at, sems, gwd_h, gwd, part) for part in (range(n // 8), range(n // 8, n // 4))]
    spread_u = Spread(at, sems, last_u, came_u)
    spread_u.start()
    regroup[0].start()

    def staged(came, first, size, outs, base=0):
        rows = came.shape[1]
        for f in range(4):
            at_col = f * size
            done = 0
            while done < size:
                block, col = divmod(at_col + done, width)
                step = min(size - done, width - col)
                tile[base + block * rows : base + (block + 1) * rows, col : col + step] = came[
                    f, :, first + done : first + done + step
                ].astype(F32)
                done += step
        copies, done = [], 0
        while done < 4 * size:
            step = min(width, 4 * size - done)
            copies.append(
                sems.local(tile.at[pl.ds(base + done // width * rows, rows), pl.ds(0, step)], outs.at[:, pl.ds(done, step)])
            )
            done += step
        return copies

    def merged_rows(m, _):
        sl = rows_at(m, here)
        for h in range(2):
            work[sl, pl.ds(h * here, here)] = mm_rt(gml[sl, :], wo[h])
        return 0

    lax.fori_loop(0, 4, merged_rows, 0)
    for c in second:
        c.wait()
    states[0:group, :] = ends[16:24, :]

    def split(c, _):
        cols = pl.ds(pl.multiple_of(c * 128, 128), 128)
        g = jnp.swapaxes(work[:, cols].reshape(group, steps, 128), 0, 1).reshape(every, 128)
        act, slope = gelu_pair(gate[:, cols])
        gate[:, cols] = g * act
        down = g * states[pl.ds(group, every), cols] * slope
        pair[:, cols] = jnp.swapaxes(down.reshape(steps, group, 128), 0, 1).reshape(every, 128).astype(BF)
        return 0

    lax.fori_loop(0, chans // 128, split, 0)
    ring_v.step(0)
    for c in third:
        c.wait()
    unroll = 8
    blocks = steps // unroll

    def totals(b, carry):
        for u in range(unroll):
            sl = pl.ds(pl.multiple_of((steps - 1 - (b * unroll + u)) * group, group), group)
            carry = decay[sl, :] * (gate[sl, :] + carry)
        return carry

    zero = jnp.zeros((group, chans), F32)
    passed[0:8, :] = ends[0:8, :]
    passed[8:16, :] = lax.fori_loop(0, blocks, totals, zero)
    line = Line(at, passed, tot, line_sem.at[0], line_sem.at[1])
    line.send(0, at.s)

    def out_rows(m, _):
        cols = pl.ds(pl.multiple_of(m * 256, 256), 256)
        go[rows_at(m, 256), 0:width] = mm_lt(merged[:, cols], gml[...]).astype(BF)
        return 0

    lax.fori_loop(0, chans // 256, out_rows, 0)
    normed, core_out = gml, wo
    fourth.append(sems.local(normed_h, normed))

    def enter(k, state):
        j = n - 1 - k
        line.wait(j)
        return tot[j, 0:8, :] * state + tot[j, 8:16, :]

    carry_in = lax.fori_loop(0, n - 1 - at.s, enter, zero)
    line.sent(0, at.s)

    def scan(b, carry):
        for u in range(unroll):
            sl = pl.ds(pl.multiple_of((steps - 1 - (b * unroll + u)) * group, group), group)
            adjoint = gate[sl, :] + carry
            gate[sl, :] = adjoint
            carry = decay[sl, :] * adjoint
        return carry

    lax.fori_loop(0, blocks, scan, carry_in)
    ring_v.step(1)
    spread_u.wait()
    staging = staged(came_u, 0, ffl, up_o)
    for c in fourth:
        c.wait()
    heads_r[...] = jnp.zeros_like(heads_r)
    heads_l[...] = jnp.zeros_like(heads_l)
    acc[...] = jnp.zeros_like(acc)
    edge = sems.remote(
        gconv.at[pl.ds(0, halo)], gconv.at[pl.ds(every, halo)], at.line(lax.rem(at.s + n - 1, n))
    )

    slope8[0:1, :], slope8[1:2, :] = decay_rows(chan[7:8, :])

    def gates(b, _):
        size = 128
        start = pl.multiple_of(b * size, size)
        sl = pl.ds(start, size)
        for h in range(chans // 128):
            cols = pl.ds(h * 128, 128)
            sp8 = slope8[0:1, cols]
            r, i, dec, adj = rate[sl, cols], inlet[sl, cols], decay[sl, cols], gate[sl, cols]
            low_bf = conv[sl, cols]
            low = low_bf.astype(F32)
            factor = jnp.sqrt(EPS_MULT - expm1_neg(2.0 * (r * sp8)))
            ai = adj * i
            af = adj * factor
            gld = adj * states[sl, cols] * dec - ai * low * (dec * dec) / factor
            gldr = gld * r
            grate = gldr * sp8 * (1.0 - r)
            ginl = af * low * i * (1.0 - i)
            grl, gil = grate.astype(BF), ginl.astype(BF)
            hb = pl.ds(h * 128, 128)
            gc = af * i + mm_rt(grl, wr[hb, :]) + mm_rt(gil, wl[hb, :])
            heads_r[hb, :] += mm_lt(low_bf, grl)
            heads_l[hb, :] += mm_lt(low_bf, gil)
            gconv[sl, cols] = gc
            fold = lambda v: jnp.sum(v.reshape(size // 8, 8, 128), axis=0)
            for k in range(taps):
                acc[k, :, cols] += fold(gc * pad[pl.ds(start + (halo - group * k), size), cols])
            acc[4, :, cols] += fold(gc)
            acc[5, :, cols] += fold(grate)
            acc[6, :, cols] += fold(ginl)
            acc[7, :, cols] += fold(gldr)

        @pl.when(jnp.logical_and(b == 0, at.s > 0))
        def _():
            edge.start()

        return 0

    lax.fori_loop(0, every // 128, gates, 0)

    @pl.when(at.s == n - 1)
    def _():
        gconv[pl.ds(every, halo), :] = jnp.zeros((halo, chans), F32)

    thirds = width // chans
    inputs = [
        sems.local(x_h.at[:, pl.ds(k * chans, chans)], pad.at[pl.ds(k * here, here)]) for k in range(thirds)
    ]
    go[:, width : width + 128] = heads_r[...].astype(BF)
    go[:, width + 128 :] = heads_l[...].astype(BF)
    regroup_o = Regroup(at, sems, go, go_own)
    regroup_o.start()
    ring_v.step(2)
    for k in range(8):
        small[k : k + 1, :] = jnp.sum(acc[k], axis=0, keepdims=True)
    small[7:8, :] = small[7:8, :] * slope8[1:2, :]

    @pl.when(at.s < n - 1)
    def _():
        edge.wait_recv()

    @pl.when(at.s > 0)
    def _():
        edge.wait_send()

    def taps_back(b, _):
        start = pl.multiple_of(b * 128, 128)
        for h in range(chans // 128):
            cols = pl.ds(h * 128, 128)
            total = chan[0:1, cols] * gconv[pl.ds(start, 128), cols]
            for k in range(1, taps):
                total = total + chan[k : k + 1, cols] * gconv[pl.ds(start + group * k, 128), cols]
            work[pl.ds(start, 128), cols] = total
        return 0

    lax.fori_loop(0, every // 128, taps_back, 0)
    swap_rows(work, pair.at[:, pl.ds(chans, chans)], steps, BF)
    ring_v.step(3)

    def normed_rows(m, _):
        cols = pl.ds(pl.multiple_of(m * 256, 256), 256)
        ggi[rows_at(m, 256), :] = mm_lt(normed[:, cols], pair[...]).astype(BF)
        return 0

    lax.fori_loop(0, width // 256, normed_rows, 0)
    ring_g.start()
    for c in staging:
        c.wait()

    def back(o):
        sl = rows_at(o, here)

        def some(c, _):
            cols = pl.ds(pl.multiple_of(c * 512, 128), 512)
            tile[:, cols] = mm_rt(pair[sl, :], wgi[cols, :])
            return 0

        lax.fori_loop(0, width // 512, some, 0)

    sc = Scatter(at, sems, core_out, core_in, over_out, over_in, toks)

    def between(k):
        for j, ring, step in ((1, ring_v, 4), (2, ring_g, 0), (3, ring_v, 5)):

            @pl.when(k == j)
            def _():
                ring.step(step)

    sc.run_tile(back, tile, None, between)
    sc.second()
    spread_v = Spread(at, sems, last_u, came_v)
    ring_v.last(last_u)
    spread_v.start()
    ring_g.step(1)
    regroup_o.wait()
    ring_o.start()
    ring_g.step(2)
    gain1 = jnp.zeros((1, width), F32)
    for c in inputs:
        c.wait()
    for r in range(2):
        sl = pl.ds(r * toks, toks)
        g = tile[sl, :] + sc.arrived(r)
        v = jnp.concatenate([pad[pl.ds(k * here + r * toks, toks), :] for k in range(thirds)], axis=1)
        s = lax.rsqrt(jnp.mean(v * v, axis=-1, keepdims=True) + EPS_NORM)
        gain1 = gain1 + jnp.sum(g * v * s, axis=0, keepdims=True)
        gg = g * whole_gain(gain, 0)
        mean = jnp.mean(gg * v, axis=-1, keepdims=True)
        own[sl, :] = own[sl, :] + s * gg - v * (s * s * s * mean)
    regroup[1].start()
    saves = [sems.local(own, ginput_o)]
    ring_o.step(0)
    ring_g.step(3)
    for k in range(3):
        small[8 + k : 9 + k, :] = gain1[:, k * chans : (k + 1) * chans]
        small[11 + k : 12 + k, :] = gain2[0:1, k * chans : (k + 1) * chans]
    small[14:16, :] = jnp.zeros((2, chans), F32)
    share = Line(at, small, small_in, line_sem.at[2], line_sem.at[3])
    share.send(0, n)
    ring_o.step(1)
    ring_g.step(4)
    spread_v.wait()
    saves += staged(came_v, 0, ffl, value_o)
    small_in[at.s] = small[...]

    def arrive(j, total):
        @pl.when(j != at.s)
        def _():
            share.wait(j)

        return total + small_in[j]

    small_sum[...] = lax.fori_loop(0, n, arrive, jnp.zeros(small.shape, F32))
    ring_o.step(2)
    ring_g.step(5)
    hops = [hop.start(sems, small_sum.at[pl.ds(0, 8)], chan_o)]
    lower = small_sum.at[pl.ds(8, 8)]
    around = [sems.remote(lower, group_in.at[at.f], at.group(p)) for p in (at.p1, at.p2, at.p3)]
    for c in around:
        c.start()
    group_in[at.f] = small_sum[8:16, :]
    ring_o.step(3)
    last_g = last_u.at[:, pl.ds(0, 2 * chans)]
    ring_g.last(last_g)
    for c in regroup:
        c.wait()
    ring_d.start()
    for c in around:
        c.wait()
    gains[...] = group_in[0] + group_in[1] + group_in[2] + group_in[3]
    came_g = came_u.at[:, :, pl.ds(0, 2 * chans)]
    spread_g = Spread(at, sems, last_g, came_g)
    spread_g.start()
    ring_o.step(4)
    ring_d.step(0)
    for c in saves:
        c.wait()
    saves = [sems.local(gains, gains_o)]
    ring_o.step(5)
    ring_d.step(1)
    crow = rate_o.shape[0]

    def store_out(i, value):
        rows = ring_o.cut[i][0]
        for k in range(thirds + 1):
            size = min(chans, width + 256 - k * chans)
            rate[pl.ds(k * crow + rows.start, rows.size), 0:size] = value[:, k * chans : k * chans + size]

    ring_o.last(None, store_out)
    saves += [
        sems.local(rate.at[pl.ds(k * crow, crow)], out_o.at[:, pl.ds(k * chans, chans)]) for k in range(thirds)
    ]
    saves += [
        sems.local(rate.at[pl.ds(thirds * crow, crow), pl.ds(k * 128, 128)], o) for k, o in enumerate((rate_o, inlet_o))
    ]
    ring_d.step(2)
    spread_g.wait()
    saves += staged(came_g, 0, chans, gate_o) + staged(came_g, chans, chans, input_o, here // 2)
    share.sent(0, n)
    sc.finish()
    hop.wait(hops[0])
    for r in (ring_v, ring_o, ring_g):
        r.finish()
    ring_d.step(3)
    ring_d.step(4)
    ring_d.step(5)
    drow, dcol = gwd.shape[0] // n, width // 4

    def store_down(i, value):
        work[i * drow : (i + 1) * drow, 0:dcol] = value

    ring_d.last(None, store_down)
    saves += [
        sems.local(work.at[pl.ds(i * drow, drow), pl.ds(0, dcol)], down_o.at[:, pl.ds(i * dcol, dcol)]) for i in range(4)
    ]
    ring_d.finish()
    for c in saves:
        c.wait()


def call_back(chan, wr, wl, gain, gain2, gml, merged, wo, wgi, normed, gate, pad, conv, rate, inlet, decay, states, ends, gwd, x, gmid, up, value):
    every, width = gml.shape
    here = x.shape[0]
    chans = chan.shape[1]
    ffl = gwd.shape[0]
    n = lax.axis_size("seq")
    f32 = lambda *s: jax.ShapeDtypeStruct(s, F32)
    vf = lambda *s: pltpu.VMEM(s, F32)
    vb = lambda *s: pltpu.VMEM(s, BF)
    rows, crow = width // n, chans // n
    outs = [
        f32(here, width), f32(rows // 4, 4 * ffl), f32(rows // 4, 4 * ffl), f32(ffl // n, width), f32(rows // 4, 4 * chans), f32(rows // 4, 4 * chans), f32(crow, width),
        f32(crow, 128), f32(crow, 128), f32(8, chans), f32(8, chans),
    ]
    scratch = [
        vb(every, width), vb(every, chans), vb(2, here, width), vb(width, 2 * chans),
        vf(every, chans), vf(every + 24, chans), vb(every, chans), vf(every, chans), vf(every, chans), vf(every, chans),
        vf(every + 8, chans), vf(24, chans), vb(ffl, width), vb(width, ffl), vf(here, width),
        vf(every, chans), vf(every + 24, chans), vb(every, 2 * chans), vf(chans, 128), vf(chans, 128), vf(8, 8, chans),
        vf(here, width), vb(2, here, width), vb(here, width), vb(here, width),
        vb(chans, width + 256), vb(width, 2 * chans), vb(n - 1, ffl // n, width), vb(n - 1, rows, ffl), vb(n - 1, crow, width + 256), vb(n - 1, rows, 2 * chans),
        vb(rows, ffl), vb(4, rows // 4, ffl), vb(4, rows // 4, ffl), vb(chans, width + 256),
        vf(16, chans), vf(n, 16, chans), vf(16, chans), vf(n, 16, chans), vf(16, chans), vf(4, 8, chans), vf(8, chans), vf(8, chans),
        pltpu.SemaphoreType.DMA((140,)), pltpu.SemaphoreType.DMA((8, 4, n - 1)), pltpu.SemaphoreType.DMA((4, n)),
    ]
    return pl.pallas_call(
        branch_back,
        out_shape=outs,
        in_specs=[VMEM] * 5 + [ANY] * 18,
        out_specs=[ANY] * len(outs),
        scratch_shapes=scratch,
        compiler_params=pltpu.CompilerParams(collective_id=3, has_side_effects=True, vmem_limit_bytes=LIMIT),
        name="branch_back",
    )(chan, wr, wl, gain, gain2, gml, merged, wo, wgi, normed, gate, pad, conv, rate, inlet, decay, states, ends, gwd, x, gmid, up, value)


def collect(chan, gains, *refs):
    count = (len(refs) - 1 - 7) // 3
    sources, results, small = refs[:count], refs[count : 2 * count], refs[2 * count : 2 * count + 7]
    held, sem = refs[2 * count + 7 : -1], refs[-1]
    loads = [pltpu.make_async_copy(a, b, sem.at[0, k]) for k, (a, b) in enumerate(zip(sources, held))]
    copies = [pltpu.make_async_copy(a, b, sem.at[1, k]) for k, (a, b) in enumerate(zip(held, results))]
    for c in loads:
        c.start()
    for a, b in zip(loads, copies):
        a.wait()
        b.start()
    taps_o, bias_o, rate_o, inlet_o, decay_o, one_o, two_o = small
    n = lax.axis_size("seq")
    place = lax.axis_index("seq") * 4 + lax.axis_index("fsdp")
    per, chans = taps_o.shape[1], chan.shape[1]
    mine = pltpu.roll(chan[...], lax.rem(chans - lax.rem(place, n) * per, chans), 1)[:, :per]
    taps_o[...] = mine[0:4, :]
    for k, o in enumerate((bias_o, rate_o, inlet_o, decay_o)):
        o[...] = mine[4 + k : 5 + k, :].reshape(per)
    per = one_o.shape[0]
    thirds = 4 * n * per // chans
    for row, o in enumerate((one_o, two_o)):
        line = jnp.concatenate([gains[row * thirds + k : row * thirds + k + 1, :] for k in range(thirds)], axis=1)
        line = jnp.broadcast_to(line, (8, thirds * chans))
        line = pltpu.roll(line, lax.rem(thirds * chans - place * per, thirds * chans), 1)
        o[...] = line[0:1, :per].reshape(per)
    for c in copies:
        c.wait()


def call_collect(chan, gains, big):
    n = lax.axis_size("seq")
    chans = chan.shape[1]
    f32 = lambda *s: jax.ShapeDtypeStruct(s, F32)
    per, own = chans // n, big[0].shape[1] // (4 * n)
    outs = [f32(*v.shape) for v in big] + [f32(4, per)] + [f32(per)] * 4 + [f32(own)] * 2
    return pl.pallas_call(
        collect,
        out_shape=outs,
        in_specs=[VMEM] * 2 + [ANY] * len(big),
        out_specs=[ANY] * len(big) + [VMEM] * 7,
        scratch_shapes=[pltpu.VMEM(v.shape, F32) for v in big] + [pltpu.SemaphoreType.DMA((2, len(big)))],
        compiler_params=pltpu.CompilerParams(has_side_effects=True, vmem_limit_bytes=LIMIT),
        name="collect",
    )(chan, gains, *big)


def body(
    block_input, teacher, valid_lengths, norm_gain, w_gate, w_input, conv_weight, conv_bias,
    w_rate, bias_rate, w_inlet, bias_inlet, decay_param, w_out, mlp_gain, w_up, w_value, w_down,
):
    n_seq, n_fs = lax.axis_size("seq"), lax.axis_size(GROUP)
    si, fi = lax.axis_index("seq"), lax.axis_index(GROUP)
    rows_dev, toks, width = block_input.shape
    rows = rows_dev * n_fs
    here = rows_dev * toks
    chans = conv_bias.shape[0]
    hb = w_rate.shape[1]
    heads = chans // hb
    taps = conv_weight.shape[0]

    cw = conv_weight.astype(F32)
    x = block_input.reshape(here, width)
    (wgi, wuv, normed, n2, middle, gate_tm, pad_tm, conv_tm, rate_tm, inlet_tm, decay_tm, states_tm, merged, ends, gain, chan) = call_forward(
        x, norm_gain, mlp_gain, conv_weight, conv_bias, bias_rate, bias_inlet, decay_param, w_rate, w_inlet, w_out, w_gate, w_input, w_up, w_value)
    lens = lax.dynamic_slice_in_dim(valid_lengths, fi * rows_dev, rows_dev)
    pos = si * toks + jnp.arange(toks, dtype=jnp.int32)
    mask = (pos[None, :] < lens[:, None]).reshape(here, 1)
    slots = valid_lengths.shape[0] * toks * n_seq
    count = jnp.sum(valid_lengths).astype(F32)
    if n_seq == 8 and all((v // n_seq) % 64 == 0 for v in (width, chans)):
        result, grad_middle, gml, gain2, g_down, up_part, value_part = call_mlp(
            n2, wuv, w_up, w_value, w_down, middle, teacher.reshape(here, width), valid_lengths, gain)
        grad_input, up_sum, value_sum, down_sum, gate_sum, input_sum, out_sum, rate_sum, inlet_sum, ch, gn = call_back(
            chan, w_rate, w_inlet, gain, gain2, gml, merged, w_out, wgi, normed, gate_tm, pad_tm,
            conv_tm, rate_tm, inlet_tm, decay_tm, states_tm, ends, g_down, x, grad_middle, up_part, value_part)
        (result, grad_input, up_sum, value_sum, down_sum, gate_sum, input_sum, out_sum, rate_sum, inlet_sum,
         s_taps, s_bias, s_rate, s_inlet, s_decay, s_one, s_two) = call_collect(
            ch, gn, [result, grad_input, up_sum, value_sum, down_sum, gate_sum, input_sum, out_sum, rate_sum, inlet_sum])
        return (
            result.reshape(block_input.shape), grad_input.reshape(block_input.shape), s_one, gate_sum, input_sum,
            s_taps, s_bias, rate_sum, s_rate, inlet_sum, s_inlet, s_decay, out_sum, s_two, up_sum, value_sum, down_sum,
        )

    sp = jax.nn.softplus(-decay_param.astype(F32))
    heads_shape = (heads, hb, hb)
    wr, wl = w_rate.reshape(heads_shape), w_inlet.reshape(heads_shape)
    wg, wi = wgi[:, :chans], wgi[:, chans:]
    ffl = w_down.shape[0]
    own = jnp.concatenate([lax.dynamic_slice_in_dim(w, fi * ffl, ffl, 1) for w in (w_up, w_value)], 1)
    wuv = lax.dynamic_update_slice_in_dim(wuv, own, fi * (width // n_fs), 0)
    wu, wv = wuv[:, :ffl], wuv[:, ffl:]
    gain_one, gain_two = gain[:, 0].reshape(-1), gain[:, 1].reshape(-1)
    s1 = lax.rsqrt(jnp.mean(x * x, axis=-1, keepdims=True) + EPS_NORM)
    s2 = lax.rsqrt(jnp.mean(middle * middle, axis=-1, keepdims=True) + EPS_NORM)
    tok = lambda v: v.reshape(-1, rows, chans).swapaxes(0, 1)
    padded, clf, r, i, decay, states = tok(pad_tm), tok(conv_tm), tok(rate_tm), tok(inlet_tm), tok(decay_tm), tok(states_tm)
    conv_low, clf = clf, clf.astype(F32)
    heads_in = conv_low.reshape(rows * toks, heads, hb)
    gate_pre = tok(gate_tm).reshape(-1, chans)
    gg, gd = gelu_pair(gate_pre)
    cum_end, state_in = ends[:8], ends[16:24]
    prev = jnp.concatenate([state_in[:, None], states[:, :-1]], axis=1)
    ld = -RATE_SCALE * r * sp
    factor = jnp.sqrt(EPS_MULT - jnp.expm1(2.0 * ld))
    up = mm(n2, wu)
    value = mm(n2, wv)
    vg, vd = gelu_pair(value)
    hidden = (vg * up).astype(BF)
    result = middle + rs(mm(hidden, w_down))
    grad_out = jnp.where(mask, result - teacher.reshape(here, width), 0.0) * (slots / count)
    gdi = ag(grad_out.astype(BF))
    g_down = mm_lt(hidden, gdi)
    gh = mm_rt(gdi, w_down)
    gu = (gh * vg).astype(BF)
    gv = (gh * up * vd).astype(BF)
    g_up = mm_lt(n2, gu)
    g_value = mm_lt(n2, gv)
    gn2 = rs(mm_rt(gu, wu) + mm_rt(gv, wv))
    gm_norm, gain2 = rms_back(middle, s2, gain_two, gn2)
    grad_middle = grad_out + gm_norm
    gml = ag(grad_middle.astype(BF))
    g_out = mm_lt(merged, gml)
    gmer = mm_rt(gml, w_out)
    gst = (gmer * gg).reshape(rows, toks, chans)
    ggate = (gmer * states.reshape(-1, chans) * gd).astype(BF)
    nextd = jnp.concatenate([decay[:, 1:], jnp.ones((rows, 1, chans), F32)], axis=1)
    carry, ladj = lax.associative_scan(linear_step, (nextd, gst), axis=1, reverse=True)
    tot2 = lax.all_gather(jnp.stack([cum_end, decay[:, 0] * ladj[:, 0]]), "seq")
    adj_in = jnp.zeros((rows, chans), F32)
    for j in reversed(range(n_seq)):
        adj_in = jnp.where(j > si, tot2[j, 0] * adj_in + tot2[j, 1], adj_in)
    adj = ladj + carry * adj_in[:, None]
    gdec = adj * prev
    gfac = adj * i * clf
    gld = gdec * decay - gfac * (decay * decay) / factor
    grate = gld * (-RATE_SCALE * sp) * r * (1.0 - r)
    ginl = adj * factor * clf * i * (1.0 - i)
    gdp = jnp.sum(gld * r, axis=(0, 1)) * RATE_SCALE * jax.nn.sigmoid(-decay_param.astype(F32))
    gcd = adj * factor * i
    grb, gib = jnp.sum(grate, (0, 1)), jnp.sum(ginl, (0, 1))
    grl, gil = grate.astype(BF).reshape(-1, heads, hb), ginl.astype(BF).reshape(-1, heads, hb)
    gwr = jnp.einsum("nhi,nhj->hij", heads_in, grl, preferred_element_type=F32).reshape(chans, hb)
    gwi = jnp.einsum("nhi,nhj->hij", heads_in, gil, preferred_element_type=F32).reshape(chans, hb)
    bk = lambda a, w: jnp.einsum("nhj,hij->nhi", a, w, preferred_element_type=F32).reshape(rows, toks, chans)
    gconv = gcd + bk(grl, wr) + bk(gil, wl)
    gcw = jnp.stack([jnp.sum(gconv * padded[:, taps - 1 - k: taps - 1 - k + toks], (0, 1)) for k in range(taps)])
    gcb = jnp.sum(gconv, (0, 1))
    gpad = jnp.zeros((rows, toks + taps - 1, chans), F32)
    for k in range(taps):
        gpad = gpad.at[:, taps - 1 - k: taps - 1 - k + toks].add(cw[k] * gconv)
    edge = shifted(gpad[:, : taps - 1], "seq", -1)
    gbr = gpad[:, taps - 1:].at[:, toks - (taps - 1):].add(edge).reshape(-1, chans).astype(BF)
    g_gate = mm_lt(normed, ggate)
    g_input = mm_lt(normed, gbr)
    gn1 = rs(mm_rt(ggate, wg) + mm_rt(gbr, wi))
    gi_norm, gain1 = rms_back(x, s1, gain_one, gn1)
    grad_input = grad_middle + gi_norm

    chan = jnp.concatenate([gcw, gcb[None], grb[None], gib[None], gdp[None]], 0)
    per = chans // n_seq
    chan = chan.reshape(8, n_seq, per).transpose(1, 0, 2).reshape(n_seq, 8 * per)
    blk = jnp.zeros((n_fs, n_seq, 8 * per), F32).at[fi].set(chan).reshape(n_fs * n_seq, 8 * per)
    gw = jnp.stack([gain1, gain2]).reshape(2, n_fs * n_seq, -1).transpose(1, 0, 2).reshape(n_fs * n_seq, -1)
    small = lax.psum_scatter(jnp.concatenate([blk, gw], 1), BOTH, scatter_dimension=0, tiled=True)[0]
    ch = small[: 8 * per].reshape(8, per)
    gn = small[8 * per:].reshape(2, -1)
    og = grads_rows(jnp.concatenate([g_out, gwr, gwi], 1))
    return (
        result.reshape(block_input.shape), grad_input.reshape(block_input.shape), gn[0],
        grads_cols(g_gate), grads_cols(g_input), ch[:4], ch[4], og[:, width: width + hb], ch[5],
        og[:, width + hb:], ch[6], ch[7], og[:, :width], gn[1], grads_cols(g_up), grads_cols(g_value), grads_rows(g_down),
    )


def solution(mesh):
    rowsh, vec, mat = P("fsdp", "seq", None), P("fsdp"), P("fsdp", None)
    ov, om = P(BOTH), P(BOTH, None)
    return jax.shard_map(
        body,
        mesh=mesh,
        in_specs=(rowsh, rowsh, P(), vec, mat, mat, P(None, "fsdp"), vec, mat, vec, mat, vec, vec, mat, vec, mat, mat, mat),
        out_specs=(rowsh, rowsh, ov, om, om, P(None, BOTH), ov, om, ov, om, ov, ov, om, ov, om, om, om),
        check_vma=False,
    )
```

```python
import jax
import jax.numpy as jnp
from jax import lax
from jax.sharding import PartitionSpec as P
from jax.experimental import pallas as pl
from jax.experimental.pallas import tpu as pltpu

EPS_NORM = 1e-06
EPS_MULT = 0.0001
RATE_SCALE = 8.0
BF = jnp.bfloat16
F32 = jnp.float32
GROUP = "fsdp"
BOTH = ("seq", "fsdp")


def mm(left, right):
    return jnp.dot(left, right, preferred_element_type=F32)


def mm_lt(left, right):
    return lax.dot_general(left, right, (((0,), (0,)), ((), ())), preferred_element_type=F32)


def mm_rt(left, right):
    return lax.dot_general(left, right, (((1,), (1,)), ((), ())), preferred_element_type=F32)


def gelu_pair(v):
    c = 0.7978845608028654
    a = 0.044715
    u = c * (v + a * v * v * v)
    t = jnp.tanh(u)
    g = 0.5 * v * (1.0 + t)
    d = 0.5 * (1.0 + t) + 0.5 * v * (1.0 - t * t) * c * (1.0 + 3.0 * a * v * v)
    return g, d


def linear_step(first_pair, second_pair):
    return (first_pair[0] * second_pair[0], second_pair[1] + second_pair[0] * first_pair[1])


def rms(v, g):
    s = lax.rsqrt(jnp.mean(v * v, axis=-1, keepdims=True) + EPS_NORM)
    return (v * s * g).astype(BF), s


def rms_back(v, s, g, grad):
    gg = grad * g
    gain = jnp.sum(grad * v * s, axis=0)
    return s * gg - v * (s * s * s) * jnp.mean(gg * v, axis=-1, keepdims=True), gain


def ag(a):
    return lax.all_gather(a, GROUP, axis=0, tiled=True)


def rs(a):
    return lax.psum_scatter(a.astype(BF), GROUP, scatter_dimension=0, tiled=True).astype(F32)


def grads_cols(g):
    part = lax.psum_scatter(g.astype(BF), "seq", scatter_dimension=0, tiled=True)
    return lax.all_to_all(part, GROUP, split_axis=0, concat_axis=1, tiled=True).astype(F32)


def grads_rows(g):
    n, m = lax.axis_size("seq"), lax.axis_size(GROUP)
    part = lax.psum_scatter(g.astype(BF), "seq", scatter_dimension=0, tiled=True)
    pairs = [(j * m + f, f * n + j) for j in range(n) for f in range(m)]
    return lax.ppermute(part, BOTH, pairs).astype(F32)


def shifted(shard, axis, by):
    length = lax.axis_size(axis)
    pairs = [(i, i + by) for i in range(length) if 0 <= i + by < length]
    return lax.ppermute(shard, axis, pairs)


MESH = pl.DeviceIdType.MESH
VMEM = pl.BlockSpec(memory_space=pltpu.VMEM)
ANY = pl.BlockSpec(memory_space=pl.ANY)
LIMIT = 63 * 2**20


def ds(start, size):
    if not isinstance(start, int):
        start = pl.multiple_of(start, size if size % 128 else 128)
    return pl.ds(start, size)


def rows_at(block, size):
    return pl.ds(pl.multiple_of(block * size, size), size)


class Place:
    def __init__(self):
        self.n = lax.axis_size("seq")
        self.s, self.f = lax.axis_index("seq"), lax.axis_index("fsdp")
        f = self.f
        self.p1 = f + 1 - 2 * lax.rem(f, 2)
        self.p2 = lax.rem(f + 2, 4)
        self.p3 = lax.rem(self.p1 + 2, 4)
        self.sx = self.s + 1 - 2 * lax.rem(self.s, 2)

    def group(self, f):
        return (self.s, f)

    def line(self, s):
        return (s, self.f)

    def greet(self, hop=None):
        barrier = pltpu.get_barrier_semaphore()
        for f in (self.p1, self.p2, self.p3):
            pl.semaphore_signal(barrier, inc=1, device_id=self.group(f), device_id_type=MESH)

        def one(j, _):
            pl.semaphore_signal(
                barrier, inc=1, device_id=self.line(lax.rem(self.s + j, self.n)), device_id_type=MESH
            )
            return 0

        lax.fori_loop(1, self.n, one, 0)
        pl.semaphore_wait(barrier, 3 + self.n - 1 + (0 if hop is None else hop.greet(barrier)))


class Sems:
    def __init__(self, ref):
        self.ref, self.used = ref, 0

    def take(self):
        self.used += 1
        return self.ref.at[self.used - 1]

    def remote(self, src, dst, device):
        return pltpu.make_async_remote_copy(
            src_ref=src, dst_ref=dst, send_sem=self.take(), recv_sem=self.take(),
            device_id=device, device_id_type=MESH,
        )

    def local(self, src, dst):
        copy = pltpu.make_async_copy(src, dst, self.take())
        copy.start()
        return copy


class Gather:
    def __init__(self, at, sems, buf, chunk):
        self.at, self.buf, self.chunk = at, buf, chunk
        mine = lambda f, r: buf.at[rows_at(f * 2 + r, chunk)]
        self.core = [sems.remote(mine(at.f, r), mine(at.f, r), at.group(at.p1)) for r in range(2)]
        self.over = [sems.remote(mine(at.f, r), mine(at.f, r), at.group(at.p2)) for r in range(2)]
        self.pass_on = [sems.remote(mine(at.p2, r), mine(at.p2, r), at.group(at.p1)) for r in range(2)]

    def send(self, r):
        self.over[r].start()
        self.core[r].start()

    def relay(self, r):
        self.over[r].wait_recv()
        self.pass_on[r].start()

    def near(self):
        for r in range(2):
            self.core[r].wait_recv()

    def finish(self):
        for r in range(2):
            self.core[r].wait_send()
            self.over[r].wait_send()
            self.pass_on[r].wait()


class Scatter:
    def __init__(self, at, sems, core_out, core_in, over_out, over_in, chunk):
        self.at, self.chunk = at, chunk
        self.core_out, self.core_in, self.over_out, self.over_in = core_out, core_in, over_out, over_in
        self.core = [sems.remote(core_out.at[k], core_in.at[k], at.group(at.p1)) for k in range(2)]
        self.over = [
            sems.remote(
                over_out.at[pl.ds(r * chunk, chunk)], over_in.at[pl.ds(r * chunk, chunk)], at.group(at.p2)
            )
            for r in range(2)
        ]

    def run(self, partial, own, between=lambda k: None):
        at = self.at

        def put(ref):
            def store(sl, cols, tile):
                ref[sl, cols] = tile.astype(BF)

            return store

        partial(at.p3, put(self.core_out.at[0]))
        self.core[0].start()
        between(0)

        def add_over(sl, cols, tile):
            self.over_out[sl, cols] = (tile + self.core_in[0, sl, cols].astype(F32)).astype(BF)

        self.core[0].wait_recv()
        partial(at.p2, add_over)
        self.over[0].start()
        between(1)
        partial(at.p1, put(self.core_out.at[1]))
        self.core[1].start()
        between(2)
        self.core[1].wait_recv()

        def add_own(sl, cols, tile):
            own[sl, cols] = own[sl, cols] + tile + self.core_in[1, sl, cols].astype(F32)

        partial(at.f, add_own)
        between(3)

    def run_tile(self, compute, tile, own, between=lambda k: None):
        at = self.at

        def one(k, _):
            compute(jnp.where(k == 0, at.p3, jnp.where(k == 1, at.p2, jnp.where(k == 2, at.p1, at.f))))

            @pl.when(k == 0)
            def _():
                self.core_out[0] = tile[...].astype(BF)
                self.core[0].start()

            @pl.when(k == 1)
            def _():
                self.core[0].wait_recv()
                for r in range(2):
                    sl = pl.ds(r * self.chunk, self.chunk)
                    self.over_out[sl, :] = (tile[sl, :] + self.core_in[0, sl, :].astype(F32)).astype(BF)
                self.over[0].start()

            @pl.when(k == 2)
            def _():
                self.core_out[1] = tile[...].astype(BF)
                self.core[1].start()

            @pl.when(k == 3)
            def _():
                self.core[1].wait_recv()
                if own is None:
                    tile[...] = tile[...] + self.core_in[1].astype(F32)
                else:
                    own[...] = own[...] + tile[...] + self.core_in[1].astype(F32)

            between(k)
            return 0

        lax.fori_loop(0, 4, one, 0)

    def second(self):
        self.over[0].wait_send()
        self.over[1].start()

    def arrived(self, r):
        self.over[r].wait_recv()
        return self.over_in[pl.ds(r * self.chunk, self.chunk), :].astype(F32)

    def finish(self):
        for copy in self.core + self.over[1:]:
            copy.wait_send()


class Columns:
    def __init__(self, at, sems, weights, buf, with_own=True, first=0):
        rows, width = weights[0].shape
        part = width // 4
        cut = rows // 4
        h = lax.rem(at.s, 4)
        one = h + 1 - 2 * lax.rem(h, 2)
        mates = [at.line(at.s - h + m) for m in (one, lax.rem(h + 2, 4), lax.rem(one + 2, 4))]
        self.near, self.own, self.far, self.side = [], [], [], []
        for k, w in enumerate(weights):
            cols = pl.ds(first + k * part, part)
            take = lambda f: pl.ds(pl.multiple_of(f * part, 128), part)
            mine = pl.ds(pl.multiple_of(at.f * rows, rows), rows)
            quarter = pl.ds(pl.multiple_of(h * cut, cut), cut)
            mine_cut = pl.ds(pl.multiple_of(at.f * rows + h * cut, cut), cut)
            if with_own:
                self.own.append(pltpu.make_async_copy(w.at[:, take(at.f)], buf.at[mine, cols], sems.take()))
            self.near.append(sems.remote(w.at[:, take(at.p1)], buf.at[mine, cols], at.group(at.p1)))
            for p in (at.p2, at.p3):
                self.far.append(sems.remote(w.at[quarter, take(p)], buf.at[mine_cut, cols], at.group(p)))
                came = buf.at[pl.ds(pl.multiple_of(p * rows + h * cut, cut), cut), cols]
                self.side.append([sems.remote(came, came, mate) for mate in mates])

    def start_far(self, first=0, end=4):
        for c in self.far[first:end]:
            c.start()

    def start_near(self):
        for c in self.near + self.own:
            c.start()

    def relay(self, k):
        self.far[k].wait_recv()
        for c in self.side[k]:
            c.start()

    def finish(self):
        for c in self.own + self.near + sum(self.side, []):
            c.wait()
        for c in self.far:
            c.wait_send()


def expm1_neg(v):
    series = v * (1 + v * (1 / 2) * (1 + v * (1 / 3) * (1 + v * (1 / 4) * (1 + v * (1 / 5) * (1 + v * (1 / 6))))))
    return jnp.where(v > -0.25, series, jnp.exp(v) - 1.0)


def decay_rows(param):
    small = jnp.exp(-jnp.abs(param))
    return (
        -RATE_SCALE * (jnp.maximum(-param, 0.0) + jnp.log1p(small)),
        RATE_SCALE * jnp.where(param > 0.0, small, 1.0) / (1.0 + small),
    )


def whole_gain(gain, row):
    return jnp.concatenate([gain[p, row : row + 1, :] for p in range(4)], axis=1)


def swap_rows(src, dst, outer, kind):
    total, width = src.shape
    inner = total // outer

    def one(c, _):
        cols = pl.ds(pl.multiple_of(c * 128, 128), 128)
        v = src[:, cols].reshape(outer, inner, 128)
        dst[:, cols] = jnp.swapaxes(v, 0, 1).reshape(total, 128).astype(kind)
        return 0

    lax.fori_loop(0, width // 128, one, 0)


def forward_branch(x_h, gain_one, gain_two, taps_w, conv_b, rate_b, inlet_b, decay_p, wr, wl, wo_h, wg, wi, wu, wv,
                   wgi_o, wuv_o, normed_o, n2_o, middle_o, gate_o, pad_o, conv_o, rate_o, inlet_o, decay_o, states_o,
                   merged_o, ends_o, gain_o, chan_o,
                   wo, wgi, normed, n2, middle, gains, chan, gain, gate, pad, conv, rate, inlet, decay, states, work, hold, merged, ends,
                   tot, core_out, core_in, over_out, over_in, sem, tsend, trecv):
    at = Place()
    here, width = middle.shape
    toks = here // 2
    chans = chan.shape[1]
    part = width // 4
    taps = 4
    steps = toks
    group = 8
    halo = (taps - 1) * group
    sems = Sems(sem)
    x, first = middle, sems.local(x_h, middle)
    late = sems.local(wo_h, wo)
    chan[0:taps, :] = taps_w[...].astype(F32)
    for row, v in enumerate((conv_b, rate_b, inlet_b, decay_p)):
        chan[taps + row : taps + row + 1, :] = v[...].astype(F32).reshape(1, chans)
    for row, v in enumerate((gain_one, gain_two)):
        gains[row : row + 1, :] = v[...].astype(F32).reshape(1, part)
    gains[2:8, :] = jnp.zeros((6, part), F32)
    at.greet()

    shares = [
        sems.remote(gains, gain.at[at.f], at.group(p)) for p in (at.p1, at.p2, at.p3)
    ]
    for c in shares:
        c.start()
    gain[at.f] = gains[...]
    ci = Columns(at, sems, [wi], wgi, True, chans)
    ci.start_far()
    ci.start_near()
    cg = Columns(at, sems, [wg], wgi)
    cg.start_near()
    uv = Columns(at, sems, [wu, wv], wuv_o, False)
    uv.start_near()
    ag1 = Gather(at, sems, normed, toks)
    first.wait()
    scales = []
    for r in range(2):
        v = x[pl.ds(r * toks, toks), :]
        scales.append(lax.rsqrt(jnp.mean(v * v, axis=-1, keepdims=True) + EPS_NORM))
    for c in shares:
        c.wait()
    for r in range(2):
        sl = pl.ds(r * toks, toks)
        scale = scales[r]
        for p in range(4):
            cols = pl.ds(p * part, part)
            normed[rows_at(at.f * 2 + r, toks), cols] = (x[sl, cols] * scale * gain[p, 0:1, :]).astype(BF)
        ag1.send(r)
    for k in range(2):
        ci.relay(k)
    ag1.relay(0)
    cg.start_far()
    uv.start_far(0, 2)
    ag1.relay(1)
    ag1.near()
    ag1.finish()
    ci.finish()
    saves = [sems.local(normed, normed_o), sems.local(gain, gain_o), sems.local(chan, chan_o)]

    def branch_rows(m, _):
        sl = rows_at(m, here)
        work[sl, :] = mm(normed[sl, :], wgi[:, chans:]).astype(BF).astype(F32)
        return 0

    lax.fori_loop(0, 4, branch_rows, 0)
    swap_rows(work, pad.at[pl.ds(halo, steps * group)], group, F32)
    edge = pad.at[pl.ds(steps * group, halo)]
    next_one = lax.rem(at.s + 1, at.n)
    tail = sems.remote(edge, pad.at[pl.ds(0, halo)], at.line(next_one))

    @pl.when(at.s < at.n - 1)
    def _():
        tail.start()

    @pl.when(at.s == 0)
    def _():
        pad[0:halo, :] = jnp.zeros((halo, chans), F32)

    for k in range(2):
        cg.relay(k)
    uv.start_far(2, 4)

    ends[16:17, :] = decay_rows(chan[7:8, :])[0]

    def gates(b, _):
        for h in range(chans // 128):
            cols = pl.ds(h * 128, 128)
            size = 128
            start = pl.multiple_of(b * size, size)
            sl = pl.ds(start, size)
            total = chan[taps : taps + 1, cols]
            for k in range(taps):
                total = total + chan[k : k + 1, cols] * pad[pl.ds(start + (halo - group * k), size), cols]
            low = total.astype(BF)
            blocks = pl.ds(h * 128, 128)
            r = jax.nn.sigmoid(mm(low, wr[blocks, :]) + chan[5:6, cols])
            i = jax.nn.sigmoid(mm(low, wl[blocks, :]) + chan[6:7, cols])
            ld = r * ends[16:17, cols]
            conv[sl, cols] = low
            low = low.astype(F32)
            decay[sl, cols] = jnp.exp(ld)
            work[sl, cols] = jnp.sqrt(EPS_MULT - expm1_neg(2.0 * ld)) * i * low
            rate[sl, cols] = r
            inlet[sl, cols] = i
        return 0

    lax.fori_loop(1, steps * group // 128, gates, 0)

    @pl.when(at.s > 0)
    def _():
        tail.wait_recv()

    @pl.when(at.s < at.n - 1)
    def _():
        tail.wait_send()


    gates(0, 0)
    saves += [
        sems.local(pad, pad_o), sems.local(conv, conv_o), sems.local(rate, rate_o),
        sems.local(inlet, inlet_o), sems.local(decay, decay_o),
    ]

    unroll = 8

    def totals(b, carry):
        h, p = carry
        for u in range(unroll):
            sl = pl.ds(pl.multiple_of((b * unroll + u) * group, group), group)
            a = decay[sl, :]
            h = a * h + work[sl, :]
            p = p * a
        return h, p

    zero = jnp.zeros((group, chans), F32)
    h, p = lax.fori_loop(0, steps // unroll, totals, (zero, zero + 1.0))
    ends[0:8, :] = p
    ends[8:16, :] = h

    def total_copy(src, to):
        return pltpu.make_async_remote_copy(
            src_ref=ends.at[pl.ds(0, 16)], dst_ref=tot.at[src], send_sem=tsend.at[to], recv_sem=trecv.at[src],
            device_id=at.line(to), device_id_type=MESH,
        )

    def send_total(j, _):
        total_copy(at.s, j).start()
        return 0

    lax.fori_loop(at.s + 1, at.n, send_total, 0)
    cg.finish()
    saves.append(sems.local(wgi, wgi_o))

    def gate_rows(m, _):
        sl = rows_at(m, here)
        hold[sl, :] = mm(normed[sl, :], wgi[:, :chans])
        return 0

    lax.fori_loop(0, 4, gate_rows, 0)
    swap_rows(hold, gate, group, F32)

    saves.append(sems.local(gate, gate_o))

    def enter(j, state):
        total_copy(j, j).wait_recv()
        return tot[j, 0:8, :] * state + tot[j, 8:16, :]

    state_in = lax.fori_loop(0, at.s, enter, zero)

    def sent_total(j, _):
        total_copy(at.s, j).wait_send()
        return 0

    lax.fori_loop(at.s + 1, at.n, sent_total, 0)
    uv.relay(0)
    uv.relay(1)
    ends[16:24, :] = state_in

    def scan(b, h):
        for u in range(unroll):
            sl = pl.ds(pl.multiple_of((b * unroll + u) * group, group), group)
            h = decay[sl, :] * h + work[sl, :]
            states[sl, :] = h
        return h

    lax.fori_loop(0, steps // unroll, scan, state_in)
    saves += [sems.local(states, states_o), sems.local(ends, ends_o)]

    def merge(c, _):
        cols = pl.ds(pl.multiple_of(c * 128, 128), 128)

        def some(b, _):
            sl = rows_at(b, 128)
            work[sl, cols] = states[sl, cols] * gelu_pair(gate[sl, cols])[0]
            return 0

        lax.fori_loop(0, steps * group // 128, some, 0)
        return 0

    lax.fori_loop(0, chans // 128, merge, 0)
    swap_rows(work, merged, steps, BF)
    saves += [sems.local(merged, merged_o)]

    late.wait()
    sc = Scatter(at, sems, core_out, core_in, over_out, over_in, toks)

    def partial(o, store):
        def half(r, _):
            sl = rows_at(r, toks)
            tile = mm(merged[rows_at(o * 2 + r, toks), :], wo[...])
            store(sl, slice(None), tile)
            return 0

        lax.fori_loop(0, 2, half, 0)

    def between(k):
        if k == 2:
            uv.relay(2)
            uv.relay(3)

    sc.run(partial, middle, between)
    sc.second()
    ag2 = Gather(at, sems, n2, toks)
    for r in range(2):
        sl = pl.ds(r * toks, toks)
        v = middle[sl, :] + sc.arrived(r)
        middle[sl, :] = v
        scale = lax.rsqrt(jnp.mean(v * v, axis=-1, keepdims=True) + EPS_NORM)
        for p in range(4):
            cols = pl.ds(p * part, part)
            n2[rows_at(at.f * 2 + r, toks), cols] = (middle[sl, cols] * scale * gain[p, 1:2, :]).astype(BF)
        ag2.send(r)
    saves += [sems.local(middle, middle_o)]
    for r in range(2):
        ag2.relay(r)
    ag2.near()
    ag2.finish()
    sc.finish()
    saves += [sems.local(n2, n2_o)]
    uv.finish()
    for c in saves:
        c.wait()


def call_forward(x, gain_one, gain_two, taps_w, conv_b, rate_b, inlet_b, decay_p, wr, wl, wo, wg, wi, wu, wv):
    here, width = x.shape
    chans = taps_w.shape[1]
    ffl = wu.shape[1] // 4
    every = here * 4
    n = lax.axis_size("seq")
    f32 = lambda *s: jax.ShapeDtypeStruct(s, F32)
    bf = lambda *s: jax.ShapeDtypeStruct(s, BF)
    vf = lambda *s: pltpu.VMEM(s, F32)
    vb = lambda *s: pltpu.VMEM(s, BF)
    outs = [
        bf(width, 2 * chans), bf(width, 2 * ffl), bf(every, width), bf(every, width), f32(here, width),
        f32(every, chans), f32(every + 24, chans), bf(every, chans), f32(every, chans), f32(every, chans),
        f32(every, chans), f32(every, chans), bf(every, chans), f32(24, chans), f32(4, 8, width // 4), f32(8, chans),
    ]
    scratch = [
        vb(chans, width), vb(width, 2 * chans), vb(every, width), vb(every, width), vf(here, width), vf(8, width // 4), vf(8, chans), vf(4, 8, width // 4),
        vf(every, chans), vf(every + 24, chans), vb(every, chans), vf(every, chans), vf(every, chans),
        vf(every, chans), vf(every, chans), vf(every, chans), vf(every, chans), vb(every, chans), vf(24, chans),
        vf(n, 16, chans), vb(2, here, width), vb(2, here, width), vb(here, width), vb(here, width),
        pltpu.SemaphoreType.DMA((170,)), pltpu.SemaphoreType.DMA((n,)), pltpu.SemaphoreType.DMA((n,)),
    ]
    return pl.pallas_call(
        forward_branch,
        out_shape=outs,
        in_specs=[ANY] + [VMEM] * 9 + [ANY] * 5,
        out_specs=[ANY] * len(outs),
        scratch_shapes=scratch,
        compiler_params=pltpu.CompilerParams(collective_id=1, has_side_effects=True, vmem_limit_bytes=LIMIT),
        name="forward_branch",
    )(x, gain_one, gain_two, taps_w, conv_b, rate_b, inlet_b, decay_p, wr, wl, wo, wg, wi, wu, wv)


class Hop:
    def __init__(self, at):
        b = at.f * at.n + at.s
        self.to = (lax.div(b, 4), lax.rem(b, 4))
        c = at.s * 4 + at.f
        self.source = (lax.rem(c, at.n), lax.div(c, at.n))
        self.stays = b == c

    def greet(self, barrier):
        @pl.when(jnp.logical_not(self.stays))
        def _():
            for device in (self.to, self.source):
                pl.semaphore_signal(barrier, inc=1, device_id=device, device_id_type=MESH)

        return jnp.where(self.stays, 0, 2)

    def start(self, sems, src, dst):
        far = sems.remote(src, dst, self.to)
        near = pltpu.make_async_copy(src, dst, sems.take())

        @pl.when(self.stays)
        def _():
            near.start()

        @pl.when(jnp.logical_not(self.stays))
        def _():
            far.start()

        return near, far

    def wait(self, pair):
        near, far = pair

        @pl.when(self.stays)
        def _():
            near.wait()

        @pl.when(jnp.logical_not(self.stays))
        def _():
            far.wait()


class Ring:
    def __init__(self, at, grads, slots, send, recv, by_rows):
        self.at, self.grads, self.slots, self.sem, self.rem = at, grads, slots, send, recv
        n = at.n
        self.q = self.place(at.s)
        rows, width = slots.shape[1:]
        self.rows = rows
        if by_rows:
            self.cut = [(pl.ds(i * rows // 4, rows // 4), pl.ds(0, width)) for i in range(4)]
        else:
            self.cut = [(pl.ds(0, rows), pl.ds(i * width // 4, width // 4)) for i in range(4)]
        self.way = (1, -1, 1, -1)
        self.to = {w: at.line(self.owner(lax.rem(self.q + w + n, n))) for w in (1, -1)}

    def place(self, s):
        half = lax.div(s, 2)
        return jnp.where(lax.rem(s, 2) == 0, half, self.at.n - 1 - half)

    def owner(self, q):
        n = self.at.n
        return jnp.where(q < n // 2, 2 * q, 2 * (n - 1 - q) + 1)

    def block(self, i, behind):
        n = self.at.n
        s = self.owner(lax.rem(self.q - self.way[i] * behind + 2 * n, n))
        r, c = self.cut[i]
        return self.grads.at[pl.ds(pl.multiple_of(s * self.rows + r.start, 16), r.size), c]

    def copy(self, i, k, src):
        r, c = self.cut[i]
        return pltpu.make_async_remote_copy(
            src_ref=src, dst_ref=self.slots.at[k, r, c], send_sem=self.sem.at[i, k], recv_sem=self.rem.at[i, k],
            device_id=self.to[self.way[i]], device_id_type=MESH,
        )

    def start(self):
        for i in range(4):
            self.copy(i, 0, self.block(i, 1)).start()

    def summed(self, i, k):
        r, c = self.cut[i]
        slot = self.slots.at[k, r, c]
        self.copy(i, k, slot).wait_recv()
        return slot, slot[...].astype(F32) + self.block(i, k + 2)[...].astype(F32)

    def step(self, k):
        for i in range(4):
            slot, value = self.summed(i, k)
            slot[...] = value.astype(BF)
            self.copy(i, k + 1, slot).start()

    def last(self, out, store=None):
        k = self.at.n - 2
        for i in range(4):
            _, value = self.summed(i, k)
            if store is None:
                out[self.cut[i]] = value.astype(out.dtype)
            else:
                store(i, value)

    def finish(self):
        def one(k, _):
            for i in range(4):
                r, c = self.cut[i]
                self.copy(i, k, self.slots.at[k, r, c]).wait_send()
            return 0

        lax.fori_loop(0, self.at.n - 1, one, 0)


class Regroup:
    def __init__(self, at, sems, src, dst, parts=None):
        size = src.shape[0] // at.n
        self.far, self.near = [], []
        for h in parts or range(at.n // 4):
            slot = dst.at[pl.ds(pl.multiple_of((at.f * (at.n // 4) + h) * size, 16), size)]
            block = lambda p: src.at[pl.ds(pl.multiple_of((p + 4 * h) * size, 16), size)]
            for p in (at.p2, at.p3, at.p1):
                self.far.append(sems.remote(block(p), slot, at.group(p)))
            self.near.append(pltpu.make_async_copy(block(at.f), slot, sems.take()))

    def start(self):
        for c in self.far + self.near:
            c.start()

    def wait(self):
        for c in self.far + self.near:
            c.wait()


class Spread:
    def __init__(self, at, sems, src, came):
        self.at, self.src, self.came = at, src, came
        rows = came.shape[1]
        send, recv = [sems.take() for _ in range(4)], [sems.take() for _ in range(4)]
        self.copies = []
        for k in range(1, 4):
            to = lax.rem(at.f + k, 4)
            piece = src.at[pl.ds(pl.multiple_of(to * rows, 16), rows)]
            self.copies.append(
                pltpu.make_async_remote_copy(
                    src_ref=piece, dst_ref=came.at[at.f], send_sem=send[k], recv_sem=recv[k],
                    device_id=at.group(to), device_id_type=MESH,
                )
            )

    def start(self):
        rows = self.came.shape[1]
        for c in self.copies:
            c.start()
        self.came[self.at.f] = self.src[pl.ds(pl.multiple_of(self.at.f * rows, 16), rows), :]

    def wait(self):
        for c in self.copies:
            c.wait()


def mlp(n2_h, wuv_h, wu_h, wv_h, wd_h, middle_h, teacher_h, lengths, gain,
        result_o, gmid_o, gml_o, gain_o, down_o, up_o, value_o,
        n2, wuv, wd, hidden, ge, gdi, gml, middle, own, gout, tile, core_out, core_in, over_out, over_in,
        gwd, gwu, gwv, acc_u, slots_u, last_u, gain_acc, sem, ring_sem):
    at = Place()
    sems = Sems(sem)
    here, width = middle.shape
    toks = here // 2
    ffl = hidden.shape[1]
    part = width // 4
    col = 384
    loads = [sems.local(n2_h, n2)]
    mine = pl.ds(pl.multiple_of(at.f * part, part), part)
    for k, w in enumerate((wu_h, wv_h)):
        cols = pl.ds(pl.multiple_of(at.f * ffl, 128), ffl)
        loads.append(sems.local(w.at[:, cols], wuv.at[mine, pl.ds(k * ffl, ffl)]))
    for p in (at.p1, at.p2, at.p3):
        rows = pl.ds(pl.multiple_of(p * part, part), part)
        loads.append(sems.local(wuv_h.at[rows], wuv.at[rows]))
    late = sems.local(wd_h, wd)
    loads2 = [sems.local(middle_h, middle), sems.local(middle_h, own), sems.local(teacher_h, gout)]
    at.greet()
    for c in loads:
        c.wait()

    def forward(o):
        sl = rows_at(o, here)

        def some(c, _):
            cols = pl.ds(pl.multiple_of(c * col, 128), col)
            cols2 = pl.ds(pl.multiple_of(c * col + ffl, 128), col)
            up = mm(n2[sl, :], wuv[:, cols])
            g, d = gelu_pair(mm(n2[sl, :], wuv[:, cols2]))
            hidden[sl, cols] = (g * up).astype(BF)
            ge[sl, cols] = g.astype(BF)
            ge[sl, cols2] = (up * d).astype(BF)
            return 0

        lax.fori_loop(0, ffl // col, some, 0)

        @pl.when(o == at.p3)
        def _():
            late.wait()

        def out(c, _):
            cols = pl.ds(pl.multiple_of(c * 512, 128), 512)
            tile[:, cols] = mm(hidden[sl, :], wd[:, cols])
            return 0

        lax.fori_loop(0, width // 512, out, 0)

    def hidden_rows(o):
        sl = rows_at(o, here)

        def some(c, _):
            cols = pl.ds(pl.multiple_of(c * col, 128), col)
            cols2 = pl.ds(pl.multiple_of(c * col + ffl, 128), col)
            gh = mm_rt(gdi[sl, :], wd[cols, :])
            ge[sl, cols] = (gh * ge[sl, cols].astype(F32)).astype(BF)
            ge[sl, cols2] = (gh * ge[sl, cols2].astype(F32)).astype(BF)
            return 0

        lax.fori_loop(0, ffl // col, some, 0)
        return 0

    sc = Scatter(at, sems, core_out, core_in, over_out, over_in, toks)

    def between(k):
        @pl.when(k == 2)
        def _():
            for c in loads2:
                c.wait()

    sc.run_tile(forward, tile, own, between)
    sc.second()
    count = lengths[0]
    for j in range(1, lengths.shape[0]):
        count = count + lengths[j]
    weight = (lengths.shape[0] * toks * at.n) / jnp.full((1, 1), count, jnp.int32).astype(F32)
    place = at.s * toks + lax.broadcasted_iota(jnp.int32, (toks, 1), 0)
    ag = Gather(at, sems, gdi, toks)
    for r in range(2):
        sl = pl.ds(r * toks, toks)
        v = own[sl, :] + sc.arrived(r)
        own[sl, :] = v
        v = jnp.where(place < lengths[at.f * 2 + r], v - gout[sl, :], 0.0) * weight
        gout[sl, :] = v
        gdi[rows_at(at.f * 2 + r, toks), :] = v.astype(BF)
        ag.send(r)
    saves = [sems.local(own, result_o)]
    ag.near()
    lax.fori_loop(0, 2, lambda k, _: hidden_rows(jnp.where(k == 0, at.f, at.p1)), 0)
    chip = pl.ds(pl.multiple_of(lax.div(at.f, 2) * 2 * here, 2 * here), 2 * here)
    other = pl.ds(pl.multiple_of((1 - lax.div(at.f, 2)) * 2 * here, 2 * here), 2 * here)
    pair = 2 * (width // at.n)

    def up_near(m, _):
        rows = pl.ds(pl.multiple_of(m * pair, 128), pair)
        acc_u[rows, :] = mm_lt(n2[chip, rows], ge[chip, 0:ffl])
        return 0

    lax.fori_loop(0, width // pair, up_near, 0)
    for r in range(2):
        ag.relay(r)
    ag.finish()
    sc.finish()
    saves.pop().wait()

    def down_rows(m, _):
        cols = pl.ds(pl.multiple_of(m * 128, 128), 128)
        gwd[rows_at(m, 128), :] = mm_lt(hidden[:, cols], gdi[...]).astype(BF)
        return 0

    def weight_rows(grads, first):
        def one(m, _):
            cols = pl.ds(pl.multiple_of(m * 256, 256), 256)
            grads[rows_at(m, 256), :] = mm_lt(n2[:, cols], ge[:, first : first + ffl]).astype(BF)
            return 0

        return one

    def backward(o):
        sl = rows_at(o, here)

        def out(c, _):
            cols = pl.ds(pl.multiple_of(c * 512, 128), 512)
            tile[:, cols] = mm_rt(ge[sl, :], wuv[cols, :])
            return 0

        lax.fori_loop(0, width // 512, out, 0)

    ring_u = Ring(at, gwu, slots_u, ring_sem.at[0], ring_sem.at[1], True)
    six = width // 256
    lax.fori_loop(0, 2, lambda k, _: hidden_rows(jnp.where(k == 0, at.p2, at.p3)), 0)
    def up_far(m):
        rows = pl.ds(pl.multiple_of(m * pair, 128), pair)
        gwu[rows, :] = (acc_u[rows, :] + mm_lt(n2[other, rows], ge[other, 0:ffl])).astype(BF)
        return 0

    sc2 = Scatter(at, sems, core_out, core_in, over_out, over_in, toks)

    def between(k):
        @pl.when(k == 1)
        def _():
            z = lax.div(at.s, 2)
            behind = lax.div(ring_u.owner(lax.rem(ring_u.q + at.n - 1, at.n)), 2)
            ahead = lax.div(ring_u.owner(lax.rem(ring_u.q + 1, at.n)), 2)
            lax.fori_loop(0, 2, lambda k, _: up_far(jnp.where(k == 0, behind, ahead)), 0)
            ring_u.start()
            at_end = jnp.logical_or(z == 0, z == 3)
            rest = lambda p: jnp.where(at_end, lax.rem(p + 2, 4), p + 1 - 2 * lax.rem(p, 2))
            lax.fori_loop(0, 2, lambda k, _: up_far(jnp.where(k == 0, rest(behind), rest(ahead))), 0)

        @pl.when(k == 3)
        def _():
            ring_u.step(0)

    sc2.run_tile(backward, tile, None, between)
    sc2.second()
    lax.fori_loop(0, six, weight_rows(gwv, ffl), 0)
    ring_u.step(1)
    lax.fori_loop(0, ffl // 128, down_rows, 0)
    ring_u.step(2)
    saves += [sems.local(gwv, value_o), sems.local(gwd, down_o)]
    ag2 = Gather(at, sems, gml, toks)
    acc = jnp.zeros((1, width), F32)
    for r in range(2):
        sl = pl.ds(r * toks, toks)
        g = tile[sl, :] + sc2.arrived(r)
        v = middle[sl, :]
        s = lax.rsqrt(jnp.mean(v * v, axis=-1, keepdims=True) + EPS_NORM)
        acc = acc + jnp.sum(g * v * s, axis=0, keepdims=True)
        gg = g * whole_gain(gain, 1)
        mean = jnp.mean(gg * v, axis=-1, keepdims=True)
        new = gout[sl, :] + s * gg - v * (s * s * s * mean)
        own[sl, :] = new
        gml[rows_at(at.f * 2 + r, toks), :] = new.astype(BF)
        ag2.send(r)
    gain_acc[...] = jnp.broadcast_to(acc, gain_acc.shape)
    saves += [sems.local(own, gmid_o), sems.local(gain_acc, gain_o)]
    ring_u.step(3)
    ring_u.step(4)
    ag2.relay(0)
    ring_u.step(5)
    ag2.relay(1)
    ring_u.last(last_u)
    saves += [sems.local(last_u, up_o)]
    ag2.near()
    saves += [sems.local(gml.at[chip], gml_o.at[chip])]
    ag2.finish()
    saves += [sems.local(gml.at[other], gml_o.at[other])]
    sc2.finish()
    ring_u.finish()
    for c in saves:
        c.wait()


def call_mlp(n2, wuv, wu, wv, wd, middle, teacher, lengths, gain):
    every, width = n2.shape
    here = middle.shape[0]
    ffl = wd.shape[0]
    n = lax.axis_size("seq")
    f32 = lambda *s: jax.ShapeDtypeStruct(s, F32)
    bf = lambda *s: jax.ShapeDtypeStruct(s, BF)
    vf = lambda *s: pltpu.VMEM(s, F32)
    vb = lambda *s: pltpu.VMEM(s, BF)
    outs = [
        f32(here, width), f32(here, width), bf(every, width), f32(8, width), bf(ffl, width),
        bf(width // n, ffl), bf(width, ffl),
    ]
    scratch = [
        vb(every, width), vb(width, 2 * ffl), vb(ffl, width), vb(every, ffl), vb(every, 2 * ffl), vb(every, width),
        vb(every, width), vf(here, width), vf(here, width), vf(here, width), vf(here, width),
        vb(2, here, width), vb(2, here, width), vb(here, width), vb(here, width),
        vb(ffl, width), vb(width, ffl), vb(width, ffl), vf(width, ffl), vb(n - 1, width // n, ffl),
        vb(width // n, ffl), vf(8, width),
        pltpu.SemaphoreType.DMA((100,)), pltpu.SemaphoreType.DMA((2, 4, n - 1)),
    ]
    return pl.pallas_call(
        mlp,
        out_shape=outs,
        in_specs=[ANY] * 7 + [pl.BlockSpec(memory_space=pltpu.SMEM), VMEM],
        out_specs=[ANY] * len(outs),
        scratch_shapes=scratch,
        compiler_params=pltpu.CompilerParams(collective_id=2, has_side_effects=True, vmem_limit_bytes=LIMIT),
        name="mlp",
    )(n2, wuv, wu, wv, wd, middle, teacher, lengths, gain)


class Line:
    def __init__(self, at, src, tot, send, recv):
        self.at, self.src, self.tot, self.send_sem, self.recv_sem = at, src, tot, send, recv

    def copy(self, slot, to):
        return pltpu.make_async_remote_copy(
            src_ref=self.src, dst_ref=self.tot.at[slot], send_sem=self.send_sem.at[to], recv_sem=self.recv_sem.at[slot],
            device_id=self.at.line(to), device_id_type=MESH,
        )

    def send(self, first, end):
        def one(j, _):
            @pl.when(j != self.at.s)
            def _():
                self.copy(self.at.s, j).start()

            return 0

        lax.fori_loop(first, end, one, 0)

    def sent(self, first, end):
        def one(j, _):
            @pl.when(j != self.at.s)
            def _():
                self.copy(self.at.s, j).wait_send()

            return 0

        lax.fori_loop(first, end, one, 0)

    def wait(self, j):
        self.copy(j, j).wait_recv()


def branch_back(chan_h, wr_h, wl_h, gain_h, gain2_h,
                gml_h, merged_h, wo_h, wgi_h, normed_h, gate_h, pad_h, conv_h, rate_h, inlet_h, decay_h, states_h, ends_h,
                gwd_h, x_h, gmid_h, up_h, value_h,
                ginput_o, up_o, value_o, down_o, gate_o, input_o, out_o, rate_o, inlet_o, chan_o, gains_o,
                chan, wr, wl, gain, gain2, gml, merged, wo, wgi, gate, pad, conv, rate, inlet, decay, states, ends, gwd, gwv, own,
                work, gconv, pair, heads_r, heads_l, acc, tile, core_in, over_out, over_in,
                go, ggi, slots_d, slots_v, slots_o, slots_g, last_u, came_u, came_v, go_own,
                passed, tot, small, small_in, small_sum, group_in, gains, slope8,
                sem, ring_sem, line_sem):
    at = Place()
    sems = Sems(sem)
    here, width = own.shape
    toks = here // 2
    chans = chan.shape[1]
    group, taps = 8, 4
    steps = toks
    every = steps * group
    halo = (taps - 1) * group
    n = at.n
    ffl = came_u.shape[2]
    early = [
        sems.local(value_h, gwv), sems.local(up_h, last_u), sems.local(gml_h, gml),
        sems.local(wo_h.at[pl.ds(0, here)], wo.at[0]), sems.local(wo_h.at[pl.ds(here, here)], wo.at[1]),
    ]
    second = [sems.local(gate_h, gate), sems.local(states_h, states.at[pl.ds(group, every)]), sems.local(ends_h, ends)]
    third = [sems.local(decay_h, decay), sems.local(merged_h, merged)]
    fourth = [
        sems.local(a, b)
        for a, b in ((pad_h, pad), (conv_h, conv), (rate_h, rate), (inlet_h, inlet), (wgi_h, wgi), (gmid_h, own))
    ]
    fourth += [
        sems.local(a, b)
        for a, b in ((chan_h, chan), (wr_h, wr), (wl_h, wl), (gain_h, gain), (gain2_h, gain2))
    ]
    hop = Hop(at)
    at.greet(hop)
    ring_d = Ring(at, gwd, slots_d, ring_sem.at[0], ring_sem.at[1], False)
    ring_v = Ring(at, gwv, slots_v, ring_sem.at[6], ring_sem.at[7], True)
    ring_o = Ring(at, go_own, slots_o, ring_sem.at[2], ring_sem.at[3], True)
    ring_g = Ring(at, ggi, slots_g, ring_sem.at[4], ring_sem.at[5], True)
    early[0].wait()
    ring_v.start()
    for c in early[1:]:
        c.wait()
    regroup = [Regroup(at, sems, gwd_h, gwd, part) for part in (range(n // 8), range(n // 8, n // 4))]
    spread_u = Spread(at, sems, last_u, came_u)
    spread_u.start()
    regroup[0].start()

    def staged(came, first, size, outs, base=0):
        rows = came.shape[1]
        for f in range(4):
            at_col = f * size
            done = 0
            while done < size:
                block, col = divmod(at_col + done, width)
                step = min(size - done, width - col)
                tile[base + block * rows : base + (block + 1) * rows, col : col + step] = came[
                    f, :, first + done : first + done + step
                ].astype(F32)
                done += step
        copies, done = [], 0
        while done < 4 * size:
            step = min(width, 4 * size - done)
            copies.append(
                sems.local(tile.at[pl.ds(base + done // width * rows, rows), pl.ds(0, step)], outs.at[:, pl.ds(done, step)])
            )
            done += step
        return copies

    def merged_rows(m, _):
        sl = rows_at(m, here)
        for h in range(2):
            work[sl, pl.ds(h * here, here)] = mm_rt(gml[sl, :], wo[h])
        return 0

    lax.fori_loop(0, 4, merged_rows, 0)
    for c in second:
        c.wait()
    states[0:group, :] = ends[16:24, :]

    def split(c, _):
        cols = pl.ds(pl.multiple_of(c * 128, 128), 128)
        g = jnp.swapaxes(work[:, cols].reshape(group, steps, 128), 0, 1).reshape(every, 128)
        act, slope = gelu_pair(gate[:, cols])
        gate[:, cols] = g * act
        down = g * states[pl.ds(group, every), cols] * slope
        pair[:, cols] = jnp.swapaxes(down.reshape(steps, group, 128), 0, 1).reshape(every, 128).astype(BF)
        return 0

    lax.fori_loop(0, chans // 128, split, 0)
    ring_v.step(0)
    for c in third:
        c.wait()
    unroll = 8
    blocks = steps // unroll

    def totals(b, carry):
        for u in range(unroll):
            sl = pl.ds(pl.multiple_of((steps - 1 - (b * unroll + u)) * group, group), group)
            carry = decay[sl, :] * (gate[sl, :] + carry)
        return carry

    zero = jnp.zeros((group, chans), F32)
    passed[0:8, :] = ends[0:8, :]
    passed[8:16, :] = lax.fori_loop(0, blocks, totals, zero)
    line = Line(at, passed, tot, line_sem.at[0], line_sem.at[1])
    line.send(0, at.s)

    def out_rows(m, _):
        cols = pl.ds(pl.multiple_of(m * 256, 256), 256)
        go[rows_at(m, 256), 0:width] = mm_lt(merged[:, cols], gml[...]).astype(BF)
        return 0

    lax.fori_loop(0, chans // 256, out_rows, 0)
    normed, core_out = gml, wo
    fourth.append(sems.local(normed_h, normed))

    def enter(k, state):
        j = n - 1 - k
        line.wait(j)
        return tot[j, 0:8, :] * state + tot[j, 8:16, :]

    carry_in = lax.fori_loop(0, n - 1 - at.s, enter, zero)
    line.sent(0, at.s)

    def scan(b, carry):
        for u in range(unroll):
            sl = pl.ds(pl.multiple_of((steps - 1 - (b * unroll + u)) * group, group), group)
            adjoint = gate[sl, :] + carry
            gate[sl, :] = adjoint
            carry = decay[sl, :] * adjoint
        return carry

    lax.fori_loop(0, blocks, scan, carry_in)
    ring_v.step(1)
    spread_u.wait()
    staging = staged(came_u, 0, ffl, up_o)
    for c in fourth:
        c.wait()
    heads_r[...] = jnp.zeros_like(heads_r)
    heads_l[...] = jnp.zeros_like(heads_l)
    acc[...] = jnp.zeros_like(acc)
    edge = sems.remote(
        gconv.at[pl.ds(0, halo)], gconv.at[pl.ds(every, halo)], at.line(lax.rem(at.s + n - 1, n))
    )

    slope8[0:1, :], slope8[1:2, :] = decay_rows(chan[7:8, :])

    def gates(b, _):
        size = 128
        start = pl.multiple_of(b * size, size)
        sl = pl.ds(start, size)
        for h in range(chans // 128):
            cols = pl.ds(h * 128, 128)
            sp8 = slope8[0:1, cols]
            r, i, dec, adj = rate[sl, cols], inlet[sl, cols], decay[sl, cols], gate[sl, cols]
            low_bf = conv[sl, cols]
            low = low_bf.astype(F32)
            factor = jnp.sqrt(EPS_MULT - expm1_neg(2.0 * (r * sp8)))
            ai = adj * i
            af = adj * factor
            gld = adj * states[sl, cols] * dec - ai * low * (dec * dec) / factor
            gldr = gld * r
            grate = gldr * sp8 * (1.0 - r)
            ginl = af * low * i * (1.0 - i)
            grl, gil = grate.astype(BF), ginl.astype(BF)
            hb = pl.ds(h * 128, 128)
            gc = af * i + mm_rt(grl, wr[hb, :]) + mm_rt(gil, wl[hb, :])
            heads_r[hb, :] += mm_lt(low_bf, grl)
            heads_l[hb, :] += mm_lt(low_bf, gil)
            gconv[sl, cols] = gc
            fold = lambda v: jnp.sum(v.reshape(size // 8, 8, 128), axis=0)
            for k in range(taps):
                acc[k, :, cols] += fold(gc * pad[pl.ds(start + (halo - group * k), size), cols])
            acc[4, :, cols] += fold(gc)
            acc[5, :, cols] += fold(grate)
            acc[6, :, cols] += fold(ginl)
            acc[7, :, cols] += fold(gldr)

        @pl.when(jnp.logical_and(b == 0, at.s > 0))
        def _():
            edge.start()

        return 0

    lax.fori_loop(0, every // 128, gates, 0)

    @pl.when(at.s == n - 1)
    def _():
        gconv[pl.ds(every, halo), :] = jnp.zeros((halo, chans), F32)

    thirds = width // chans
    inputs = [
        sems.local(x_h.at[:, pl.ds(k * chans, chans)], pad.at[pl.ds(k * here, here)]) for k in range(thirds)
    ]
    go[:, width : width + 128] = heads_r[...].astype(BF)
    go[:, width + 128 :] = heads_l[...].astype(BF)
    regroup_o = Regroup(at, sems, go, go_own)
    regroup_o.start()
    ring_v.step(2)
    for k in range(8):
        small[k : k + 1, :] = jnp.sum(acc[k], axis=0, keepdims=True)
    small[7:8, :] = small[7:8, :] * slope8[1:2, :]

    @pl.when(at.s < n - 1)
    def _():
        edge.wait_recv()

    @pl.when(at.s > 0)
    def _():
        edge.wait_send()

    def taps_back(b, _):
        start = pl.multiple_of(b * 128, 128)
        for h in range(chans // 128):
            cols = pl.ds(h * 128, 128)
            total = chan[0:1, cols] * gconv[pl.ds(start, 128), cols]
            for k in range(1, taps):
                total = total + chan[k : k + 1, cols] * gconv[pl.ds(start + group * k, 128), cols]
            work[pl.ds(start, 128), cols] = total
        return 0

    lax.fori_loop(0, every // 128, taps_back, 0)
    swap_rows(work, pair.at[:, pl.ds(chans, chans)], steps, BF)
    ring_v.step(3)

    def normed_rows(m, _):
        cols = pl.ds(pl.multiple_of(m * 256, 256), 256)
        ggi[rows_at(m, 256), :] = mm_lt(normed[:, cols], pair[...]).astype(BF)
        return 0

    lax.fori_loop(0, width // 256, normed_rows, 0)
    ring_g.start()
    for c in staging:
        c.wait()

    def back(o):
        sl = rows_at(o, here)

        def some(c, _):
            cols = pl.ds(pl.multiple_of(c * 512, 128), 512)
            tile[:, cols] = mm_rt(pair[sl, :], wgi[cols, :])
            return 0

        lax.fori_loop(0, width // 512, some, 0)

    sc = Scatter(at, sems, core_out, core_in, over_out, over_in, toks)

    def between(k):
        for j, ring, step in ((1, ring_v, 4), (2, ring_g, 0), (3, ring_v, 5)):

            @pl.when(k == j)
            def _():
                ring.step(step)

    sc.run_tile(back, tile, None, between)
    sc.second()
    spread_v = Spread(at, sems, last_u, came_v)
    ring_v.last(last_u)
    spread_v.start()
    ring_g.step(1)
    regroup_o.wait()
    ring_o.start()
    ring_g.step(2)
    gain1 = jnp.zeros((1, width), F32)
    for c in inputs:
        c.wait()
    for r in range(2):
        sl = pl.ds(r * toks, toks)
        g = tile[sl, :] + sc.arrived(r)
        v = jnp.concatenate([pad[pl.ds(k * here + r * toks, toks), :] for k in range(thirds)], axis=1)
        s = lax.rsqrt(jnp.mean(v * v, axis=-1, keepdims=True) + EPS_NORM)
        gain1 = gain1 + jnp.sum(g * v * s, axis=0, keepdims=True)
        gg = g * whole_gain(gain, 0)
        mean = jnp.mean(gg * v, axis=-1, keepdims=True)
        own[sl, :] = own[sl, :] + s * gg - v * (s * s * s * mean)
    regroup[1].start()
    saves = [sems.local(own, ginput_o)]
    ring_o.step(0)
    ring_g.step(3)
    for k in range(3):
        small[8 + k : 9 + k, :] = gain1[:, k * chans : (k + 1) * chans]
        small[11 + k : 12 + k, :] = gain2[0:1, k * chans : (k + 1) * chans]
    small[14:16, :] = jnp.zeros((2, chans), F32)
    share = Line(at, small, small_in, line_sem.at[2], line_sem.at[3])
    share.send(0, n)
    ring_o.step(1)
    ring_g.step(4)
    spread_v.wait()
    saves += staged(came_v, 0, ffl, value_o)
    small_in[at.s] = small[...]

    def arrive(j, total):
        @pl.when(j != at.s)
        def _():
            share.wait(j)

        return total + small_in[j]

    small_sum[...] = lax.fori_loop(0, n, arrive, jnp.zeros(small.shape, F32))
    ring_o.step(2)
    ring_g.step(5)
    hops = [hop.start(sems, small_sum.at[pl.ds(0, 8)], chan_o)]
    lower = small_sum.at[pl.ds(8, 8)]
    around = [sems.remote(lower, group_in.at[at.f], at.group(p)) for p in (at.p1, at.p2, at.p3)]
    for c in around:
        c.start()
    group_in[at.f] = small_sum[8:16, :]
    ring_o.step(3)
    last_g = last_u.at[:, pl.ds(0, 2 * chans)]
    ring_g.last(last_g)
    for c in regroup:
        c.wait()
    ring_d.start()
    for c in around:
        c.wait()
    gains[...] = group_in[0] + group_in[1] + group_in[2] + group_in[3]
    came_g = came_u.at[:, :, pl.ds(0, 2 * chans)]
    spread_g = Spread(at, sems, last_g, came_g)
    spread_g.start()
    ring_o.step(4)
    ring_d.step(0)
    for c in saves:
        c.wait()
    saves = [sems.local(gains, gains_o)]
    ring_o.step(5)
    ring_d.step(1)
    crow = rate_o.shape[0]

    def store_out(i, value):
        rows = ring_o.cut[i][0]
        for k in range(thirds + 1):
            size = min(chans, width + 256 - k * chans)
            rate[pl.ds(k * crow + rows.start, rows.size), 0:size] = value[:, k * chans : k * chans + size]

    ring_o.last(None, store_out)
    saves += [
        sems.local(rate.at[pl.ds(k * crow, crow)], out_o.at[:, pl.ds(k * chans, chans)]) for k in range(thirds)
    ]
    saves += [
        sems.local(rate.at[pl.ds(thirds * crow, crow), pl.ds(k * 128, 128)], o) for k, o in enumerate((rate_o, inlet_o))
    ]
    ring_d.step(2)
    spread_g.wait()
    saves += staged(came_g, 0, chans, gate_o) + staged(came_g, chans, chans, input_o, here // 2)
    share.sent(0, n)
    sc.finish()
    hop.wait(hops[0])
    for r in (ring_v, ring_o, ring_g):
        r.finish()
    ring_d.step(3)
    ring_d.step(4)
    ring_d.step(5)
    drow, dcol = gwd.shape[0] // n, width // 4

    def store_down(i, value):
        work[i * drow : (i + 1) * drow, 0:dcol] = value

    ring_d.last(None, store_down)
    saves += [
        sems.local(work.at[pl.ds(i * drow, drow), pl.ds(0, dcol)], down_o.at[:, pl.ds(i * dcol, dcol)]) for i in range(4)
    ]
    ring_d.finish()
    for c in saves:
        c.wait()


def call_back(chan, wr, wl, gain, gain2, gml, merged, wo, wgi, normed, gate, pad, conv, rate, inlet, decay, states, ends, gwd, x, gmid, up, value):
    every, width = gml.shape
    here = x.shape[0]
    chans = chan.shape[1]
    ffl = gwd.shape[0]
    n = lax.axis_size("seq")
    f32 = lambda *s: jax.ShapeDtypeStruct(s, F32)
    vf = lambda *s: pltpu.VMEM(s, F32)
    vb = lambda *s: pltpu.VMEM(s, BF)
    rows, crow = width // n, chans // n
    outs = [
        f32(here, width), f32(rows // 4, 4 * ffl), f32(rows // 4, 4 * ffl), f32(ffl // n, width), f32(rows // 4, 4 * chans), f32(rows // 4, 4 * chans), f32(crow, width),
        f32(crow, 128), f32(crow, 128), f32(8, chans), f32(8, chans),
    ]
    scratch = [
        vf(8, chans), vb(chans, 128), vb(chans, 128), vf(4, 8, width // 4), vf(8, width),
        vb(every, width), vb(every, chans), vb(2, here, width), vb(width, 2 * chans),
        vf(every, chans), vf(every + 24, chans), vb(every, chans), vf(every, chans), vf(every, chans), vf(every, chans),
        vf(every + 8, chans), vf(24, chans), vb(ffl, width), vb(width, ffl), vf(here, width),
        vf(every, chans), vf(every + 24, chans), vb(every, 2 * chans), vf(chans, 128), vf(chans, 128), vf(8, 8, chans),
        vf(here, width), vb(2, here, width), vb(here, width), vb(here, width),
        vb(chans, width + 256), vb(width, 2 * chans), vb(n - 1, ffl // n, width), vb(n - 1, rows, ffl), vb(n - 1, crow, width + 256), vb(n - 1, rows, 2 * chans),
        vb(rows, ffl), vb(4, rows // 4, ffl), vb(4, rows // 4, ffl), vb(chans, width + 256),
        vf(16, chans), vf(n, 16, chans), vf(16, chans), vf(n, 16, chans), vf(16, chans), vf(4, 8, chans), vf(8, chans), vf(8, chans),
        pltpu.SemaphoreType.DMA((150,)), pltpu.SemaphoreType.DMA((8, 4, n - 1)), pltpu.SemaphoreType.DMA((4, n)),
    ]
    return pl.pallas_call(
        branch_back,
        out_shape=outs,
        in_specs=[ANY] * 23,
        out_specs=[ANY] * len(outs),
        scratch_shapes=scratch,
        compiler_params=pltpu.CompilerParams(collective_id=3, has_side_effects=True, vmem_limit_bytes=LIMIT),
        name="branch_back",
    )(chan, wr, wl, gain, gain2, gml, merged, wo, wgi, normed, gate, pad, conv, rate, inlet, decay, states, ends, gwd, x, gmid, up, value)


def collect(chan, gains, *refs):
    count = (len(refs) - 1 - 7) // 3
    sources, results, small = refs[:count], refs[count : 2 * count], refs[2 * count : 2 * count + 7]
    held, sem = refs[2 * count + 7 : -1], refs[-1]
    loads = [pltpu.make_async_copy(a, b, sem.at[0, k]) for k, (a, b) in enumerate(zip(sources, held))]
    copies = [pltpu.make_async_copy(a, b, sem.at[1, k]) for k, (a, b) in enumerate(zip(held, results))]
    for c in loads:
        c.start()
    for a, b in zip(loads, copies):
        a.wait()
        b.start()
    taps_o, bias_o, rate_o, inlet_o, decay_o, one_o, two_o = small
    n = lax.axis_size("seq")
    place = lax.axis_index("seq") * 4 + lax.axis_index("fsdp")
    per, chans = taps_o.shape[1], chan.shape[1]
    mine = pltpu.roll(chan[...], lax.rem(chans - lax.rem(place, n) * per, chans), 1)[:, :per]
    taps_o[...] = mine[0:4, :]
    for k, o in enumerate((bias_o, rate_o, inlet_o, decay_o)):
        o[...] = mine[4 + k : 5 + k, :].reshape(per)
    per = one_o.shape[0]
    thirds = 4 * n * per // chans
    for row, o in enumerate((one_o, two_o)):
        line = jnp.concatenate([gains[row * thirds + k : row * thirds + k + 1, :] for k in range(thirds)], axis=1)
        line = jnp.broadcast_to(line, (8, thirds * chans))
        line = pltpu.roll(line, lax.rem(thirds * chans - place * per, thirds * chans), 1)
        o[...] = line[0:1, :per].reshape(per)
    for c in copies:
        c.wait()


def call_collect(chan, gains, big):
    n = lax.axis_size("seq")
    chans = chan.shape[1]
    f32 = lambda *s: jax.ShapeDtypeStruct(s, F32)
    per, own = chans // n, big[0].shape[1] // (4 * n)
    outs = [f32(*v.shape) for v in big] + [f32(4, per)] + [f32(per)] * 4 + [f32(own)] * 2
    return pl.pallas_call(
        collect,
        out_shape=outs,
        in_specs=[VMEM] * 2 + [ANY] * len(big),
        out_specs=[ANY] * len(big) + [VMEM] * 7,
        scratch_shapes=[pltpu.VMEM(v.shape, F32) for v in big] + [pltpu.SemaphoreType.DMA((2, len(big)))],
        compiler_params=pltpu.CompilerParams(has_side_effects=True, vmem_limit_bytes=LIMIT),
        name="collect",
    )(chan, gains, *big)


def body(
    block_input, teacher, valid_lengths, norm_gain, w_gate, w_input, conv_weight, conv_bias,
    w_rate, bias_rate, w_inlet, bias_inlet, decay_param, w_out, mlp_gain, w_up, w_value, w_down,
):
    n_seq, n_fs = lax.axis_size("seq"), lax.axis_size(GROUP)
    si, fi = lax.axis_index("seq"), lax.axis_index(GROUP)
    rows_dev, toks, width = block_input.shape
    rows = rows_dev * n_fs
    here = rows_dev * toks
    chans = conv_bias.shape[0]
    hb = w_rate.shape[1]
    heads = chans // hb
    taps = conv_weight.shape[0]

    cw = conv_weight.astype(F32)
    x = block_input.reshape(here, width)
    (wgi, wuv, normed, n2, middle, gate_tm, pad_tm, conv_tm, rate_tm, inlet_tm, decay_tm, states_tm, merged, ends, gain, chan) = call_forward(
        x, norm_gain, mlp_gain, conv_weight, conv_bias, bias_rate, bias_inlet, decay_param, w_rate, w_inlet, w_out, w_gate, w_input, w_up, w_value)
    lens = lax.dynamic_slice_in_dim(valid_lengths, fi * rows_dev, rows_dev)
    pos = si * toks + jnp.arange(toks, dtype=jnp.int32)
    mask = (pos[None, :] < lens[:, None]).reshape(here, 1)
    slots = valid_lengths.shape[0] * toks * n_seq
    count = jnp.sum(valid_lengths).astype(F32)
    if n_seq == 8 and all((v // n_seq) % 64 == 0 for v in (width, chans)):
        result, grad_middle, gml, gain2, g_down, up_part, value_part = call_mlp(
            n2, wuv, w_up, w_value, w_down, middle, teacher.reshape(here, width), valid_lengths, gain)
        grad_input, up_sum, value_sum, down_sum, gate_sum, input_sum, out_sum, rate_sum, inlet_sum, ch, gn = call_back(
            chan, w_rate, w_inlet, gain, gain2, gml, merged, w_out, wgi, normed, gate_tm, pad_tm,
            conv_tm, rate_tm, inlet_tm, decay_tm, states_tm, ends, g_down, x, grad_middle, up_part, value_part)
        (result, grad_input, up_sum, value_sum, down_sum, gate_sum, input_sum, out_sum, rate_sum, inlet_sum,
         s_taps, s_bias, s_rate, s_inlet, s_decay, s_one, s_two) = call_collect(
            ch, gn, [result, grad_input, up_sum, value_sum, down_sum, gate_sum, input_sum, out_sum, rate_sum, inlet_sum])
        return (
            result.reshape(block_input.shape), grad_input.reshape(block_input.shape), s_one, gate_sum, input_sum,
            s_taps, s_bias, rate_sum, s_rate, inlet_sum, s_inlet, s_decay, out_sum, s_two, up_sum, value_sum, down_sum,
        )

    sp = jax.nn.softplus(-decay_param.astype(F32))
    heads_shape = (heads, hb, hb)
    wr, wl = w_rate.reshape(heads_shape), w_inlet.reshape(heads_shape)
    wg, wi = wgi[:, :chans], wgi[:, chans:]
    ffl = w_down.shape[0]
    own = jnp.concatenate([lax.dynamic_slice_in_dim(w, fi * ffl, ffl, 1) for w in (w_up, w_value)], 1)
    wuv = lax.dynamic_update_slice_in_dim(wuv, own, fi * (width // n_fs), 0)
    wu, wv = wuv[:, :ffl], wuv[:, ffl:]
    gain_one, gain_two = gain[:, 0].reshape(-1), gain[:, 1].reshape(-1)
    s1 = lax.rsqrt(jnp.mean(x * x, axis=-1, keepdims=True) + EPS_NORM)
    s2 = lax.rsqrt(jnp.mean(middle * middle, axis=-1, keepdims=True) + EPS_NORM)
    tok = lambda v: v.reshape(-1, rows, chans).swapaxes(0, 1)
    padded, clf, r, i, decay, states = tok(pad_tm), tok(conv_tm), tok(rate_tm), tok(inlet_tm), tok(decay_tm), tok(states_tm)
    conv_low, clf = clf, clf.astype(F32)
    heads_in = conv_low.reshape(rows * toks, heads, hb)
    gate_pre = tok(gate_tm).reshape(-1, chans)
    gg, gd = gelu_pair(gate_pre)
    cum_end, state_in = ends[:8], ends[16:24]
    prev = jnp.concatenate([state_in[:, None], states[:, :-1]], axis=1)
    ld = -RATE_SCALE * r * sp
    factor = jnp.sqrt(EPS_MULT - jnp.expm1(2.0 * ld))
    up = mm(n2, wu)
    value = mm(n2, wv)
    vg, vd = gelu_pair(value)
    hidden = (vg * up).astype(BF)
    result = middle + rs(mm(hidden, w_down))
    grad_out = jnp.where(mask, result - teacher.reshape(here, width), 0.0) * (slots / count)
    gdi = ag(grad_out.astype(BF))
    g_down = mm_lt(hidden, gdi)
    gh = mm_rt(gdi, w_down)
    gu = (gh * vg).astype(BF)
    gv = (gh * up * vd).astype(BF)
    g_up = mm_lt(n2, gu)
    g_value = mm_lt(n2, gv)
    gn2 = rs(mm_rt(gu, wu) + mm_rt(gv, wv))
    gm_norm, gain2 = rms_back(middle, s2, gain_two, gn2)
    grad_middle = grad_out + gm_norm
    gml = ag(grad_middle.astype(BF))
    g_out = mm_lt(merged, gml)
    gmer = mm_rt(gml, w_out)
    gst = (gmer * gg).reshape(rows, toks, chans)
    ggate = (gmer * states.reshape(-1, chans) * gd).astype(BF)
    nextd = jnp.concatenate([decay[:, 1:], jnp.ones((rows, 1, chans), F32)], axis=1)
    carry, ladj = lax.associative_scan(linear_step, (nextd, gst), axis=1, reverse=True)
    tot2 = lax.all_gather(jnp.stack([cum_end, decay[:, 0] * ladj[:, 0]]), "seq")
    adj_in = jnp.zeros((rows, chans), F32)
    for j in reversed(range(n_seq)):
        adj_in = jnp.where(j > si, tot2[j, 0] * adj_in + tot2[j, 1], adj_in)
    adj = ladj + carry * adj_in[:, None]
    gdec = adj * prev
    gfac = adj * i * clf
    gld = gdec * decay - gfac * (decay * decay) / factor
    grate = gld * (-RATE_SCALE * sp) * r * (1.0 - r)
    ginl = adj * factor * clf * i * (1.0 - i)
    gdp = jnp.sum(gld * r, axis=(0, 1)) * RATE_SCALE * jax.nn.sigmoid(-decay_param.astype(F32))
    gcd = adj * factor * i
    grb, gib = jnp.sum(grate, (0, 1)), jnp.sum(ginl, (0, 1))
    grl, gil = grate.astype(BF).reshape(-1, heads, hb), ginl.astype(BF).reshape(-1, heads, hb)
    gwr = jnp.einsum("nhi,nhj->hij", heads_in, grl, preferred_element_type=F32).reshape(chans, hb)
    gwi = jnp.einsum("nhi,nhj->hij", heads_in, gil, preferred_element_type=F32).reshape(chans, hb)
    bk = lambda a, w: jnp.einsum("nhj,hij->nhi", a, w, preferred_element_type=F32).reshape(rows, toks, chans)
    gconv = gcd + bk(grl, wr) + bk(gil, wl)
    gcw = jnp.stack([jnp.sum(gconv * padded[:, taps - 1 - k: taps - 1 - k + toks], (0, 1)) for k in range(taps)])
    gcb = jnp.sum(gconv, (0, 1))
    gpad = jnp.zeros((rows, toks + taps - 1, chans), F32)
    for k in range(taps):
        gpad = gpad.at[:, taps - 1 - k: taps - 1 - k + toks].add(cw[k] * gconv)
    edge = shifted(gpad[:, : taps - 1], "seq", -1)
    gbr = gpad[:, taps - 1:].at[:, toks - (taps - 1):].add(edge).reshape(-1, chans).astype(BF)
    g_gate = mm_lt(normed, ggate)
    g_input = mm_lt(normed, gbr)
    gn1 = rs(mm_rt(ggate, wg) + mm_rt(gbr, wi))
    gi_norm, gain1 = rms_back(x, s1, gain_one, gn1)
    grad_input = grad_middle + gi_norm

    chan = jnp.concatenate([gcw, gcb[None], grb[None], gib[None], gdp[None]], 0)
    per = chans // n_seq
    chan = chan.reshape(8, n_seq, per).transpose(1, 0, 2).reshape(n_seq, 8 * per)
    blk = jnp.zeros((n_fs, n_seq, 8 * per), F32).at[fi].set(chan).reshape(n_fs * n_seq, 8 * per)
    gw = jnp.stack([gain1, gain2]).reshape(2, n_fs * n_seq, -1).transpose(1, 0, 2).reshape(n_fs * n_seq, -1)
    small = lax.psum_scatter(jnp.concatenate([blk, gw], 1), BOTH, scatter_dimension=0, tiled=True)[0]
    ch = small[: 8 * per].reshape(8, per)
    gn = small[8 * per:].reshape(2, -1)
    og = grads_rows(jnp.concatenate([g_out, gwr, gwi], 1))
    return (
        result.reshape(block_input.shape), grad_input.reshape(block_input.shape), gn[0],
        grads_cols(g_gate), grads_cols(g_input), ch[:4], ch[4], og[:, width: width + hb], ch[5],
        og[:, width + hb:], ch[6], ch[7], og[:, :width], gn[1], grads_cols(g_up), grads_cols(g_value), grads_rows(g_down),
    )


def solution(mesh):
    rowsh, vec, mat = P("fsdp", "seq", None), P("fsdp"), P("fsdp", None)
    ov, om = P(BOTH), P(BOTH, None)
    return jax.shard_map(
        body,
        mesh=mesh,
        in_specs=(rowsh, rowsh, P(), vec, mat, mat, P(None, "fsdp"), vec, mat, vec, mat, vec, vec, mat, vec, mat, mat, mat),
        out_specs=(rowsh, rowsh, ov, om, om, P(None, BOTH), ov, om, ov, om, ov, ov, om, ov, om, om, om),
        check_vma=False,
    )
```
